32 devices in a mesh: seq: 8 (over z, y), mp: 4 (over x, core).
Axes of the slice: x: 2, y: 2, z: 4, core: 2. Of those that a mesh axis runs over, the one named last changes fastest.
Arguments:
- inputs: bfloat16 [8192, 2048], P('seq'), may hold values from -11 to 11
- seq_start: int32 [8192], P('seq'), may hold values from 0 to 8191, as said below
- norm_in: float32 [2048], replicated, may hold values from 0.1 to 1.9
- w_input: bfloat16 [2048, 2048], P(None, 'mp'), may hold values from -0.125 to 0.125
- w_forget: bfloat16 [2048, 2048], P(None, 'mp'), may hold values from -0.125 to 0.125
- w_mix_gate: bfloat16 [2048, 2048], P(None, 'mp'), may hold values from -0.125 to 0.125
- lower_bound: float32 [2048], P('mp'), may hold values from 0 to 1
- mix_gain: float32 [2048], P('mp'), may hold values from 0.1 to 1.9
- w_output: bfloat16 [2048, 2048], P('mp'), may hold values from -0.1875 to 0.1875
- norm_ffn: float32 [2048], replicated, may hold values from 0.1 to 1.9
- w_gate: bfloat16 [2048, 5632], P(None, 'mp'), may hold values from -0.125 to 0.125
- w_up: bfloat16 [2048, 5632], P(None, 'mp'), may hold values from -0.125 to 0.125
- w_down: bfloat16 [5632, 2048], P('mp'), may hold values from -0.15625 to 0.15625
- cotangent: bfloat16 [8192, 2048], P('seq'), may hold values from -6 to 6
Outputs:
- out: bfloat16 [8192, 2048], P('seq')
- d_inputs: float32 [8192, 2048], P('seq')
- d_norm_in: float32 [2048], P('seq')
- d_w_input: float32 [2048, 2048], P('seq', 'mp')
- d_w_forget: float32 [2048, 2048], P('seq', 'mp')
- d_w_mix_gate: float32 [2048, 2048], P('seq', 'mp')
- d_lower_bound: float32 [2048], P('mp')
- d_mix_gain: float32 [2048], P('mp')
- d_w_output: float32 [2048, 2048], P('mp', 'seq')
- d_norm_ffn: float32 [2048], P('seq')
- d_w_gate: float32 [2048, 5632], P('seq', 'mp')
- d_w_up: float32 [2048, 5632], P('seq', 'mp')
- d_w_down: float32 [5632, 2048], P('mp', 'seq')
- forget_mean: float32 [2048], P('mp')
The draws below stay inside these ranges and needn't reach their ends.
Inputs may be any that keep to these rules, and one draw needn't show every extreme that they name: seq_start[t] is the position of the first token of the sequence that holds token t; the stream holds five contiguous sequences, and the middle one begins within the first 1024 tokens and ends within the last 1024.
All inputs are finite; a program needn't handle non-finite values.
Results may differ from the reference program's by a relative error of at most 0.0073.
Values sent between devices are 32-bit elements; how exact they have to be, the bound alone decides.
No kernel may reach another device: no remote copies, remote signals or barrier semaphores. Data moves between devices by JAX's collectives and lax.ppermute only.
A program may use at most 256 MiB of HBM per device.

```python
import jax
import jax.numpy as jnp
from jax import lax

D = 2048
FF = 5632
TOK_DEV = 1024
TOKENS = 8192


def draw_seq_start(key, part):
    keys = jax.random.split(key, 4)
    opening = jax.random.randint(keys[0], (), 2, TOK_DEV)
    head_cut = jax.random.randint(keys[1], (), 1, opening)
    closing = jax.random.randint(keys[2], (), TOKENS - TOK_DEV + 1, TOKENS - 1)
    tail_cut = jax.random.randint(keys[3], (), closing + 1, TOKENS)
    places = jnp.arange(TOKENS, dtype=jnp.int32)
    starts = jnp.where(places >= head_cut, head_cut, 0)
    starts = jnp.where(places >= opening, opening, starts)
    starts = jnp.where(places >= closing, closing, starts)
    starts = jnp.where(places >= tail_cut, tail_cut, starts)
    return starts.astype(jnp.int32)


def draw_lower_bound(key, part):
    first = jax.random.fold_in(key, 0)
    slowest = jnp.log(0.03 / TOKENS)
    fastest = jnp.log(0.04)
    spread = jax.random.uniform(first, (D,), jnp.float32)
    logs = slowest + spread * (fastest - slowest)
    return (1.0 - jnp.exp(logs)).astype(jnp.float32)


def draw_inputs(key, part):
    key = jax.random.fold_in(key, 11)
    keys = jax.random.split(key, 3)
    blocks = TOKENS // TOK_DEV
    noise = jnp.clip(jax.random.normal(keys[0], (TOKENS, D), jnp.float32), -3.5, 3.5)
    offset = jnp.clip(0.7 * jax.random.normal(keys[1], (D,), jnp.float32), -2.0, 2.0)
    pairing = jax.random.permutation(keys[2], blocks)
    row_block = jnp.arange(TOKENS, dtype=jnp.int32) // TOK_DEV
    col_block = jnp.arange(D, dtype=jnp.int32) // (D // blocks)
    paired = col_block[None, :] == pairing[row_block][:, None]
    factor = jnp.where(paired, 2.5, 1.0)
    return (noise * factor + offset[None, :]).astype(jnp.float32).astype(jnp.bfloat16)


def with_spikes(entries, key, source, target, shards_of, factor):
    owner, partner = [(jnp.arange(entries.shape[dim]) // (entries.shape[dim] // shards_of)).reshape([-1 if axis == dim else 1 for axis in range(entries.ndim)]) for dim in (source, target)]
    chosen = jax.random.permutation(key, shards_of)[partner]
    strong = (owner == chosen) | (owner == (partner + shards_of // 2) % shards_of)
    return jnp.where(strong, factor * entries, entries)


def block_levels(rng, extent, pieces, least, top_value):
    loudness = 1.0
    for axis_at, shards_of in pieces:
        steps = jax.random.uniform(jax.random.fold_in(jax.random.fold_in(rng, 6), axis_at), (shards_of,), jnp.float32, least / len(pieces), top_value / len(pieces))
        loudness = loudness * jnp.repeat(jnp.exp(steps), extent[axis_at] // shards_of).reshape((-1,) + (1,) * (len(extent) - 1 - axis_at))
    return loudness


def scatter_about(key, extent, scale, most, pieces=(), kind=jnp.bfloat16):
    drawn = jax.random.normal(key, extent, jnp.float32) * scale
    if len(pieces) > 0:
        drawn = block_levels(key, extent, pieces, -0.22, 0.18) * drawn
    return jnp.clip(drawn, min=-most, max=most).astype(kind)


def heavy_noise(key, dims, scale, reach, cuts, heavy, kind=jnp.bfloat16):
    drawn = scale * jax.random.normal(key, dims, jnp.float32)
    if cuts:
        drawn = drawn * block_levels(key, dims, cuts, -0.22, 0.18)
    return jnp.clip(with_spikes(drawn, jax.random.fold_in(key, 3), *heavy), -reach, reach).astype(kind)


def setup_inputs(seed: int = 0) -> dict:
    seeds = jax.random.split(jax.random.key(seed), 15)
    return {
        "inputs": draw_inputs(jax.random.fold_in(seeds[14], 71), 0),
        "seq_start": draw_seq_start(jax.random.fold_in(seeds[14], 71), 0),
        "norm_in": jnp.clip(1.0 + 0.18 * jax.random.normal(seeds[2], (D,), jnp.float32), 0.1, 1.9),
        "w_input": scatter_about(seeds[3], (D, D), D ** -0.5, 0.125, ((1, 4),)),
        "w_forget": scatter_about(seeds[4], (D, D), D ** -0.5, 0.125, ((1, 4),)),
        "w_mix_gate": scatter_about(seeds[5], (D, D), D ** -0.5, 0.125, ((1, 4),)),
        "lower_bound": draw_lower_bound(jax.random.fold_in(seeds[14], 71), 0),
        "mix_gain": jnp.clip(1.0 + 0.18 * jax.random.normal(seeds[7], (D,), jnp.float32), 0.1, 1.9),
        "w_output": scatter_about(seeds[8], (D, D), (D // 2) ** -0.5, 0.1875, ((0, 4),)),
        "norm_ffn": jnp.clip(1.0 + 0.18 * jax.random.normal(seeds[9], (D,), jnp.float32), 0.1, 1.9),
        "w_gate": scatter_about(seeds[10], (D, FF), D ** -0.5, 0.125, ((1, 4),)),
        "w_up": scatter_about(seeds[11], (D, FF), D ** -0.5, 0.125, ((1, 4),)),
        "w_down": scatter_about(seeds[12], (FF, D), (FF // 4) ** -0.5, 0.15625, ((0, 4),)),
        "cotangent": heavy_noise(seeds[13], (TOKENS, D), 1.0, 6.0, ((0, 8),), (0, 1, 8, 2.0)),
    }


@jax.custom_vjp
def low(v):
    return lax.optimization_barrier(v.astype(jnp.bfloat16)).astype(jnp.float32)

@jax.custom_vjp
def low_back(v):
    return v

def low_keep(v):
    return (low(v), None)

def low_pass(kept, grad):
    return (grad,)

def back_keep(v):
    return (v, None)

def back_low(kept, grad):
    return (low(grad),)
low.defvjp(low_keep, low_pass)
low_back.defvjp(back_keep, back_low)
epsilon = 1e-06

def product(left, right):
    return jnp.dot(left, right, precision=lax.Precision.HIGHEST, preferred_element_type=jnp.float32)

def rms_scale(values):
    return lax.rsqrt(lax.optimization_barrier(jnp.mean(values * values, axis=-1, keepdims=True)) + epsilon)

def compose(earlier, later):
    return (earlier[0] * later[0], later[0] * earlier[1] + later[1])

def block(inputs, norm_in, w_input, w_forget, w_mix_gate, lower_bound, mix_gain, w_output, norm_ffn, w_gate, w_up, w_down, restart):
    normed = low(inputs * rms_scale(inputs) * norm_in)
    in_pre = low_back(product(normed, w_input))
    forget_pre = low_back(product(normed, w_forget))
    mix_pre = low_back(product(normed, w_mix_gate))
    keep = (1.0 - lower_bound) * jax.nn.sigmoid(-forget_pre)
    decay = (1.0 - keep) * (1.0 - restart)
    drive = jax.nn.silu(in_pre) * keep
    state = lax.associative_scan(compose, (decay, drive), axis=0)[1]
    mixed = low(state * rms_scale(state) * mix_gain * jax.nn.silu(mix_pre))
    middle = inputs + low_back(product(mixed, w_output))
    normed_ffn = low(middle * rms_scale(middle) * norm_ffn)
    gate = low_back(product(normed_ffn, w_gate))
    upward = low_back(product(normed_ffn, w_up))
    hidden = low(jax.nn.silu(gate) * upward)
    return middle + product(hidden, w_down)

def reference(inputs, seq_start, norm_in, w_input, w_forget, w_mix_gate, lower_bound, mix_gain, w_output, norm_ffn, w_gate, w_up, w_down, cotangent):
    places = jnp.arange(seq_start.shape[0], dtype=jnp.int32)
    restart = (seq_start == places).astype(jnp.float32)[:, None]
    params = (inputs, norm_in, w_input, w_forget, w_mix_gate, lower_bound, mix_gain, w_output, norm_ffn, w_gate, w_up, w_down)
    params = tuple((item.astype(jnp.float32) for item in params))

    def forward(*values):
        return block(*values, restart)
    result, pull = jax.vjp(forward, *params)
    grads = pull(cotangent.astype(jnp.float32))
    in_float = params[0]
    normed = (in_float * rms_scale(in_float) * params[1]).astype(jnp.bfloat16).astype(jnp.float32)
    forget_pre = product(normed, params[3])
    forget_mean = lax.optimization_barrier(jnp.sum(jax.nn.sigmoid(forget_pre), axis=0)) / forget_pre.shape[0]
    return (result.astype(jnp.bfloat16), grads[0], grads[1], grads[2], grads[3], grads[4], grads[5], grads[6], grads[7], grads[8], grads[9], grads[10], grads[11], forget_mean)
```

```python
import functools

import jax
import jax.numpy as jnp
from jax import lax
from jax.experimental import pallas as pl
from jax.experimental.pallas import tpu as pltpu
from jax.sharding import PartitionSpec as P

epsilon = 1e-06
f32 = jnp.float32
bf16 = jnp.bfloat16
together = lax.optimization_barrier


def multiply(left, right):
    return jnp.dot(left, right, preferred_element_type=f32)


def inner_rows(left, right):
    return lax.dot_general(left, right, (((0,), (0,)), ((), ())), preferred_element_type=f32)


def outer_cols(left, right):
    return lax.dot_general(left, right, (((1,), (1,)), ((), ())), preferred_element_type=f32)


def rms_scale(values):
    return lax.rsqrt(jnp.mean(values * values, axis=-1, keepdims=True) + epsilon)


def silu_slope(values):
    sig = jax.nn.sigmoid(values)
    return sig * (1.0 + values * (1.0 - sig))


LANES = 8
STRIP = 128
BIG = 48 * 1024 * 1024


def scan_forward_kernel(in_ref, forget_ref, cut_ref, bound_ref, local_ref, run_ref, whole_ref, sum_ref):
    length = forget_ref.shape[0] // LANES
    lift = 1.0 - bound_ref[...]
    shape = (LANES, forget_ref.shape[1])

    def step(t, carry):
        state, run, gates = carry
        at = pl.ds(t, LANES, stride=length)
        fade = jax.nn.sigmoid(-forget_ref[at, :])
        keep = lift * fade
        decay = (1.0 - keep) * (1.0 - cut_ref[at, :])
        pre = in_ref[at, :]
        state = decay * state + pre * jax.nn.sigmoid(pre) * keep
        run = run * decay
        local_ref[at, :] = state
        run_ref[at, :] = run
        return state, run, gates + (1.0 - fade)

    zero = jnp.zeros(shape, f32)
    state, run, gates = lax.fori_loop(0, length, step, (zero, jnp.ones(shape, f32), zero), unroll=8)
    ends, product = (state[0:1], run[0:1])
    for k in range(1, LANES):
        ends = run[k : k + 1] * ends + state[k : k + 1]
        product = product * run[k : k + 1]
    whole_ref[0:1, :] = product
    whole_ref[1:2, :] = ends
    sum_ref[...] = jnp.sum(gates, axis=0, keepdims=True)


def scan_forward(in_pre, forget_pre, cut, bound):
    tokens, width = in_pre.shape
    full = jax.ShapeDtypeStruct((tokens, width), f32)
    strip = pl.BlockSpec((tokens, STRIP), lambda i: (0, i))
    row = pl.BlockSpec((1, STRIP), lambda i: (0, i))
    return pl.pallas_call(
        scan_forward_kernel,
        grid=(width // STRIP,),
        in_specs=[strip, strip, pl.BlockSpec((tokens, STRIP), lambda i: (0, 0)), row],
        out_specs=[strip, strip, pl.BlockSpec((2, STRIP), lambda i: (0, i)), row],
        out_shape=(full, full, jax.ShapeDtypeStruct((2, width), f32), jax.ShapeDtypeStruct((1, width), f32)),
        compiler_params=pltpu.CompilerParams(vmem_limit_bytes=BIG),
        cost_estimate=pl.CostEstimate(flops=20 * tokens * width, bytes_accessed=16 * tokens * width, transcendentals=4 * tokens * width),
        name="scan_forward",
    )(in_pre, forget_pre, cut, bound)


def arriving(far_ref):
    total = jnp.zeros_like(far_ref[0, 0:1, :])
    for k in range(far_ref.shape[0]):
        total = far_ref[k, 0:1, :] * total + far_ref[k, 1:2, :]
    return total


def join_forward_kernel(local_ref, run_ref, mix_ref, far_ref, gain_ref, seg_ref, state_ref, prev_ref, u_ref, hold):
    @pl.when(pl.program_id(0) == 0)
    def _():
        hold[...] = arriving(far_ref)

    first = hold[...]
    state = local_ref[...] + run_ref[...] * first
    mix = mix_ref[...]
    rows = lax.broadcasted_iota(jnp.int32, state.shape, 0)
    state_ref[...] = state
    prev_ref[...] = jnp.where(rows == 0, first, pltpu.roll(state, 1, 0))
    u_ref[...] = (state * gain_ref[...] * (mix * jax.nn.sigmoid(mix))).astype(u_ref.dtype)
    seg_ref[...] = first
    hold[...] = state[state.shape[0] - 1 :, :]


def join_forward(local, run, mix_pre, far, gain):
    tokens, width = local.shape
    length = tokens // LANES
    block = pl.BlockSpec((length, width), lambda i: (i, 0))
    full = jax.ShapeDtypeStruct((tokens, width), f32)
    return pl.pallas_call(
        join_forward_kernel,
        grid=(LANES,),
        in_specs=[
            block,
            block,
            block,
            pl.BlockSpec(far.shape, lambda i: (0, 0, 0)),
            pl.BlockSpec((1, width), lambda i: (0, 0)),
        ],
        out_specs=[pl.BlockSpec((1, width), lambda i: (0, 0)), block, block, block],
        out_shape=(
            jax.ShapeDtypeStruct((1, width), f32),
            full,
            full,
            jax.ShapeDtypeStruct((tokens, width), bf16),
        ),
        scratch_shapes=[pltpu.VMEM((1, width), f32)],
        compiler_params=pltpu.CompilerParams(vmem_limit_bytes=BIG),
        cost_estimate=pl.CostEstimate(flops=10 * tokens * width, bytes_accessed=22 * tokens * width, transcendentals=2 * tokens * width),
        name="join_forward",
    )(local, run, mix_pre, far, gain)[1:]


def scan_backward_kernel(
    grad_ref, state_ref, mix_ref, forget_ref, cut_ref, scale_ref, pull_ref, bound_ref, gain_ref, local_ref, run_ref, whole_ref
):
    length = forget_ref.shape[0] // LANES
    lift = 1.0 - bound_ref[...]
    gain = gain_ref[...]
    shape = (LANES, forget_ref.shape[1])

    def step(i, carry):
        message, run = carry
        at = pl.ds(length - 1 - i, LANES, stride=length)
        decay = (1.0 - lift * jax.nn.sigmoid(-forget_ref[at, :])) * (1.0 - cut_ref[at, :])
        mix = mix_ref[at, :]
        weighed = grad_ref[at, :] * gain * (mix * jax.nn.sigmoid(mix))
        total = scale_ref[at, :] * weighed - state_ref[at, :] * pull_ref[at, :] + message
        local_ref[at, :] = total
        run_ref[at, :] = run
        return decay * total, decay * run

    message, run = lax.fori_loop(0, length, step, (jnp.zeros(shape, f32), jnp.ones(shape, f32)), unroll=8)
    ends, product = (message[LANES - 1 :], run[LANES - 1 :])
    for k in range(LANES - 2, -1, -1):
        ends = run[k : k + 1] * ends + message[k : k + 1]
        product = product * run[k : k + 1]
    whole_ref[0:1, :] = product
    whole_ref[1:2, :] = ends


def scan_backward(grad, state, mix_pre, forget_pre, cut, scale, pull, bound, gain):
    tokens, width = grad.shape
    full = jax.ShapeDtypeStruct((tokens, width), f32)
    strip = pl.BlockSpec((tokens, STRIP), lambda i: (0, i))
    column = pl.BlockSpec((tokens, STRIP), lambda i: (0, 0))
    row = pl.BlockSpec((1, STRIP), lambda i: (0, i))
    return pl.pallas_call(
        scan_backward_kernel,
        grid=(width // STRIP,),
        in_specs=[strip, strip, strip, strip, column, column, column, row, row],
        out_specs=[strip, strip, pl.BlockSpec((2, STRIP), lambda i: (0, i))],
        out_shape=(full, full, jax.ShapeDtypeStruct((2, width), f32)),
        compiler_params=pltpu.CompilerParams(vmem_limit_bytes=BIG),
        cost_estimate=pl.CostEstimate(flops=20 * tokens * width, bytes_accessed=24 * tokens * width, transcendentals=4 * tokens * width),
        name="scan_backward",
    )(grad, state, mix_pre, forget_pre, cut, scale, pull, bound, gain)


def join_backward_kernel(local_ref, run_ref, in_ref, forget_ref, prev_ref, cut_ref, far_ref, bound_ref, lower_ref, both_ref, hold):
    @pl.when(pl.program_id(0) == 0)
    def _():
        hold[...] = arriving(far_ref)
        lower_ref[...] = jnp.zeros_like(lower_ref)

    width = local_ref.shape[1]
    total = local_ref[...] + run_ref[...] * hold[...]
    lift = 1.0 - bound_ref[...]
    fade = jax.nn.sigmoid(-forget_ref[...])
    keep = lift * fade
    open_here = 1.0 - cut_ref[...]
    pre = in_ref[...]
    sig = jax.nn.sigmoid(pre)
    d_keep = total * (pre * sig) - total * prev_ref[...] * open_here
    lower_ref[...] -= jnp.sum(d_keep * fade, axis=0, keepdims=True)
    both_ref[:, :width] = (total * keep * (sig * (1.0 + pre * (1.0 - sig)))).astype(both_ref.dtype)
    both_ref[:, width:] = (-d_keep * lift * fade * (1.0 - fade)).astype(both_ref.dtype)
    hold[...] = (1.0 - keep[0:1]) * open_here[0:1] * total[0:1]


def join_backward(local, run, in_pre, forget_pre, prev, cut, far, bound):
    tokens, width = local.shape
    length = tokens // LANES
    block = pl.BlockSpec((length, width), lambda i: (LANES - 1 - i, 0))
    row = pl.BlockSpec((1, width), lambda i: (0, 0))
    return pl.pallas_call(
        join_backward_kernel,
        grid=(LANES,),
        in_specs=[
            block,
            block,
            block,
            block,
            block,
            pl.BlockSpec((length, 1), lambda i: (LANES - 1 - i, 0)),
            pl.BlockSpec(far.shape, lambda i: (0, 0, 0)),
            row,
        ],
        out_specs=[row, pl.BlockSpec((length, 2 * width), lambda i: (LANES - 1 - i, 0))],
        out_shape=(jax.ShapeDtypeStruct((1, width), f32), jax.ShapeDtypeStruct((tokens, 2 * width), bf16)),
        scratch_shapes=[pltpu.VMEM((1, width), f32)],
        compiler_params=pltpu.CompilerParams(vmem_limit_bytes=BIG),
        cost_estimate=pl.CostEstimate(flops=25 * tokens * width, bytes_accessed=24 * tokens * width, transcendentals=4 * tokens * width),
        name="join_backward",
    )(local, run, in_pre, forget_pre, prev, cut, far, bound)


ANY = pl.BlockSpec(memory_space=pl.ANY)


def params():
    return pltpu.CompilerParams(vmem_limit_bytes=BIG)


def cost(flops, moved):
    return pl.CostEstimate(flops=flops, bytes_accessed=moved, transcendentals=0)


def enter_kernel(place, input_ref, kept_ref, came_ref, scale_ref, middle_ref, level_ref):
    middle = input_ref[...].astype(f32) + (kept_ref[...] + came_ref[...]) * scale_ref[...]
    middle_ref[...] = middle
    level_ref[...] = middle * rms_scale(middle)


def enter(place, k, inputs, kept, came, scale):
    rows, width = kept.shape
    steps = 4
    part = rows // steps
    here = pl.BlockSpec((part, width), lambda i, p: (i, 0))
    full = jax.ShapeDtypeStruct((rows, width), f32)
    return pl.pallas_call(
        enter_kernel,
        grid_spec=pltpu.PrefetchScalarGridSpec(
            num_scalar_prefetch=1,
            grid=(steps,),
            in_specs=[
                pl.BlockSpec((part, width), lambda i, p: ((2 * k + p[2]) * steps + i, 0)),
                here,
                here,
                pl.BlockSpec((part, 1), lambda i, p: ((2 * k + p[2]) * steps + i, 0)),
            ],
            out_specs=[here, here],
        ),
        out_shape=(full, full),
        compiler_params=params(),
        cost_estimate=cost(10 * rows * width, 18 * rows * width),
        name="enter",
    )(place, inputs, kept, came, scale)


def feed_kernel(place, mine_ref, theirs_ref, norm_ref, gate_w_ref, up_w_ref, pull_ref, *rest):
    nf_ref, hid_ref, dg_ref, du_ref = rest[-4:]
    rows = mine_ref.shape[0]
    core = place[2]
    norm = norm_ref[...]
    nf_ref[pl.ds(pl.multiple_of(core * rows, rows), rows), :] = (mine_ref[...] * norm).astype(bf16)
    nf_ref[pl.ds(pl.multiple_of((1 - core) * rows, rows), rows), :] = (theirs_ref[...] * norm).astype(bf16)
    nf = nf_ref[...]
    gate = multiply(nf, gate_w_ref[...])
    upward = multiply(nf, up_w_ref[...])
    sig = jax.nn.sigmoid(gate)
    act = gate * sig
    pull = pull_ref[...]
    hid_ref[...] = (act * upward).astype(bf16)
    dg_ref[...] = (pull * upward * (sig * (1.0 + gate * (1.0 - sig)))).astype(bf16)
    du_ref[...] = (pull * act).astype(bf16)


def feed_forward(place, k, mine, theirs, norm, w_gate, w_up, pull, before):
    rows, width = mine.shape
    units = w_gate.shape[1]
    tokens = pull.shape[0]
    once = pl.Buffered(1)
    shapes = [(tokens, width)] + [(tokens, units)] * 3
    outs = [pl.BlockSpec((2 * rows, n), lambda i, p: (k, 0)) for _, n in shapes]
    fixed = [(rows, width), (rows, width), (1, width), (width, units), (width, units)]
    return pl.pallas_call(
        feed_kernel,
        grid_spec=pltpu.PrefetchScalarGridSpec(
            num_scalar_prefetch=1,
            grid=(1,),
            in_specs=[pl.BlockSpec(shape, lambda i, p: (0, 0), pipeline_mode=once) for shape in fixed]
            + [pl.BlockSpec((2 * rows, units), lambda i, p: (k, 0), pipeline_mode=once)]
            + [ANY] * len(before),
            out_specs=outs,
        ),
        out_shape=tuple(jax.ShapeDtypeStruct(shape, bf16) for shape in shapes),
        input_output_aliases={7 + i: i for i in range(len(before))},
        compiler_params=params(),
        cost_estimate=cost(8 * rows * width * units, 4 * width * units + 20 * rows * width),
        name="feed_forward",
    )(place, mine, theirs, norm, w_gate, w_up, pull, *before)


def unfeed_kernel(place, dg_ref, du_ref, gate_w_ref, up_w_ref, mine_ref, theirs_ref):
    core = place[2]
    rows = mine_ref.shape[0]
    for ref, at in ((mine_ref, core), (theirs_ref, 1 - core)):
        here = pl.ds(pl.multiple_of(at * rows, rows), rows)
        ref[...] = outer_cols(dg_ref[here, :], gate_w_ref[...]) + outer_cols(du_ref[here, :], up_w_ref[...])


def unfeed(place, k, d_gate, d_upward, w_gate, w_up):
    tokens, units = d_gate.shape
    width = w_gate.shape[0]
    rows = tokens // 4
    tile = width // 4
    chunk = pl.BlockSpec((2 * rows, units), lambda i, p: (k, 0))
    weight = pl.BlockSpec((tile, units), lambda i, p: (i, 0))
    out = pl.BlockSpec((rows, tile), lambda i, p: (0, i))
    full = jax.ShapeDtypeStruct((rows, width), f32)
    return pl.pallas_call(
        unfeed_kernel,
        grid_spec=pltpu.PrefetchScalarGridSpec(
            num_scalar_prefetch=1, grid=(4,), in_specs=[chunk, chunk, weight, weight], out_specs=[out, out]
        ),
        out_shape=(full, full),
        compiler_params=params(),
        cost_estimate=cost(8 * rows * width * units, 4 * width * units + 20 * rows * width),
        name="unfeed",
    )(place, d_gate, d_upward, w_gate, w_up)


def leave_kernel(place, value_ref, base_ref, kept_ref, came_ref, gain_ref, grad_ref, total_ref, change_ref):
    @pl.when(pl.program_id(0) == 0)
    def _():
        grad_ref[...] = jnp.zeros_like(grad_ref)

    value = value_ref[...].astype(f32)
    scale = rms_scale(value)
    level = value * scale
    grad = kept_ref[...] + came_ref[...]
    weighed = grad * gain_ref[...]
    change = scale * (weighed - level * jnp.mean(weighed * level, axis=-1, keepdims=True))
    grad_ref[...] += jnp.sum(grad * level, axis=0, keepdims=True)
    total_ref[...] = base_ref[...].astype(f32) + change
    change_ref[...] = change


def leave(place, k, value, base, kept, came, gain):
    rows, width = kept.shape
    steps = 4
    part = rows // steps
    here = pl.BlockSpec((part, width), lambda i, p: (i, 0))
    among = pl.BlockSpec((part, width), lambda i, p: ((2 * k + p[2]) * steps + i, 0))
    row = pl.BlockSpec((1, width), lambda i, p: (0, 0))
    full = jax.ShapeDtypeStruct((rows, width), f32)
    return pl.pallas_call(
        leave_kernel,
        grid_spec=pltpu.PrefetchScalarGridSpec(
            num_scalar_prefetch=1,
            grid=(steps,),
            in_specs=[here if v.shape[0] == rows else among for v in (value, base)] + [here, here, row],
            out_specs=[row, here, here],
        ),
        out_shape=(jax.ShapeDtypeStruct((1, width), f32), full, full),
        compiler_params=params(),
        cost_estimate=cost(16 * rows * width, 24 * rows * width),
        name="leave",
    )(place, value, base, kept, came, gain)


def assemble_kernel(place, *refs):
    based = len(refs) == 6
    mine, theirs, whole = (refs[:2], refs[2:4], refs[-1])
    core = place[2]
    for k in range(2):
        for source, at in ((mine[k], core), (theirs[k], 1 - core)):
            value = source[...]
            if based:
                value = value + refs[4][k, at].astype(f32)
            whole[k, at] = value.astype(whole.dtype)


def assemble(place, mine, theirs, kind, base=None):
    rows, width = mine[0].shape
    steps = 8
    part = rows // steps
    block = pl.BlockSpec((part, width), lambda i, p: (i, 0))
    whole = pl.BlockSpec((2, 2, part, width), lambda i, p: (0, 0, i, 0))
    extra = [] if base is None else [base.reshape(2, 2, rows, width)]
    return pl.pallas_call(
        assemble_kernel,
        grid_spec=pltpu.PrefetchScalarGridSpec(
            num_scalar_prefetch=1, grid=(steps,), in_specs=[block] * 4 + [whole] * len(extra), out_specs=whole
        ),
        out_shape=jax.ShapeDtypeStruct((2, 2, rows, width), kind),
        compiler_params=params(),
        cost_estimate=cost(0, 32 * rows * width),
        name="assemble",
    )(place, *mine, *theirs, *extra).reshape(4 * rows, width)


def weigh_kernel(pairs, place, *refs):
    out_ref = refs[-1]
    at = 0
    for i in range(pairs):
        value = inner_rows(refs[2 * i][...], refs[2 * i + 1][...])
        wide = value.shape[1]
        if len(refs) > 2 * pairs + 1:
            value = value + refs[2 * pairs][0, :, at : at + wide]
        out_ref[0, :, at : at + wide] = value
        at += wide


def weigh(place, pairs, side, add=None, first=0, count=None):
    deep = DEEP
    count = deep if count is None else count
    rows = pairs[0][0].shape[1] // (2 * deep)
    wide = sum(right.shape[1] for _, right in pairs)
    specs, values = ([], [])
    for left, right in pairs:
        specs.append(
            pl.BlockSpec(
                (left.shape[0], rows), lambda j, p: (0, 2 * lax.rem(p[0] + first + j, deep) + (p[1] if side == 0 else 1 - p[1]))
            )
        )
        specs.append(pl.BlockSpec(right.shape, lambda j, p: (0, 0)))
        values += [left, right]
    if add is not None:
        specs.append(pl.BlockSpec((1, rows, wide), lambda j, p: (j, 0, 0)))
        values.append(add)
    tokens = pairs[0][0].shape[0]
    return pl.pallas_call(
        functools.partial(weigh_kernel, len(pairs)),
        grid_spec=pltpu.PrefetchScalarGridSpec(
            num_scalar_prefetch=1,
            grid=(count,),
            in_specs=specs,
            out_specs=pl.BlockSpec((1, rows, wide), lambda j, p: (j, 0, 0)),
        ),
        out_shape=jax.ShapeDtypeStruct((count, rows, wide), f32),
        compiler_params=params(),
        cost_estimate=cost(2 * tokens * rows * count * wide, 2 * tokens * (wide + rows * count) + 8 * rows * count * wide),
        name="weigh",
    )(place, *values)


SEQ, MP, DEEP = 8, 4, 4
CORE = [(i, i ^ 1) for i in range(MP)]
ACROSS = [(i, i ^ 2) for i in range(MP)]
BESIDE = [(i, i ^ 1) for i in range(SEQ)]
UP = [[(2 * z + y, 2 * z + 2 + y) for z in range(t) for y in range(2)] for t in range(DEEP)]
DOWN = [[(2 * z + y, 2 * z - 2 + y) for z in range(DEEP - t, DEEP) for y in range(2)] for t in range(DEEP)]


def over_core(v):
    return lax.ppermute(v, "mp", CORE)


def over_x(v):
    return lax.ppermute(v, "mp", ACROSS)


def over_y(v):
    return lax.ppermute(v, "seq", BESIDE)


class Order:
    def __init__(self):
        self.last = ()

    def __call__(self, work, *values):
        values, _ = together((values, self.last))
        done = work(*values)
        self.last = done
        return done


class Line:
    def __init__(self, order, blocks):
        self.order = order
        self.blocks = blocks
        self.step = 0
        self.up = self.down = None

    def advance(self):
        self.step += 1
        t = self.step

        def pick(blocks, *came):
            up, down = (blocks[DEEP - t], blocks[t])
            return (up + came[0], down + came[1]) if came else (up, down)

        came = () if self.up is None else (self.up, self.down)
        up, down = together(self.order(pick, self.blocks, *came))
        self.up = lax.ppermute(up, "seq", UP[t])
        self.down = lax.ppermute(down, "seq", DOWN[t])

    def result(self):
        return self.order(lambda blocks, up, down: blocks[0] + up + down, self.blocks, self.up, self.down)


def gathered(order, whole, y, reverse):
    rounds = [whole]
    for k in range(1, DEEP):
        pairs = [(2 * z + i, 2 * (z + k) + i) for z in range(DEEP - k) for i in range(2)]
        rounds.append(lax.ppermute(whole, "seq", [(b, a) for a, b in pairs] if reverse else pairs))
    return rounds


def ranked(order, mine, y, reverse):
    theirs = over_y(mine)

    def rank(mine, theirs):
        later = (y == 0) if reverse else (y == 1)
        parts = []
        for k in range(DEEP - 1, 0, -1):
            parts += [jnp.where(later, theirs[k], mine[k]), jnp.where(later, mine[k], theirs[k])]
        nothing = jnp.concatenate([jnp.ones_like(mine[0, :1]), jnp.zeros_like(mine[0, :1])])
        parts.append(jnp.where(later, theirs[0], nothing))
        return jnp.stack(parts)

    return theirs, rank


def planned(
    inputs, seq_start, norm_in, w_input, w_forget, w_mix_gate, lower_bound, mix_gain, w_output, norm_ffn, w_gate, w_up, w_down, cotangent
):
    tokens, width = inputs.shape
    quarter = tokens // 4
    seq = lax.axis_index("seq")
    core = lax.axis_index("mp") % 2
    y = seq % 2
    place = jnp.stack([seq // 2, y, core])
    bound = lower_bound[None, :]
    gain = mix_gain[None, :]
    step = Order()

    def quarters(v, at):
        parts = v.reshape((2, 2, quarter) + v.shape[1:])
        return lax.dynamic_index_in_dim(parts, at, 1, keepdims=False)

    def own(v):
        return quarters(v, core)

    def other(v):
        return quarters(v, 1 - core)

    places = seq * tokens + jnp.arange(tokens, dtype=jnp.int32)
    cut = (seq_start == places).astype(f32)[:, None]
    cut_wide = jnp.broadcast_to(cut, (tokens, STRIP))
    in_float = inputs.astype(f32)
    normed = (in_float * rms_scale(in_float) * norm_in).astype(bf16)
    in_pre = multiply(normed, w_input)
    forget_pre = multiply(normed, w_forget)
    local, run, whole, forget_local = step(scan_forward, in_pre, forget_pre, cut_wide, bound)
    rounds = gathered(step, whole, y, False)
    mix_pre = step(multiply, normed, w_mix_gate)
    mine = step(lambda *v: jnp.stack(v), *rounds)
    theirs, rank = ranked(step, mine, y, False)
    far = step(rank, mine, theirs)
    state, prev, weighed = step(join_forward, local, run, mix_pre, far, gain)

    squares = step(lambda v: jnp.sum(v * v, axis=1), state)
    squares_came = over_core(squares)
    sent = [over_core(step(lambda v, w: multiply(other(v)[0], w), weighed, w_output)), None]
    squares = step(lambda a, b: a + b, squares, squares_came)
    squares_came = over_x(squares)
    sent[1] = over_core(step(lambda v, w: multiply(other(v)[1], w), weighed, w_output))
    crossing = []
    for k in range(2):
        kept = step(lambda v, w, s: multiply(own(v)[k], w) + s, weighed, w_output, sent[k])
        crossing.append((kept, over_x(kept)))
    mix_scale = step(lambda a, b: lax.rsqrt((a + b) / width + epsilon)[:, None], squares, squares_came)
    pull_hidden = step(outer_cols, cotangent, w_down)

    middle, across = ([], [])
    buffers = ()
    norm = norm_ffn[None, :]
    for k in range(2):
        kept, came = crossing[k]
        mid, level = step(functools.partial(enter, place, k), inputs, kept, came, mix_scale)
        middle.append(mid)
        level_theirs = over_core(level)
        buffers = step(
            lambda *v: feed_forward(place, k, *v[:6], v[6:]), level, level_theirs, norm, w_gate, w_up, pull_hidden, *buffers
        )
        if k == 0:
            part_mine, part_theirs = step(functools.partial(unfeed, place, k), buffers[2], buffers[3], w_gate, w_up)
            part_came = over_core(part_theirs)
            kept = step(lambda a, b: a + b, part_mine, part_came)
            across.append((kept, over_x(kept)))
    nf, hidden, d_gate, d_upward = buffers

    wide = 1024 * hidden.shape[1] // 1408

    def weight(pairs, side, **how):
        flat = [v for pair in pairs for v in pair]
        return lambda *v: weigh(place, [(v[2 * i], v[2 * i + 1]) for i in range(len(pairs))], side, **how), flat

    def weights(pairs, side, add=None, **how):
        flat = [v for pair in pairs for v in pair]

        def work(*v):
            split = [(v[2 * i], v[2 * i + 1]) for i in range(len(pairs))]
            return weigh(place, split, side, add=v[-1] if add is not None else None, **how)

        return step(work, *flat, *(() if add is None else (add,)))

    def send_y(pairs):
        return [over_y(weights(pairs, 1, first=first, count=2)) for first in (0, 2)]

    def keep_y(pairs, came):
        return Line(step, weights(pairs, 0, add=jnp.concatenate(came)))

    hid_first, hid_rest = step(lambda v: (v[:, :wide], v[:, wide:]), hidden)
    down_other = Line(step, weights([(cotangent, hid_first)], 1))
    down_other.advance()
    down_own = Line(step, weights([(cotangent, hid_first)], 0))
    down_own.advance()
    gate_pairs, up_pairs, rest_pairs = ([(nf, d_gate)], [(nf, d_upward)], [(cotangent, hid_rest)])
    gate_came = send_y(gate_pairs)

    part_mine, part_theirs = step(functools.partial(unfeed, place, 1), d_gate, d_upward, w_gate, w_up)
    part_came = over_core(part_theirs)
    kept = step(lambda a, b: a + b, part_mine, part_came)
    across.append((kept, over_x(kept)))

    down_other.advance()
    fed_theirs = step(lambda v, w: multiply(other(v).reshape(2 * quarter, -1), w), hidden, w_down)
    fed_came = over_core(fed_theirs)
    fed = step(lambda v, w, s: multiply(own(v).reshape(2 * quarter, -1), w) + s, hidden, w_down, fed_came)
    down_own.advance()

    d_middle, change, change_came, norm_parts = ([], [], [], [])
    for k in range(2):
        grad, total, delta = step(functools.partial(leave, place, k), middle[k], cotangent, across[k][0], across[k][1], norm)
        d_middle.append(total)
        change.append(delta)
        change_came.append(over_core(delta))
        norm_parts.append(grad)
        if k == 0:
            down_other.advance()
    d_branch = step(
        lambda a, b, c, d, e: assemble(place, (a, b), (c, d), bf16, e), change[0], change[1], change_came[0], change_came[1], cotangent
    )
    d_mixed = step(outer_cols, d_branch, w_output)

    def gates(d_mixed, state, mix_pre, mix_scale):
        act = jax.nn.silu(mix_pre)
        return jnp.sum(d_mixed * gain * act * state, axis=1)

    cross = step(gates, d_mixed, state, mix_pre, mix_scale)
    cross_came = over_core(cross)

    def mixing(d_mixed, state, mix_pre, mix_scale):
        act = jax.nn.silu(mix_pre)
        level = state * mix_scale
        return (
            (level * gain * act).astype(bf16),
            (d_mixed * level * gain * silu_slope(mix_pre)).astype(bf16),
            jnp.sum(d_mixed * level * act, axis=0),
        )

    down_own.advance()
    cross = step(lambda a, b: a + b, cross, cross_came)
    cross_came = over_x(cross)
    mixed, d_mix_pre, d_mix_gain = step(mixing, d_mixed, state, mix_pre, mix_scale)
    pull = step(lambda a, b, s: s**3 * ((a + b)[:, None] / width), cross, cross_came, mix_scale)
    fed, _ = together((fed, cross_came))
    fed_across = over_x(fed)
    local, run, whole = step(
        lambda *v: scan_backward(
            *v[:4], cut_wide, jnp.broadcast_to(v[4], (tokens, STRIP)), jnp.broadcast_to(v[5], (tokens, STRIP)), bound, gain
        ),
        d_mixed,
        state,
        mix_pre,
        forget_pre,
        mix_scale,
        pull,
    )
    rounds = gathered(step, whole, y, True)
    down_theirs = down_other.result()
    down_mine = down_own.result()
    mine = step(lambda *v: jnp.stack(v), *rounds)
    theirs, rank = ranked(step, mine, y, True)
    gate = keep_y(gate_pairs, gate_came)
    gate.advance()
    up_came = send_y(up_pairs)
    far = step(rank, mine, theirs)
    d_lower, d_both = step(join_backward, local, run, in_pre, forget_pre, prev, cut, far, bound)
    units = in_pre.shape[1]

    def partial_input(rows, both, mix, wi, wf, wm):
        both = rows(both).reshape(2 * quarter, -1)
        mix = rows(mix).reshape(2 * quarter, -1)
        return outer_cols(both[:, :units], wi) + outer_cols(both[:, units:], wf) + outer_cols(mix, wm)

    part = step(functools.partial(partial_input, other), d_both, d_mix_pre, w_input, w_forget, w_mix_gate)
    part_came = over_core(part)
    normed_kept = step(
        lambda *v: partial_input(own, *v[:5]) + v[5], d_both, d_mix_pre, w_input, w_forget, w_mix_gate, part_came
    )
    normed_across = over_x(normed_kept)
    gate.advance()
    rest_came = over_y(weights(rest_pairs, 1))
    gate.advance()
    mix_pairs, both_pairs = ([(normed, d_mix_pre), (d_branch, mixed)], [(normed, d_both)])
    up = keep_y(up_pairs, up_came)
    up.advance()
    mix_came = send_y(mix_pairs)
    gate_grad = gate.result()
    rest = Line(step, weights(rest_pairs, 0, add=rest_came))
    rest.advance()
    up.advance()
    out_own = step(lambda a, b, c, d: jnp.concatenate([a, b]) + c + d, middle[0], middle[1], fed, fed_across)
    out_came = over_core(out_own)
    rest.advance()
    up.advance()
    out = step(
        lambda a, b: assemble(place, (a[:quarter], a[quarter:]), (b[:quarter], b[quarter:]), bf16), out_own, out_came
    )
    rest.advance()
    mix = keep_y(mix_pairs, mix_came)
    mix.advance()
    both_came = send_y(both_pairs)
    up_grad = up.result()
    rest_grad = rest.result()

    d_inputs, norm_in_parts = ([], [])
    for k in range(2):
        rows = slice(k * quarter, (k + 1) * quarter)
        grad, total, _ = step(
            lambda v, d, a, b, g: leave(place, k, v, d, a[rows], b[rows], g), inputs, d_middle[k], normed_kept, normed_across, norm_in[None, :]
        )
        d_inputs.append(total)
        norm_in_parts.append(grad)
    mix.advance()
    inputs_came = [over_core(v) for v in d_inputs]
    norms = step(lambda a, b, c, d: jnp.concatenate([a + b, c + d], axis=1)[0], *norm_in_parts, *norm_parts)
    norms_came = over_core(norms)
    d_inputs = step(lambda a, b, c, d: assemble(place, (a, b), (c, d), f32), *d_inputs, *inputs_came)
    smalls = step(
        lambda a, b, c, d, e: jnp.concatenate([a + b, c, d, e]), norms, norms_came, d_lower[0], d_mix_gain, forget_local[0]
    )
    mix.advance()
    down_came = over_y(step(lambda v: v + 0.0, down_theirs))
    for bit in (1, 2, 4):
        came = lax.ppermute(smalls, "seq", [(i, i ^ bit) for i in range(SEQ)])
        smalls = step(lambda a, b: a + b, smalls, came)
    both = keep_y(both_pairs, both_came)
    both.advance()
    piece = width // SEQ
    d_norm_in = lax.dynamic_slice_in_dim(smalls, seq * piece, piece)
    d_norm_ffn = lax.dynamic_slice_in_dim(smalls, width + seq * piece, piece)
    d_lower, d_mix_gain, forget_sum = (smalls[2 * width + i * units : 2 * width + (i + 1) * units] for i in range(3))
    mix_grad = mix.result()
    out_grad = step(lambda v: v[:, units:].T, mix_grad)
    both.advance()
    down_grad = step(lambda a, b, c: jnp.concatenate([a + b, c], axis=1).T, down_mine, down_came, rest_grad)
    both.advance()
    both_grad = both.result()
    return (
        out,
        d_inputs,
        d_norm_in,
        both_grad[:, :units],
        both_grad[:, units:],
        mix_grad[:, :units],
        d_lower,
        d_mix_gain,
        out_grad,
        d_norm_ffn,
        gate_grad,
        up_grad,
        down_grad,
        forget_sum / (tokens * SEQ),
    )


def entering(x, axis, combine, identity, reverse):
    length, index = (lax.axis_size(axis), lax.axis_index(axis))
    everything = jax.tree.map(lambda part: lax.all_gather(part, axis), x)
    start = jax.tree.map(
        lambda part, zero: jnp.broadcast_to(jnp.asarray(zero, part.dtype), part.shape), x, identity
    )

    def turn(k, before):
        at = length - 1 - k if reverse else k
        reached = at > index if reverse else at < index
        new = combine(before, jax.tree.map(lambda part: part[at], everything))
        return jax.tree.map(lambda a, b: jnp.where(reached, a, b), new, before)

    return lax.fori_loop(0, length, turn, start)


def compose(earlier, later):
    return (earlier[0] * later[0], later[0] * earlier[1] + later[1])


def carry_forward(whole, ending):
    result = entering(
        (whole, ending), "seq", compose, (jnp.ones_like(whole), jnp.zeros_like(ending)), False
    )
    return result[1]


def carry_backward(whole, leading):
    result = entering(
        (whole, leading), "seq", compose, (jnp.ones_like(whole), jnp.zeros_like(leading)), True
    )
    return result[1]


def general(
    inputs,
    seq_start,
    norm_in,
    w_input,
    w_forget,
    w_mix_gate,
    lower_bound,
    mix_gain,
    w_output,
    norm_ffn,
    w_gate,
    w_up,
    w_down,
    cotangent,
):
    tokens_here = inputs.shape[0]
    width = inputs.shape[1]
    places = lax.axis_index("seq") * tokens_here + jnp.arange(tokens_here, dtype=jnp.int32)
    restart = (seq_start == places).astype(jnp.float32)[:, None]
    in_float = inputs.astype(jnp.float32)
    scale_in = rms_scale(in_float)
    normed = (in_float * scale_in * norm_in).astype(jnp.bfloat16)
    in_pre = multiply(normed, w_input)
    forget_pre = multiply(normed, w_forget)
    mix_pre = multiply(normed, w_mix_gate)
    fade = jax.nn.sigmoid(-forget_pre)
    forget_local = jnp.sum(1.0 - fade, axis=0)
    keep = (1.0 - lower_bound) * fade
    decay = (1.0 - keep) * (1.0 - restart)
    act_in = jax.nn.silu(in_pre)
    drive = act_in * keep
    decay_run, state_local = lax.associative_scan(compose, (decay, drive), axis=0)
    state_in = carry_forward(decay_run[-1], state_local[-1])
    state = state_local + decay_run * state_in
    squares = lax.psum(jnp.sum(state * state, axis=1), "mp")
    mix_scale = lax.rsqrt(squares / width + epsilon)[:, None]
    gate_act = jax.nn.silu(mix_pre)
    normed_state = state * mix_scale
    mixed = (normed_state * mix_gain * gate_act).astype(jnp.bfloat16)
    branch = lax.psum(multiply(mixed, w_output), "mp")
    middle = in_float + branch
    scale_ffn = rms_scale(middle)
    normed_ffn = (middle * scale_ffn * norm_ffn).astype(jnp.bfloat16)
    gate = multiply(normed_ffn, w_gate)
    upward = multiply(normed_ffn, w_up)
    silu_gate = jax.nn.silu(gate)
    hidden = (silu_gate * upward).astype(jnp.bfloat16)
    feed = lax.psum(multiply(hidden, w_down), "mp")
    out = (middle + feed).astype(jnp.bfloat16)
    grad_float = cotangent.astype(jnp.float32)
    d_hidden = outer_cols(cotangent, w_down)
    d_w_down = inner_rows(hidden, cotangent)
    d_gate = (d_hidden * upward * silu_slope(gate)).astype(jnp.bfloat16)
    d_upward = (d_hidden * silu_gate).astype(jnp.bfloat16)
    d_normed_ffn = lax.psum(outer_cols(d_gate, w_gate) + outer_cols(d_upward, w_up), "mp")
    d_w_gate = inner_rows(normed_ffn, d_gate)
    d_w_up = inner_rows(normed_ffn, d_upward)
    d_norm_ffn = jnp.sum(d_normed_ffn * middle * scale_ffn, axis=0)
    scaled_ffn = d_normed_ffn * norm_ffn
    d_middle = (
        grad_float
        + scale_ffn * scaled_ffn
        - middle * scale_ffn**3 * jnp.mean(scaled_ffn * middle, axis=-1, keepdims=True)
    )
    d_branch = d_middle.astype(jnp.bfloat16)
    d_w_output = inner_rows(mixed, d_branch)
    d_mixed = outer_cols(d_branch, w_output)
    d_mix_gain = jnp.sum(d_mixed * normed_state * gate_act, axis=0)
    d_mix_pre = (d_mixed * normed_state * mix_gain * silu_slope(mix_pre)).astype(jnp.bfloat16)
    scaled_mix = d_mixed * mix_gain * gate_act
    cross = lax.psum(jnp.sum(scaled_mix * state, axis=1), "mp")
    d_state = mix_scale * scaled_mix - state * mix_scale**3 * (cross / width)[:, None]
    next_decay = jnp.concatenate([decay[1:], jnp.ones_like(decay[:1])], axis=0)
    tail_decay, tail_grad = lax.associative_scan(
        compose, (next_decay, d_state), reverse=True, axis=0
    )
    carried = carry_backward(decay_run[-1], decay[0] * tail_grad[0])
    total = tail_grad + tail_decay * carried
    prev_state = jnp.concatenate([state_in[None], state[:-1]], axis=0)
    d_keep = total * act_in - total * prev_state * (1.0 - restart)
    d_lower = -jnp.sum(d_keep * fade, axis=0)
    d_in_pre = (total * keep * silu_slope(in_pre)).astype(jnp.bfloat16)
    d_forget_pre = (-d_keep * (1.0 - lower_bound) * fade * (1.0 - fade)).astype(jnp.bfloat16)
    d_normed = lax.psum(
        outer_cols(d_in_pre, w_input)
        + outer_cols(d_forget_pre, w_forget)
        + outer_cols(d_mix_pre, w_mix_gate),
        "mp",
    )
    d_w_input = inner_rows(normed, d_in_pre)
    d_w_forget = inner_rows(normed, d_forget_pre)
    d_w_mix_gate = inner_rows(normed, d_mix_pre)
    d_norm_in = jnp.sum(d_normed * in_float * scale_in, axis=0)
    scaled_in = d_normed * norm_in
    d_inputs = (
        d_middle
        + scale_in * scaled_in
        - in_float * scale_in**3 * jnp.mean(scaled_in * in_float, axis=-1, keepdims=True)
    )
    row_part = (
        lax.psum_scatter(d_w_input, "seq", scatter_dimension=0, tiled=True),
        lax.psum_scatter(d_w_forget, "seq", scatter_dimension=0, tiled=True),
        lax.psum_scatter(d_w_mix_gate, "seq", scatter_dimension=0, tiled=True),
        lax.psum_scatter(d_w_gate, "seq", scatter_dimension=0, tiled=True),
        lax.psum_scatter(d_w_up, "seq", scatter_dimension=0, tiled=True),
        lax.psum_scatter(d_norm_in, "seq", scatter_dimension=0, tiled=True),
        lax.psum_scatter(d_norm_ffn, "seq", scatter_dimension=0, tiled=True),
    )
    col_part = (
        lax.psum_scatter(d_w_output, "seq", scatter_dimension=1, tiled=True),
        lax.psum_scatter(d_w_down, "seq", scatter_dimension=1, tiled=True),
    )
    out_grad = col_part[0]
    down_grad = col_part[1]
    small_part = lax.psum((d_lower, d_mix_gain, forget_local), "seq")
    forget_mean = small_part[2] / (tokens_here * lax.axis_size("seq"))
    return (
        out,
        d_inputs,
        row_part[5],
        row_part[0],
        row_part[1],
        row_part[2],
        small_part[0],
        small_part[1],
        out_grad,
        row_part[6],
        row_part[3],
        row_part[4],
        down_grad,
        forget_mean,
    )


def solution(mesh):
    fits = mesh.shape["seq"] == SEQ and mesh.shape["mp"] == MP
    return jax.shard_map(
        planned if fits else general,
        mesh=mesh,
        in_specs=(
            P("seq", None),
            P("seq"),
            P(),
            P(None, "mp"),
            P(None, "mp"),
            P(None, "mp"),
            P("mp"),
            P("mp"),
            P("mp", None),
            P(),
            P(None, "mp"),
            P(None, "mp"),
            P("mp", None),
            P("seq", None),
        ),
        out_specs=(
            P("seq", None),
            P("seq", None),
            P("seq"),
            P("seq", "mp"),
            P("seq", "mp"),
            P("seq", "mp"),
            P("mp"),
            P("mp"),
            P("mp", "seq"),
            P("seq"),
            P("seq", "mp"),
            P("seq", "mp"),
            P("mp", "seq"),
            P("mp"),
        ),
        check_vma=False,
    )
```

```python
import functools

import jax
import jax.numpy as jnp
from jax import lax
from jax.experimental import pallas as pl
from jax.experimental.pallas import tpu as pltpu
from jax.sharding import PartitionSpec as P

epsilon = 1e-06
f32 = jnp.float32
bf16 = jnp.bfloat16
together = lax.optimization_barrier


def multiply(left, right):
    return jnp.dot(left, right, preferred_element_type=f32)


def inner_rows(left, right):
    return lax.dot_general(left, right, (((0,), (0,)), ((), ())), preferred_element_type=f32)


def outer_cols(left, right):
    return lax.dot_general(left, right, (((1,), (1,)), ((), ())), preferred_element_type=f32)


def rms_scale(values):
    return lax.rsqrt(jnp.mean(values * values, axis=-1, keepdims=True) + epsilon)


def silu_slope(values):
    sig = jax.nn.sigmoid(values)
    return sig * (1.0 + values * (1.0 - sig))


BIG = 48 * 1024 * 1024
ANY = pl.BlockSpec(memory_space=pl.ANY)


def params():
    return pltpu.CompilerParams(vmem_limit_bytes=BIG)


def light():
    return pl.CostEstimate(flops=0, bytes_accessed=1024, transcendentals=0)


ROWS = 8
STEPS = 4


def scan_forward_kernel(in_ref, forget_ref, cut_ref, bound_ref, local_ref, run_ref, whole_ref, sum_ref, carry):
    @pl.when(pl.program_id(0) == 0)
    def _():
        carry[0:1, :] = jnp.ones_like(carry[0:1, :])
        carry[1:2, :] = jnp.zeros_like(carry[1:2, :])
        sum_ref[...] = jnp.zeros_like(sum_ref)

    lift = 1.0 - bound_ref[...]
    shape = (ROWS, forget_ref.shape[1])
    row = lax.broadcasted_iota(jnp.int32, shape, 0)

    def step(i, before):
        product, state, gates = before
        at = pl.ds(pl.multiple_of(i * ROWS, ROWS), ROWS)
        fade = jax.nn.sigmoid(-forget_ref[at, :])
        keep = lift * fade
        a = (1.0 - keep) * (1.0 - cut_ref[at, :])
        pre = in_ref[at, :]
        b = pre * jax.nn.sigmoid(pre) * keep
        for s in (1, 2, 4):
            reach = row >= s
            b = b + a * jnp.where(reach, pltpu.roll(b, s, 0), 0.0)
            a = a * jnp.where(reach, pltpu.roll(a, s, 0), 1.0)
        b = b + a * state
        a = a * product
        local_ref[at, :] = b
        run_ref[at, :] = a
        return a[ROWS - 1 :, :], b[ROWS - 1 :, :], gates + (1.0 - fade)

    start = (carry[0:1, :], carry[1:2, :], jnp.zeros(shape, f32))
    product, state, gates = lax.fori_loop(0, forget_ref.shape[0] // ROWS, step, start, unroll=4)
    carry[0:1, :] = product
    carry[1:2, :] = state
    whole_ref[...] = carry[...]
    sum_ref[...] += jnp.sum(gates, axis=0, keepdims=True)


def scan_forward(in_pre, forget_pre, cut, bound):
    tokens, width = in_pre.shape
    full = jax.ShapeDtypeStruct((tokens, width), f32)
    block = pl.BlockSpec((tokens // STEPS, width), lambda i: (i, 0))
    row = pl.BlockSpec((1, width), lambda i: (0, 0))
    return pl.pallas_call(
        scan_forward_kernel,
        grid=(STEPS,),
        in_specs=[block, block, pl.BlockSpec((tokens // STEPS, 1), lambda i: (i, 0)), row],
        out_specs=[block, block, pl.BlockSpec((2, width), lambda i: (0, 0)), row],
        out_shape=(full, full, jax.ShapeDtypeStruct((2, width), f32), jax.ShapeDtypeStruct((1, width), f32)),
        scratch_shapes=[pltpu.VMEM((2, width), f32)],
        compiler_params=params(),
        cost_estimate=light(),
        name="scan_forward",
    )(in_pre, forget_pre, cut, bound)


def arriving(mine_ref, theirs_ref, later):
    def over(pair, total):
        return pair[0] * total + pair[1]

    total = jnp.zeros_like(mine_ref[0, 0:1, :])
    for k in range(mine_ref.shape[0] - 1, -1, -1):
        mine, theirs = ((ref[k, 0:1, :], ref[k, 1:2, :]) for ref in (mine_ref, theirs_ref))
        if k == 0:
            return jnp.where(later, over(theirs, total), total)
        total = jnp.where(later, over(mine, over(theirs, total)), over(theirs, over(mine, total)))


def join_forward_kernel(place, local_ref, run_ref, mix_ref, mine_ref, theirs_ref, gain_ref, state_ref, prev_ref, u_ref, square_ref, hold):
    @pl.when(pl.program_id(0) == 0)
    def _():
        hold[0:1, :] = arriving(mine_ref, theirs_ref, place[1] == 1)
        hold[1:2, :] = hold[0:1, :]

    state = local_ref[...] + run_ref[...] * hold[0:1, :]
    mix = mix_ref[...]
    rows = lax.broadcasted_iota(jnp.int32, state.shape, 0)
    state_ref[...] = state
    prev_ref[...] = jnp.where(rows == 0, hold[1:2, :], pltpu.roll(state, 1, 0))
    u_ref[...] = (state * gain_ref[...] * (mix * jax.nn.sigmoid(mix))).astype(u_ref.dtype)
    square_ref[...] = jnp.sum(state * state, axis=1, keepdims=True)
    hold[1:2, :] = state[state.shape[0] - 1 :, :]


def join_forward(place, local, run, mix_pre, mine, theirs, gain):
    tokens, width = local.shape
    length = tokens // STEPS
    block = pl.BlockSpec((length, width), lambda i, p: (i, 0))
    pairs = pl.BlockSpec(mine.shape, lambda i, p: (0, 0, 0))
    row = pl.BlockSpec((1, width), lambda i, p: (0, 0))
    full = jax.ShapeDtypeStruct((tokens, width), f32)
    return pl.pallas_call(
        join_forward_kernel,
        grid_spec=pltpu.PrefetchScalarGridSpec(
            num_scalar_prefetch=1,
            grid=(STEPS,),
            in_specs=[block, block, block, pairs, pairs, row],
            out_specs=[block, block, block, pl.BlockSpec((length, 1), lambda i, p: (i, 0))],
            scratch_shapes=[pltpu.VMEM((2, width), f32)],
        ),
        out_shape=(full, full, jax.ShapeDtypeStruct((tokens, width), bf16), jax.ShapeDtypeStruct((tokens, 1), f32)),
        compiler_params=params(),
        cost_estimate=light(),
        name="join_forward",
    )(place, local, run, mix_pre, mine, theirs, gain)


def scan_backward_kernel(
    grad_ref, state_ref, mix_ref, forget_ref, cut_ref, scale_ref, pull_ref, bound_ref, gain_ref, local_ref, run_ref, whole_ref, carry
):
    @pl.when(pl.program_id(0) == 0)
    def _():
        carry[0:1, :] = jnp.ones_like(carry[0:1, :])
        carry[1:2, :] = jnp.zeros_like(carry[1:2, :])

    lift = 1.0 - bound_ref[...]
    gain = gain_ref[...]
    row = lax.broadcasted_iota(jnp.int32, (ROWS, forget_ref.shape[1]), 0)
    blocks = forget_ref.shape[0] // ROWS

    def step(i, after):
        product, message = after
        at = pl.ds(pl.multiple_of((blocks - 1 - i) * ROWS, ROWS), ROWS)
        a = (1.0 - lift * jax.nn.sigmoid(-forget_ref[at, :])) * (1.0 - cut_ref[at, :])
        mix = mix_ref[at, :]
        weighed = grad_ref[at, :] * gain * (mix * jax.nn.sigmoid(mix))
        own = scale_ref[at, :] * weighed - state_ref[at, :] * pull_ref[at, :]
        b = a * own
        for s in (1, 2, 4):
            reach = row < ROWS - s
            b = b + a * jnp.where(reach, pltpu.roll(b, ROWS - s, 0), 0.0)
            a = a * jnp.where(reach, pltpu.roll(a, ROWS - s, 0), 1.0)
        b = b + a * message
        a = a * product
        last = row == ROWS - 1
        local_ref[at, :] = own + jnp.where(last, message, pltpu.roll(b, ROWS - 1, 0))
        run_ref[at, :] = jnp.where(last, product, pltpu.roll(a, ROWS - 1, 0))
        return a[0:1, :], b[0:1, :]

    product, message = lax.fori_loop(0, blocks, step, (carry[0:1, :], carry[1:2, :]), unroll=4)
    carry[0:1, :] = product
    carry[1:2, :] = message
    whole_ref[...] = carry[...]


def scan_backward(grad, state, mix_pre, forget_pre, cut, scale, pull, bound, gain):
    tokens, width = grad.shape
    full = jax.ShapeDtypeStruct((tokens, width), f32)
    block = pl.BlockSpec((tokens // STEPS, width), lambda i: (STEPS - 1 - i, 0))
    column = pl.BlockSpec((tokens // STEPS, 1), lambda i: (STEPS - 1 - i, 0))
    row = pl.BlockSpec((1, width), lambda i: (0, 0))
    return pl.pallas_call(
        scan_backward_kernel,
        grid=(STEPS,),
        in_specs=[block, block, block, block, column, column, column, row, row],
        out_specs=[block, block, pl.BlockSpec((2, width), lambda i: (0, 0))],
        out_shape=(full, full, jax.ShapeDtypeStruct((2, width), f32)),
        scratch_shapes=[pltpu.VMEM((2, width), f32)],
        compiler_params=params(),
        cost_estimate=light(),
        name="scan_backward",
    )(grad, state, mix_pre, forget_pre, cut, scale, pull, bound, gain)


def join_backward_kernel(
    place, local_ref, run_ref, in_ref, forget_ref, prev_ref, cut_ref, mine_ref, theirs_ref, bound_ref, lower_ref, both_ref, hold
):
    @pl.when(pl.program_id(0) == 0)
    def _():
        hold[...] = arriving(mine_ref, theirs_ref, place[1] == 0)
        lower_ref[...] = jnp.zeros_like(lower_ref)

    width = local_ref.shape[1]
    total = local_ref[...] + run_ref[...] * hold[...]
    lift = 1.0 - bound_ref[...]
    fade = jax.nn.sigmoid(-forget_ref[...])
    keep = lift * fade
    pre = in_ref[...]
    sig = jax.nn.sigmoid(pre)
    d_keep = total * (pre * sig) - total * prev_ref[...] * (1.0 - cut_ref[...])
    lower_ref[...] -= jnp.sum(d_keep * fade, axis=0, keepdims=True)
    both_ref[:, :width] = (total * keep * (sig * (1.0 + pre * (1.0 - sig)))).astype(both_ref.dtype)
    both_ref[:, width:] = (-d_keep * lift * fade * (1.0 - fade)).astype(both_ref.dtype)


def join_backward(place, local, run, in_pre, forget_pre, prev, cut, mine, theirs, bound):
    tokens, width = local.shape
    length = tokens // STEPS
    block = pl.BlockSpec((length, width), lambda i, p: (i, 0))
    column = pl.BlockSpec((length, 1), lambda i, p: (i, 0))
    pairs = pl.BlockSpec(mine.shape, lambda i, p: (0, 0, 0))
    row = pl.BlockSpec((1, width), lambda i, p: (0, 0))
    return pl.pallas_call(
        join_backward_kernel,
        grid_spec=pltpu.PrefetchScalarGridSpec(
            num_scalar_prefetch=1,
            grid=(STEPS,),
            in_specs=[block] * 5 + [column, pairs, pairs, row],
            out_specs=[row, pl.BlockSpec((length, 2 * width), lambda i, p: (i, 0))],
            scratch_shapes=[pltpu.VMEM((1, width), f32)],
        ),
        out_shape=(jax.ShapeDtypeStruct((1, width), f32), jax.ShapeDtypeStruct((tokens, 2 * width), bf16)),
        compiler_params=params(),
        cost_estimate=light(),
        name="join_backward",
    )(place, local, run, in_pre, forget_pre, prev, cut, mine, theirs, bound)


def mixing_kernel(grad_ref, state_ref, mix_ref, scale_ref, gain_ref, mixed_ref, mix_grad_ref, sum_ref, cross_ref):
    @pl.when(pl.program_id(0) == 0)
    def _():
        sum_ref[...] = jnp.zeros_like(sum_ref)

    mix = mix_ref[...]
    sig = jax.nn.sigmoid(mix)
    act = mix * sig
    gain = gain_ref[...]
    grad = grad_ref[...]
    state = state_ref[...]
    level = state * scale_ref[...]
    mixed_ref[...] = (level * gain * act).astype(mixed_ref.dtype)
    mix_grad_ref[...] = (grad * level * gain * (sig * (1.0 + mix * (1.0 - sig)))).astype(mix_grad_ref.dtype)
    sum_ref[...] += jnp.sum(grad * level * act, axis=0, keepdims=True)
    cross_ref[...] = jnp.sum(grad * gain * act * state, axis=1, keepdims=True)


def mixing(grad, state, mix_pre, scale, gain):
    tokens, width = grad.shape
    length = tokens // STEPS
    block = pl.BlockSpec((length, width), lambda i: (i, 0))
    column = pl.BlockSpec((length, 1), lambda i: (i, 0))
    row = pl.BlockSpec((1, width), lambda i: (0, 0))
    half = jax.ShapeDtypeStruct((tokens, width), bf16)
    return pl.pallas_call(
        mixing_kernel,
        grid=(STEPS,),
        in_specs=[block, block, block, column, row],
        out_specs=[block, block, row, column],
        out_shape=(half, half, jax.ShapeDtypeStruct((1, width), f32), jax.ShapeDtypeStruct((tokens, 1), f32)),
        compiler_params=params(),
        cost_estimate=light(),
        name="mixing",
    )(grad, state, mix_pre, scale, gain)


TILES = 1
HALVES = 2


def tiled(rows, width):
    return [jax.ShapeDtypeStruct((rows, width // TILES), f32)] * TILES


def columns(refs):
    return jnp.concatenate([ref[...] for ref in refs], axis=1)


def spread(refs, value):
    wide = value.shape[1] // TILES
    for i, ref in enumerate(refs):
        ref[...] = value[:, i * wide : (i + 1) * wide].astype(ref.dtype)


def call(kernel, name, place, grid, in_specs, out_specs, out_shape, *values, scratch=(), **how):
    return pl.pallas_call(
        kernel,
        grid_spec=pltpu.PrefetchScalarGridSpec(
            num_scalar_prefetch=1, grid=grid, in_specs=in_specs, out_specs=out_specs, scratch_shapes=scratch
        ),
        out_shape=out_shape,
        compiler_params=params(),
        cost_estimate=light(),
        name=name,
        **how,
    )(place, *values)


def enter_kernel(place, input_ref, kept_ref, came_ref, scale_ref, middle_ref, level_ref, *halves):
    middle = input_ref[...].astype(f32) + (kept_ref[...] + came_ref[...]) * scale_ref[...]
    middle_ref[...] = middle
    level = middle * rms_scale(middle)
    level_ref[...] = level
    wide = level.shape[1] // HALVES
    for i, ref in enumerate(halves):
        ref[...] = level[:, i * wide : (i + 1) * wide]


def enter(place, k, inputs, kept, came, scale):
    rows, width = kept.shape
    steps = 4
    part = rows // steps
    here = pl.BlockSpec((part, width), lambda i, p: (i, 0))
    full = jax.ShapeDtypeStruct((rows, width), f32)
    among = lambda i, p: ((2 * k + p[2]) * steps + i, 0)
    specs = [pl.BlockSpec((part, width), among), here, here, pl.BlockSpec((part, 1), among)]
    half = pl.BlockSpec((part, width // HALVES), lambda i, p: (i, 0))
    shapes = [full, full] + [jax.ShapeDtypeStruct((rows, width // HALVES), f32)] * HALVES
    done = call(enter_kernel, "enter", place, (steps,), specs, [here, here] + [half] * HALVES, shapes, inputs, kept, came, scale)
    return done[0], done[1], tuple(done[2:])


def feed_kernel(place, mine_ref, norm_ref, gate_w_ref, up_w_ref, pull_ref, *rest):
    theirs_refs = rest[:HALVES]
    nf_ref, hid_ref, dg_ref, du_ref = rest[-4:]
    rows = mine_ref.shape[0]
    core = place[2]
    norm = norm_ref[...]
    nf_ref[pl.ds(pl.multiple_of(core * rows, rows), rows), :] = (mine_ref[...] * norm).astype(bf16)
    nf_ref[pl.ds(pl.multiple_of((1 - core) * rows, rows), rows), :] = (columns(theirs_refs) * norm).astype(bf16)
    nf = nf_ref[...]
    gate = multiply(nf, gate_w_ref[...])
    upward = multiply(nf, up_w_ref[...])
    sig = jax.nn.sigmoid(gate)
    act = gate * sig
    pull = pull_ref[...]
    hid_ref[...] = (act * upward).astype(bf16)
    dg_ref[...] = (pull * upward * (sig * (1.0 + gate * (1.0 - sig)))).astype(bf16)
    du_ref[...] = (pull * act).astype(bf16)


def feed_forward(place, k, mine, theirs, norm, w_gate, w_up, pull, before):
    rows, width = mine.shape
    units = w_gate.shape[1]
    tokens = pull.shape[0]
    shapes = [(tokens, width)] + [(tokens, units)] * 3
    outs = [pl.BlockSpec((2 * rows, n), lambda i, p: (k, 0)) for _, n in shapes]

    def once(shape, at=lambda i, p: (0, 0)):
        return pl.BlockSpec(shape, at, pipeline_mode=pl.Buffered(1))

    specs = [once(v.shape) for v in (mine, norm, w_gate, w_up)] + [once((2 * rows, units), lambda i, p: (k, 0))]
    specs += [once(v.shape) for v in theirs] + [ANY] * len(before)
    return call(
        feed_kernel,
        "feed_forward",
        place,
        (1,),
        specs,
        outs,
        tuple(jax.ShapeDtypeStruct(shape, bf16) for shape in shapes),
        mine,
        norm,
        w_gate,
        w_up,
        pull,
        *theirs,
        *before,
        input_output_aliases={6 + HALVES + i: i for i in range(len(before))},
    )


def product_kernel(pairs, flipped, place, *refs):
    mine_ref, theirs_ref, held = refs[2 * pairs :]
    core = place[2]
    rows = mine_ref.shape[0] // 2
    times = outer_cols if flipped else multiply
    value = times(refs[0][...], refs[1][...])
    for i in range(1, pairs):
        value = value + times(refs[2 * i][...], refs[2 * i + 1][...])
    held[...] = value
    for k in range(2):
        for ref, at in ((mine_ref, core), (theirs_ref, 1 - core)):
            ref[k * rows : (k + 1) * rows, :] = held[pl.ds(pl.multiple_of((2 * k + at) * rows, rows), rows), :]


def product(place, pairs, flipped):
    first = pairs[0][0]
    tokens = (first[0] if isinstance(first, tuple) else first).shape[0]
    width = pairs[0][1].shape[0 if flipped else 1]
    steps = 4
    tile = width // steps
    specs, values = ([], [])
    for left, right in pairs:
        left, block = left if isinstance(left, tuple) else (left, 0)
        deep = right.shape[1 if flipped else 0]
        specs.append(pl.BlockSpec((tokens, deep), lambda i, p, block=block: (0, block)))
        specs.append(pl.BlockSpec((tile, deep), lambda i, p: (i, 0)) if flipped else pl.BlockSpec((deep, tile), lambda i, p: (0, i)))
        values += [left, right]
    out = pl.BlockSpec((tokens // 2, tile), lambda i, p: (0, i))
    shape = jax.ShapeDtypeStruct((tokens // 2, width), f32)
    kernel = functools.partial(product_kernel, len(pairs), flipped)
    held = [pltpu.VMEM((tokens, tile), f32)]
    mine, theirs = call(kernel, "product", place, (steps,), specs, [out, out], [shape, shape], *values, scratch=held)
    return mine, (theirs,)


def merge_kernel(place, full_ref, *refs):
    refs[-1][...] = full_ref[...] + columns(refs[:-1])


def merge(place, full, pieces):
    rows, width = full.shape
    steps = 4
    here = pl.BlockSpec((rows // steps, width), lambda i, p: (i, 0))
    piece = pl.BlockSpec((rows // steps, width // TILES), lambda i, p: (i, 0))
    return call(
        merge_kernel, "merge", place, (steps,), [here] + [piece] * TILES, here, jax.ShapeDtypeStruct(full.shape, f32), full, *pieces
    )


def leave_kernel(place, value_ref, base_ref, kept_ref, came_ref, gain_ref, grad_ref, total_ref, *change_refs, whole):
    @pl.when(pl.program_id(0) == 0)
    def _():
        grad_ref[...] = jnp.zeros_like(grad_ref)

    value = value_ref[...].astype(f32)
    scale = rms_scale(value)
    level = value * scale
    grad = kept_ref[...] + came_ref[...]
    weighed = grad * gain_ref[...]
    change = scale * (weighed - level * jnp.mean(weighed * level, axis=-1, keepdims=True))
    total = base_ref[...].astype(f32) + change
    grad_ref[...] += jnp.sum(grad * level, axis=0, keepdims=True)
    total_ref[...] = total
    spread(change_refs, total if whole else change)


def leave(place, k, value, base, kept, came, gain, whole):
    rows, width = (kept.shape[0] // 2, kept.shape[1])
    steps = 4
    part = rows // steps
    here = pl.BlockSpec((part, width), lambda i, p: (i, 0))
    mine = pl.BlockSpec((part, width), lambda i, p: (k * steps + i, 0))
    among = pl.BlockSpec((part, width), lambda i, p: ((2 * k + p[2]) * steps + i, 0))
    piece = pl.BlockSpec((part, width // TILES), lambda i, p: (i, 0))
    row = pl.BlockSpec((1, width), lambda i, p: (0, 0))
    done = call(
        functools.partial(leave_kernel, whole=whole),
        "leave",
        place,
        (steps,),
        [here if v.shape[0] == rows else among for v in (value, base)] + [mine, mine, row],
        [row, here] + [piece] * TILES,
        [jax.ShapeDtypeStruct((1, width), f32), jax.ShapeDtypeStruct((rows, width), f32)] + tiled(rows, width),
        value,
        base,
        kept,
        came,
        gain,
    )
    return done[0], done[1], tuple(done[2:])


def result_kernel(place, first_ref, second_ref, kept_ref, came_ref, total_ref, *pieces):
    k = pl.program_id(0) // (pl.num_programs(0) // 2)
    total = jnp.where(k == 0, first_ref[...], second_ref[...]) + kept_ref[...] + came_ref[...]
    total_ref[...] = total
    spread(pieces, total)


def result(place, first, second, kept, came):
    rows, width = kept.shape
    steps = 8
    part = rows // steps
    here = pl.BlockSpec((part, width), lambda i, p: (i, 0))
    folded = pl.BlockSpec((part, width), lambda i, p: (lax.rem(i, steps // 2), 0))
    piece = pl.BlockSpec((part, width // TILES), lambda i, p: (i, 0))
    full = jax.ShapeDtypeStruct((rows, width), f32)
    done = call(
        result_kernel,
        "result",
        place,
        (steps,),
        [folded, folded, here, here],
        [here] + [piece] * TILES,
        [full] + tiled(rows, width),
        first,
        second,
        kept,
        came,
    )
    return done[0], tuple(done[1:])


def assemble_kernel(own, based, scaled, place, *refs):
    whole = refs[-1]
    core = place[2]
    groups, at = ([], 0)
    for count in (own, own, TILES, TILES):
        groups.append(refs[at : at + count])
        at += count
    for i, group in enumerate(groups):
        k, where = (i % 2, core if i < 2 else 1 - core)
        value = columns(group)
        if based:
            value = value + refs[at][k, where].astype(f32)
        if scaled:
            value = value * refs[at][...]
        whole[k, where] = value.astype(whole.dtype)


def assemble(place, mine, theirs, kind, base=None, gain=None):
    mine = [v if isinstance(v, (tuple, list)) else (v,) for v in mine]
    rows = mine[0][0].shape[0]
    width = sum(v.shape[1] for v in mine[0])
    steps = 8
    part = rows // steps
    values = [v for group in (*mine, *theirs) for v in group]
    specs = [pl.BlockSpec((part, v.shape[1]), lambda i, p: (i, 0)) for v in values]
    whole = pl.BlockSpec((2, 2, part, width), lambda i, p: (0, 0, i, 0))
    if base is not None:
        specs.append(whole)
        values.append(base.reshape(2, 2, rows, width))
    if gain is not None:
        specs.append(pl.BlockSpec((1, width), lambda i, p: (0, 0)))
        values.append(gain)
    kernel = functools.partial(assemble_kernel, len(mine[0]), base is not None, gain is not None)
    shape = jax.ShapeDtypeStruct((2, 2, rows, width), kind)
    return call(kernel, "assemble", place, (steps,), specs, whole, shape, *values).reshape(4 * rows, width)


def swap_kernel(place, gate_ref, up_ref, out_ref):
    out_ref[...] = jnp.where(place[1] == 0, up_ref[...].astype(f32), gate_ref[...].astype(f32))


def swap(place, k, d_gate, d_upward):
    tokens, units = d_gate.shape
    steps = 4
    here = pl.BlockSpec((tokens // 2 // steps, units), lambda i, p: (k * steps + i, 0))
    out = pl.BlockSpec((tokens // 2 // steps, units), lambda i, p: (i, 0))
    shape = jax.ShapeDtypeStruct((tokens // 2, units), f32)
    return call(swap_kernel, "swap", place, (steps,), [here, here], out, shape, d_gate, d_upward)


def rise_kernel(place, up_ref, down_ref, came_up_ref, came_down_ref, up_out_ref, down_out_ref):
    up_out_ref[...] = up_ref[...] + came_up_ref[...]
    down_out_ref[...] = down_ref[...] + came_down_ref[...]


def rise(place, *values):
    rows, wide = values[0].shape
    steps = 4
    here = pl.BlockSpec((rows // steps, wide), lambda i, p: (i, 0))
    shape = jax.ShapeDtypeStruct((rows, wide), f32)
    return call(rise_kernel, "rise", place, (steps,), [here] * 4, [here, here], [shape, shape], *values)


def settle_kernel(place, block_ref, up_ref, down_ref, out_ref):
    out_ref[...] = block_ref[...] + up_ref[...] + down_ref[...]


def settle(place, *values):
    rows, wide = values[0].shape
    steps = 4
    here = pl.BlockSpec((rows // steps, wide), lambda i, p: (i, 0))
    return call(settle_kernel, "settle", place, (steps,), [here] * 3, here, jax.ShapeDtypeStruct((rows, wide), f32), *values)


def back_kernel(place, left_ref, right_ref, out_ref):
    out_ref[...] = outer_cols(left_ref[...], right_ref[...])


def back(place, left, right):
    tokens, width = left.shape
    deep = right.shape[0]
    steps = 4
    here = pl.BlockSpec((tokens // steps, width), lambda i, p: (i, 0))
    out = pl.BlockSpec((tokens // steps, deep), lambda i, p: (i, 0))
    specs = [here, pl.BlockSpec(right.shape, lambda i, p: (0, 0))]
    return call(back_kernel, "back", place, (steps,), specs, out, jax.ShapeDtypeStruct((tokens, deep), f32), left, right)


def place_block(outs, value, at=0):
    wide = value.shape[1]
    if len(outs) == 1:
        outs[0][0, :, at : at + wide] = value
        return
    for j, ref in enumerate(outs):

        @pl.when(pl.program_id(0) == j)
        def _():
            ref[:, at : at + wide] = value


def weigh_kernel(pairs, halves, place, *refs):
    outs = refs[2 * pairs + (2 if halves else 0) :]
    at = 0
    for i in range(pairs):
        value = inner_rows(refs[2 * i][...], refs[2 * i + 1][...])
        wide = value.shape[1]
        if halves:
            first, second = refs[2 * pairs : 2 * pairs + 2]
            early = pl.program_id(0) < pl.num_programs(0) // 2
            value = value + jnp.where(early, first[0, :, at : at + wide], second[0, :, at : at + wide])
        place_block(outs, value, at)
        at += wide


def weigh_both_kernel(place, left_ref, gate_ref, up_ref, far_left_ref, first_ref, second_ref, *outs):
    half = first_ref.shape[0]
    right = jnp.where(place[1] == 0, gate_ref[...], up_ref[...])
    value = inner_rows(left_ref[...], right)
    value = value + inner_rows(far_left_ref[:half, :], first_ref[...].astype(bf16))
    place_block(outs, value + inner_rows(far_left_ref[half:, :], second_ref[...].astype(bf16)))


def weigh_call(kernel, place, side, lefts, rights, order, wide, halves=(), count=None, first=0):
    count = DEEP if count is None else count
    rows = lefts[0].shape[1] // (2 * DEEP)

    def chosen(j, p):
        return (0, 2 * lax.rem(p[0] + first + j, DEEP) + (p[1] if side == 0 else 1 - p[1]))

    specs = {id(v): pl.BlockSpec((v.shape[0], rows), chosen) for v in lefts}
    specs |= {id(v): pl.BlockSpec(v.shape, lambda j, p: (0, 0)) for v in rights}
    half = pl.BlockSpec((1, rows, wide), lambda j, p: (lax.rem(j, DEEP // 2), 0, 0))
    if count == DEEP:
        block = [pl.BlockSpec((rows, wide), lambda j, p: (0, 0))] * DEEP
        shape = [jax.ShapeDtypeStruct((rows, wide), f32)] * DEEP
    else:
        block = pl.BlockSpec((1, rows, wide), lambda j, p: (j, 0, 0))
        shape = jax.ShapeDtypeStruct((count, rows, wide), f32)
    return call(
        kernel, "weigh", place, (count,), [specs[id(v)] for v in order] + [half] * len(halves), block, shape, *order, *halves
    )


def weigh(place, pairs, side, halves=(), count=None, first=0):
    order = [v for pair in pairs for v in pair]
    wide = sum(right.shape[1] for _, right in pairs)
    kernel = functools.partial(weigh_kernel, len(pairs), len(halves) == 2)
    return weigh_call(kernel, place, side, order[::2], order[1::2], order, wide, halves, count, first)


def weigh_both(place, side, left, gate, up, far_left, first, second):
    order = [left, gate, up, far_left, first, second]
    return weigh_call(weigh_both_kernel, place, side, [left, far_left], [gate, up, first, second], order, gate.shape[1])


SEQ, MP, DEEP = 8, 4, 4
CORE = [(i, i ^ 1) for i in range(MP)]
ACROSS = [(i, i ^ 2) for i in range(MP)]
BESIDE = [(i, i ^ 1) for i in range(SEQ)]
UP = [[(2 * z + y, 2 * z + 2 + y) for z in range(t) for y in range(2)] for t in range(DEEP)]
DOWN = [[(2 * z + y, 2 * z - 2 + y) for z in range(DEEP - t, DEEP) for y in range(2)] for t in range(DEEP)]


def over_core(v):
    return jax.tree.map(lambda part: lax.ppermute(part, "mp", CORE), v)


def over_x(v):
    return lax.ppermute(v, "mp", ACROSS)


def over_y(v):
    return lax.ppermute(v, "seq", BESIDE)


def along(bit):
    return lambda v: lax.ppermute(v, "seq", [(i, i ^ bit) for i in range(SEQ)])


def along_line(t):
    return lambda v: (lax.ppermute(v[0], "seq", UP[t]), lax.ppermute(v[1], "seq", DOWN[t]))


def reaching(reverse):
    def send(whole):
        rounds = [whole]
        for k in range(1, DEEP):
            pairs = [(2 * z + i, 2 * (z + k) + i) for z in range(DEEP - k) for i in range(2)]
            rounds.append(lax.ppermute(whole, "seq", [(b, a) for a, b in pairs] if reverse else pairs))
        return tuple(rounds)

    return send


class Names:
    def __getattr__(self, name):
        return name


N = Names()


def of(name, k):
    return name + str(k)


def sent(name):
    return name + "_"


def wait(name):
    return name + "!"


def flat(reads):
    return [reads] if isinstance(reads, str) else [name for part in reads for name in flat(part)]


class Steps:
    def __init__(self, place, known):
        self.place = place
        self.known = known
        self.steps = {}
        self.arrivals = set()
        self.last = None

    def add(self, name, reads, work, *sends):
        self.steps[name] = (flat(reads), work, sends)

    def settle(self, *names):
        if self.last is None:
            return
        last, sends = self.last
        self.last = None
        names = [v for v in dict.fromkeys(names) if v != last]
        held = {v: self.known[v] for v in [*names, last]}
        self.known.update(together(held))
        done = self.known[last]
        for arrival, how, *part in sends:
            self.known[arrival] = how(done[part[0]] if part else done)
            self.arrivals.add(arrival)

    def run(self, name):
        if name.endswith("!"):
            self.settle()
            name = name[:-1]
            self.arrivals.discard(name)
            self.last = (name, ())
            return
        reads, work, sends = self.steps.pop(name)
        self.settle(*[v for v in reads if v in self.known and v not in self.arrivals])
        self.known[name] = work(*[self.known[v] for v in reads])
        self.last = (name, sends)

    def line(self, name, source):
        reads, work, _ = self.steps[source]
        self.steps[source] = (reads, work, ((sent(of(name, 1)), lambda v: along_line(1)((v[DEEP - 1], v[1]))),))
        for t in range(2, DEEP):
            self.add(
                of(name, t),
                (source, sent(of(name, t - 1))),
                lambda v, came, t=t: rise(self.place, v[DEEP - t], v[t], *came),
                (sent(of(name, t)), along_line(t)),
            )


ORDER = (
    N.in_pre,
    N.forget,
    N.scan,
    N.mix,
    N.stack,
    N.join,
    N.square,
    wait(N.square_),
    N.send0,
    N.square2,
    N.send1,
    wait(N.square2_),
    N.keep0,
    N.keep1,
    N.scale,
    N.pull,
    N.enter0,
    N.feed0,
    N.gates0,
    N.enter1,
    N.feed1,
    wait(N.beside0),
    N.unfeed,
    N.down_far,
    N.unfed,
    N.down_own,
    N.p2,
    N.gates1,
    N.spread,
    wait(N.gates0_),
    N.q2,
    N.beside0_,
    N.leave0,
    N.leave1,
    N.p3,
    N.beside1_,
    N.branch,
    wait(N.spread_),
    N.mixed,
    N.far_nf,
    N.mixing,
    N.cross,
    N.cross2,
    N.mix_send0,
    N.spread_sum,
    wait(N.p3_),
    N.tug,
    N.scan_b,
    N.pair_own,
    N.q3,
    N.stack_b,
    N.pair_far,
    N.join_b,
    wait(N.mix_send0_),
    N.both_send1,
    wait(N.q3_),
    N.p_sum,
    N.origin,
    N.r2,
    N.mix_send1,
    wait(N.both_send1_),
    N.result,
    N.s2,
    wait(N.r2_),
    N.both_send0,
    N.source,
    N.mix_keep,
    N.s3,
    N.t2,
    N.out,
    N.both_keep,
    N.r3,
    N.t3,
    N.u2,
    N.enter_b0,
    N.r_sum,
    N.enter_b1,
    N.norms,
    N.small,
    N.u3,
    N.q_sum,
    wait(N.u3_),
    N.small2,
    N.t_sum,
    wait(N.p_sum_),
    wait(N.small2_),
    N.u_sum,
    N.small3,
    N.d_inputs,
    N.s_sum,
    N.smalls,
)


def planned(
    inputs, seq_start, norm_in, w_input, w_forget, w_mix_gate, lower_bound, mix_gain, w_output, norm_ffn, w_gate, w_up, w_down, cotangent
):
    tokens, width = inputs.shape
    quarter = tokens // 4
    units = w_input.shape[1]
    seq = lax.axis_index("seq")
    core = lax.axis_index("mp") % 2
    y = seq % 2
    place = jnp.stack([seq // 2, y, core])
    bound = lower_bound[None, :]
    gain = mix_gain[None, :]
    places = seq * tokens + jnp.arange(tokens, dtype=jnp.int32)
    cut = (seq_start == places).astype(f32)[:, None]
    known = dict(
        inputs=inputs,
        w_output=w_output,
        w_gate=w_gate,
        w_up=w_up,
        w_down=w_down,
        cot=cotangent,
        norm=norm_ffn[None, :],
        norm_in=norm_in[None, :],
        wi=w_input,
        wf=w_forget,
        wm=w_mix_gate,
    )
    plan = Steps(place, known)
    step = plan.add

    def quarters(v, at):
        parts = v.reshape((2, 2, quarter) + v.shape[1:])
        return lax.dynamic_index_in_dim(parts, at, 1, keepdims=False)

    def add(a, b):
        return a + b

    in_float = inputs.astype(f32)
    known[N.normed] = (in_float * rms_scale(in_float) * norm_in).astype(bf16)
    step(N.in_pre, (N.normed, N.wi), multiply)
    step(N.forget, (N.normed, N.wf), multiply)
    step(N.scan, (N.in_pre, N.forget), lambda a, b: scan_forward(a, b, cut, bound), (N.scan_, reaching(False), 2))
    step(N.mix, (N.normed, N.wm), multiply)
    step(N.stack, N.scan_, lambda v: jnp.stack(v), (N.stack_, over_y))
    step(N.join, (N.scan, N.mix, N.stack, N.stack_), lambda a, b, *v: join_forward(place, a[0], a[1], b, *v, gain))

    step(N.square, N.join, lambda v: v[3][:, 0], (N.square_, over_core))
    step(N.square2, (N.square, N.square_), add, (N.square2_, over_x))
    step(N.scale, (N.square2, N.square2_), lambda a, b: lax.rsqrt((a + b) / width + epsilon)[:, None])
    for k in range(2):
        step(of(N.send, k), (N.join, N.w_output), lambda v, w, k=k: multiply(quarters(v[2], 1 - core)[k], w), (sent(of(N.send, k)), over_core))
        step(
            of(N.keep, k), (N.join, N.w_output, sent(of(N.send, k))), lambda v, w, s, k=k: multiply(quarters(v[2], core)[k], w) + s, (sent(of(N.keep, k)), over_x)
        )
    step(N.pull, (N.cot, N.w_down), lambda a, b: back(place, a, b))

    for k in range(2):
        step(
            of(N.enter, k),
            (N.inputs, of(N.keep, k), sent(of(N.keep, k)), N.scale),
            functools.partial(enter, place, k),
            (sent(of(N.level, k)), over_core, 2),
            (of(N.beside, k), over_y, 1),
        )
        step(
            of(N.feed, k),
            ((of(N.enter, k), sent(of(N.level, k)), N.norm, N.w_gate), (N.w_up, N.pull), (N.feed0, N.gates0) if k else ()),
            lambda e, t, n, g, u, p, *before, k=k: feed_forward(place, k, e[1], t, n, g, u, p, before[0] if before else ()),
        )
        step(of(N.gates, k), of(N.feed, k), lambda v, k=k: swap(place, k, v[2], v[3]), (sent(of(N.gates, k)), over_y))

    step(N.down_far, (N.cot, N.feed1), lambda a, b: weigh(place, [(a, b[1])], 1))
    step(N.down_own, (N.cot, N.feed1), lambda a, b: weigh(place, [(a, b[1])], 0))
    plan.line(N.p, N.down_far)
    plan.line(N.q, N.down_own)
    step(N.p_sum, (N.down_far, N.p3_), lambda b, c: settle(place, b[0], *c), (N.p_sum_, over_y))
    step(N.q_sum, (N.down_own, N.q3_, N.p_sum_), lambda b, c, d: (b[0] + c[0] + c[1] + d).T)
    for k in range(2):
        step(sent(of(N.beside, k)), of(N.beside, k), lambda v: (v,), (sent(sent(of(N.beside, k))), over_core))
    step(
        N.far_nf,
        ((N.beside0_, N.beside1_, N.beside0__, N.beside1__), N.norm),
        lambda a, b, c, d, e: assemble(place, (a, b), (c, d), bf16, gain=e),
    )
    both_args = (N.feed1, N.far_nf, N.gates0_, N.gates1_)
    step(N.pair_far, both_args, lambda f, *v: weigh_both(place, 1, f[0], f[2], f[3], *v))
    step(N.pair_own, both_args, lambda f, *v: weigh_both(place, 0, f[0], f[2], f[3], *v))
    plan.line(N.r, N.pair_far)
    plan.line(N.s, N.pair_own)
    step(N.r_sum, (N.pair_far, N.r3_), lambda b, c: settle(place, b[0], *c), (N.r_sum_, over_y))

    def sort_pair(b, c, theirs):
        mine = b[0] + c[0] + c[1]
        return jnp.where(y == 0, mine, theirs), jnp.where(y == 0, theirs, mine)

    step(N.s_sum, (N.pair_own, N.s3_, N.r_sum_), sort_pair)

    step(
        N.unfeed, (N.feed1, N.w_gate, N.w_up), lambda f, g, u: product(place, [(f[2], g), (f[3], u)], True), (N.unfeed_, over_core, 1)
    )
    step(N.unfed, (N.unfeed, N.unfeed_), lambda a, b: merge(place, a[0], b), (N.unfed_, over_x))
    step(N.spread, (N.feed1, N.w_down), lambda f, w: product(place, [(f[1], w)], False), (N.spread_, over_core, 1))
    step(N.spread_sum, (N.spread, N.spread_, N.cross2_), lambda a, b, c: merge(place, a[0], b), (N.spread_sum_, over_x))
    step(
        N.result,
        (N.enter0, N.enter1, N.spread_sum, N.spread_sum_),
        lambda a, b, c, d: result(place, a[0], b[0], c, d),
        (N.result_, over_core, 1),
    )

    def halves(v):
        return (v[:quarter], v[quarter:])

    step(
        N.out,
        (N.result, N.result_),
        lambda a, b: assemble(place, halves(a[0]), list(zip(*[halves(v) for v in b], strict=True)), bf16),
    )

    for k in range(2):
        step(
            of(N.leave, k),
            ((of(N.enter, k), N.cot, N.unfed, N.unfed_), N.norm),
            lambda e, *v, k=k: leave(place, k, e[0], *v, False),
            (sent(of(N.leave, k)), over_core, 2),
        )
    step(
        N.branch,
        ((N.leave0, N.leave1, N.leave0_, N.leave1_), N.cot),
        lambda a, b, c, d, e: assemble(place, (a[2], b[2]), (c, d), bf16, base=e),
    )
    step(N.mixed, (N.branch, N.w_output), lambda a, b: back(place, a, b))
    step(N.mixing, (N.mixed, N.join, N.mix, N.scale), lambda d, j, m, s: mixing(d, j[0], m, s, gain))
    step(N.cross, N.mixing, lambda v: v[3][:, 0], (N.cross_, over_core))
    step(N.cross2, (N.cross, N.cross_), add, (N.cross2_, over_x))
    step(N.tug, (N.cross2, N.cross2_, N.scale), lambda a, b, s: s**3 * ((a + b)[:, None] / width))
    step(
        N.scan_b,
        ((N.mixed, N.join, N.mix, N.forget), (N.scale, N.tug)),
        lambda d, j, m, f, s, t: scan_backward(d, j[0], m, f, cut, s, t, bound, gain),
        (N.scan_b_, reaching(True), 2),
    )
    step(N.stack_b, N.scan_b_, lambda v: jnp.stack(v), (N.stack_b_, over_y))
    step(
        N.join_b,
        ((N.scan_b, N.in_pre, N.forget, N.join), (N.stack_b, N.stack_b_)),
        lambda s, i, f, j, *v: join_backward(place, s[0], s[1], i, f, j[1], cut, *v, bound),
    )

    def mix_pairs(n, m, b):
        return [(n, m[1]), (b, m[0])]

    for k in range(2):
        step(
            of(N.mix_send, k),
            (N.normed, N.mixing, N.branch),
            lambda *v, k=k: weigh(place, mix_pairs(*v), 1, (), DEEP // 2, k * DEEP // 2),
            (sent(of(N.mix_send, k)), over_y),
        )
        step(
            of(N.both_send, k),
            (N.normed, N.join_b),
            lambda n, b, k=k: weigh(place, [(n, b[1])], 1, (), DEEP // 2, k * DEEP // 2),
            (sent(of(N.both_send, k)), over_y),
        )
    step(N.mix_keep, ((N.normed, N.mixing, N.branch, N.mix_send0_), N.mix_send1_), lambda *v: weigh(place, mix_pairs(*v[:3]), 0, v[3:]))
    step(N.both_keep, (N.normed, N.join_b, N.both_send0_, N.both_send1_), lambda n, b, *v: weigh(place, [(n, b[1])], 0, v))
    plan.line(N.t, N.mix_keep)
    plan.line(N.u, N.both_keep)

    def sort_mix(b, c):
        total = b[0] + c[0] + c[1]
        return total[:, :units], total[:, units:].T

    def sort_both(b, c):
        total = b[0] + c[0] + c[1]
        return total[:, :units], total[:, units:]

    step(N.t_sum, (N.mix_keep, N.t3_), sort_mix)
    step(N.u_sum, (N.both_keep, N.u3_), sort_both)

    step(
        N.origin,
        ((N.join_b, N.mixing, N.wi, N.wf), N.wm),
        lambda b, m, i, f, w: product(place, [((b[1], 0), i), ((b[1], 1), f), (m[1], w)], True),
        (N.origin_, over_core, 1),
    )
    step(N.source, (N.origin, N.origin_), lambda a, b: merge(place, a[0], b), (N.source_, over_x))
    for k in range(2):
        step(
            of(N.enter_b, k),
            ((N.inputs, of(N.leave, k), N.source, N.source_), N.norm_in),
            lambda i, m, *v, k=k: leave(place, k, i, m[1], *v, True),
            (sent(of(N.enter_b, k)), over_core, 2),
        )
    step(
        N.d_inputs,
        (N.enter_b0, N.enter_b1, N.enter_b0_, N.enter_b1_),
        lambda a, b, c, d: assemble(place, (a[1], b[1]), (c, d), f32),
    )
    step(
        N.norms,
        (N.enter_b0, N.enter_b1, N.leave0, N.leave1),
        lambda a, b, c, d: jnp.concatenate([a[0] + b[0], c[0] + d[0]], axis=1)[0],
        (N.norms_, over_core),
    )
    step(
        N.small,
        ((N.norms, N.norms_, N.join_b, N.mixing), N.scan),
        lambda a, b, c, d, e: jnp.concatenate([a + b, c[0][0], d[2][0], e[3][0]]),
        (N.small_, along(1)),
    )
    step(N.small2, (N.small, N.small_), add, (N.small2_, along(2)))
    step(N.small3, (N.small2, N.small2_), add, (N.small3_, along(4)))
    step(N.smalls, (N.small3, N.small3_), add)

    for name in ORDER:
        plan.run(name)
    plan.settle()
    smalls = known[N.smalls]
    piece = width // SEQ
    d_norm_in = lax.dynamic_slice_in_dim(smalls, seq * piece, piece)
    d_norm_ffn = lax.dynamic_slice_in_dim(smalls, width + seq * piece, piece)
    d_lower, d_mix_gain, forget_sum = (smalls[2 * width + i * units : 2 * width + (i + 1) * units] for i in range(3))
    mix_grad, out_grad = known[N.t_sum]
    in_grad, forget_grad = known[N.u_sum]
    gate_grad, up_grad = known[N.s_sum]
    return (
        known[N.out],
        known[N.d_inputs],
        d_norm_in,
        in_grad,
        forget_grad,
        mix_grad,
        d_lower,
        d_mix_gain,
        out_grad,
        d_norm_ffn,
        gate_grad,
        up_grad,
        known[N.q_sum],
        forget_sum / (tokens * SEQ),
    )


def entering(x, axis, combine, identity, reverse):
    length, index = (lax.axis_size(axis), lax.axis_index(axis))
    everything = jax.tree.map(lambda part: lax.all_gather(part, axis), x)
    start = jax.tree.map(
        lambda part, zero: jnp.broadcast_to(jnp.asarray(zero, part.dtype), part.shape), x, identity
    )

    def turn(k, before):
        at = length - 1 - k if reverse else k
        reached = at > index if reverse else at < index
        new = combine(before, jax.tree.map(lambda part: part[at], everything))
        return jax.tree.map(lambda a, b: jnp.where(reached, a, b), new, before)

    return lax.fori_loop(0, length, turn, start)


def compose(earlier, later):
    return (earlier[0] * later[0], later[0] * earlier[1] + later[1])


def carry_forward(whole, ending):
    result = entering(
        (whole, ending), "seq", compose, (jnp.ones_like(whole), jnp.zeros_like(ending)), False
    )
    return result[1]


def carry_backward(whole, leading):
    result = entering(
        (whole, leading), "seq", compose, (jnp.ones_like(whole), jnp.zeros_like(leading)), True
    )
    return result[1]


def general(
    inputs,
    seq_start,
    norm_in,
    w_input,
    w_forget,
    w_mix_gate,
    lower_bound,
    mix_gain,
    w_output,
    norm_ffn,
    w_gate,
    w_up,
    w_down,
    cotangent,
):
    tokens_here = inputs.shape[0]
    width = inputs.shape[1]
    places = lax.axis_index("seq") * tokens_here + jnp.arange(tokens_here, dtype=jnp.int32)
    restart = (seq_start == places).astype(jnp.float32)[:, None]
    in_float = inputs.astype(jnp.float32)
    scale_in = rms_scale(in_float)
    normed = (in_float * scale_in * norm_in).astype(jnp.bfloat16)
    in_pre = multiply(normed, w_input)
    forget_pre = multiply(normed, w_forget)
    mix_pre = multiply(normed, w_mix_gate)
    fade = jax.nn.sigmoid(-forget_pre)
    forget_local = jnp.sum(1.0 - fade, axis=0)
    keep = (1.0 - lower_bound) * fade
    decay = (1.0 - keep) * (1.0 - restart)
    act_in = jax.nn.silu(in_pre)
    drive = act_in * keep
    decay_run, state_local = lax.associative_scan(compose, (decay, drive), axis=0)
    state_in = carry_forward(decay_run[-1], state_local[-1])
    state = state_local + decay_run * state_in
    squares = lax.psum(jnp.sum(state * state, axis=1), "mp")
    mix_scale = lax.rsqrt(squares / width + epsilon)[:, None]
    gate_act = jax.nn.silu(mix_pre)
    normed_state = state * mix_scale
    mixed = (normed_state * mix_gain * gate_act).astype(jnp.bfloat16)
    branch = lax.psum(multiply(mixed, w_output), "mp")
    middle = in_float + branch
    scale_ffn = rms_scale(middle)
    normed_ffn = (middle * scale_ffn * norm_ffn).astype(jnp.bfloat16)
    gate = multiply(normed_ffn, w_gate)
    upward = multiply(normed_ffn, w_up)
    silu_gate = jax.nn.silu(gate)
    hidden = (silu_gate * upward).astype(jnp.bfloat16)
    feed = lax.psum(multiply(hidden, w_down), "mp")
    out = (middle + feed).astype(jnp.bfloat16)
    grad_float = cotangent.astype(jnp.float32)
    d_hidden = outer_cols(cotangent, w_down)
    d_w_down = inner_rows(hidden, cotangent)
    d_gate = (d_hidden * upward * silu_slope(gate)).astype(jnp.bfloat16)
    d_upward = (d_hidden * silu_gate).astype(jnp.bfloat16)
    d_normed_ffn = lax.psum(outer_cols(d_gate, w_gate) + outer_cols(d_upward, w_up), "mp")
    d_w_gate = inner_rows(normed_ffn, d_gate)
    d_w_up = inner_rows(normed_ffn, d_upward)
    d_norm_ffn = jnp.sum(d_normed_ffn * middle * scale_ffn, axis=0)
    scaled_ffn = d_normed_ffn * norm_ffn
    d_middle = (
        grad_float
        + scale_ffn * scaled_ffn
        - middle * scale_ffn**3 * jnp.mean(scaled_ffn * middle, axis=-1, keepdims=True)
    )
    d_branch = d_middle.astype(jnp.bfloat16)
    d_w_output = inner_rows(mixed, d_branch)
    d_mixed = outer_cols(d_branch, w_output)
    d_mix_gain = jnp.sum(d_mixed * normed_state * gate_act, axis=0)
    d_mix_pre = (d_mixed * normed_state * mix_gain * silu_slope(mix_pre)).astype(jnp.bfloat16)
    scaled_mix = d_mixed * mix_gain * gate_act
    cross = lax.psum(jnp.sum(scaled_mix * state, axis=1), "mp")
    d_state = mix_scale * scaled_mix - state * mix_scale**3 * (cross / width)[:, None]
    next_decay = jnp.concatenate([decay[1:], jnp.ones_like(decay[:1])], axis=0)
    tail_decay, tail_grad = lax.associative_scan(
        compose, (next_decay, d_state), reverse=True, axis=0
    )
    carried = carry_backward(decay_run[-1], decay[0] * tail_grad[0])
    total = tail_grad + tail_decay * carried
    prev_state = jnp.concatenate([state_in[None], state[:-1]], axis=0)
    d_keep = total * act_in - total * prev_state * (1.0 - restart)
    d_lower = -jnp.sum(d_keep * fade, axis=0)
    d_in_pre = (total * keep * silu_slope(in_pre)).astype(jnp.bfloat16)
    d_forget_pre = (-d_keep * (1.0 - lower_bound) * fade * (1.0 - fade)).astype(jnp.bfloat16)
    d_normed = lax.psum(
        outer_cols(d_in_pre, w_input)
        + outer_cols(d_forget_pre, w_forget)
        + outer_cols(d_mix_pre, w_mix_gate),
        "mp",
    )
    d_w_input = inner_rows(normed, d_in_pre)
    d_w_forget = inner_rows(normed, d_forget_pre)
    d_w_mix_gate = inner_rows(normed, d_mix_pre)
    d_norm_in = jnp.sum(d_normed * in_float * scale_in, axis=0)
    scaled_in = d_normed * norm_in
    d_inputs = (
        d_middle
        + scale_in * scaled_in
        - in_float * scale_in**3 * jnp.mean(scaled_in * in_float, axis=-1, keepdims=True)
    )
    row_part = (
        lax.psum_scatter(d_w_input, "seq", scatter_dimension=0, tiled=True),
        lax.psum_scatter(d_w_forget, "seq", scatter_dimension=0, tiled=True),
        lax.psum_scatter(d_w_mix_gate, "seq", scatter_dimension=0, tiled=True),
        lax.psum_scatter(d_w_gate, "seq", scatter_dimension=0, tiled=True),
        lax.psum_scatter(d_w_up, "seq", scatter_dimension=0, tiled=True),
        lax.psum_scatter(d_norm_in, "seq", scatter_dimension=0, tiled=True),
        lax.psum_scatter(d_norm_ffn, "seq", scatter_dimension=0, tiled=True),
    )
    col_part = (
        lax.psum_scatter(d_w_output, "seq", scatter_dimension=1, tiled=True),
        lax.psum_scatter(d_w_down, "seq", scatter_dimension=1, tiled=True),
    )
    out_grad = col_part[0]
    down_grad = col_part[1]
    small_part = lax.psum((d_lower, d_mix_gain, forget_local), "seq")
    forget_mean = small_part[2] / (tokens_here * lax.axis_size("seq"))
    return (
        out,
        d_inputs,
        row_part[5],
        row_part[0],
        row_part[1],
        row_part[2],
        small_part[0],
        small_part[1],
        out_grad,
        row_part[6],
        row_part[3],
        row_part[4],
        down_grad,
        forget_mean,
    )


def solution(mesh):
    fits = mesh.shape["seq"] == SEQ and mesh.shape["mp"] == MP
    return jax.shard_map(
        planned if fits else general,
        mesh=mesh,
        in_specs=(
            P("seq", None),
            P("seq"),
            P(),
            P(None, "mp"),
            P(None, "mp"),
            P(None, "mp"),
            P("mp"),
            P("mp"),
            P("mp", None),
            P(),
            P(None, "mp"),
            P(None, "mp"),
            P("mp", None),
            P("seq", None),
        ),
        out_specs=(
            P("seq", None),
            P("seq", None),
            P("seq"),
            P("seq", "mp"),
            P("seq", "mp"),
            P("seq", "mp"),
            P("mp"),
            P("mp"),
            P("mp", "seq"),
            P("seq"),
            P("seq", "mp"),
            P("seq", "mp"),
            P("mp", "seq"),
            P("mp"),
        ),
        check_vma=False,
    )
```

```python
import functools

import jax
import jax.numpy as jnp
from jax import lax
from jax.experimental import pallas as pl
from jax.experimental.pallas import tpu as pltpu
from jax.sharding import PartitionSpec as P

epsilon = 1e-06
f32 = jnp.float32
bf16 = jnp.bfloat16
together = lax.optimization_barrier


def multiply(left, right):
    return jnp.dot(left, right, preferred_element_type=f32)


def inner_rows(left, right):
    return lax.dot_general(left, right, (((0,), (0,)), ((), ())), preferred_element_type=f32)


def outer_cols(left, right):
    return lax.dot_general(left, right, (((1,), (1,)), ((), ())), preferred_element_type=f32)


def rms_scale(values):
    return lax.rsqrt(jnp.mean(values * values, axis=-1, keepdims=True) + epsilon)


def silu_slope(values):
    sig = jax.nn.sigmoid(values)
    return sig * (1.0 + values * (1.0 - sig))


BIG = 48 * 1024 * 1024
ANY = pl.BlockSpec(memory_space=pl.ANY)


def params():
    return pltpu.CompilerParams(vmem_limit_bytes=BIG)


def light():
    return pl.CostEstimate(flops=0, bytes_accessed=1024, transcendentals=0)


ROWS = 8
STEPS = 4


def scan_forward_kernel(in_ref, forget_ref, cut_ref, bound_ref, local_ref, run_ref, whole_ref, sum_ref, carry):
    @pl.when(pl.program_id(0) == 0)
    def _():
        carry[0:1, :] = jnp.ones_like(carry[0:1, :])
        carry[1:2, :] = jnp.zeros_like(carry[1:2, :])
        sum_ref[...] = jnp.zeros_like(sum_ref)

    lift = 1.0 - bound_ref[...]
    shape = (ROWS, forget_ref.shape[1])
    row = lax.broadcasted_iota(jnp.int32, shape, 0)

    def step(i, before):
        product, state, gates = before
        at = pl.ds(pl.multiple_of(i * ROWS, ROWS), ROWS)
        fade = jax.nn.sigmoid(-forget_ref[at, :])
        keep = lift * fade
        a = (1.0 - keep) * (1.0 - cut_ref[at, :])
        pre = in_ref[at, :]
        b = pre * jax.nn.sigmoid(pre) * keep
        for s in (1, 2, 4):
            reach = row >= s
            b = b + a * jnp.where(reach, pltpu.roll(b, s, 0), 0.0)
            a = a * jnp.where(reach, pltpu.roll(a, s, 0), 1.0)
        b = b + a * state
        a = a * product
        local_ref[at, :] = b
        run_ref[at, :] = a
        return a[ROWS - 1 :, :], b[ROWS - 1 :, :], gates + (1.0 - fade)

    start = (carry[0:1, :], carry[1:2, :], jnp.zeros(shape, f32))
    product, state, gates = lax.fori_loop(0, forget_ref.shape[0] // ROWS, step, start, unroll=4)
    carry[0:1, :] = product
    carry[1:2, :] = state
    whole_ref[...] = carry[...]
    sum_ref[...] += jnp.sum(gates, axis=0, keepdims=True)


def scan_forward(in_pre, forget_pre, cut, bound):
    tokens, width = in_pre.shape
    full = jax.ShapeDtypeStruct((tokens, width), f32)
    block = pl.BlockSpec((tokens // STEPS, width), lambda i: (i, 0))
    row = pl.BlockSpec((1, width), lambda i: (0, 0))
    return pl.pallas_call(
        scan_forward_kernel,
        grid=(STEPS,),
        in_specs=[block, block, pl.BlockSpec((tokens // STEPS, 1), lambda i: (i, 0)), row],
        out_specs=[block, block, pl.BlockSpec((2, width), lambda i: (0, 0)), row],
        out_shape=(full, full, jax.ShapeDtypeStruct((2, width), f32), jax.ShapeDtypeStruct((1, width), f32)),
        scratch_shapes=[pltpu.VMEM((2, width), f32)],
        compiler_params=params(),
        cost_estimate=light(),
        name="scan_forward",
    )(in_pre, forget_pre, cut, bound)


def arriving(mine_ref, theirs_ref, later):
    def over(pair, total):
        return pair[0] * total + pair[1]

    total = jnp.zeros_like(mine_ref[0, 0:1, :])
    for k in range(mine_ref.shape[0] - 1, -1, -1):
        mine, theirs = ((ref[k, 0:1, :], ref[k, 1:2, :]) for ref in (mine_ref, theirs_ref))
        if k == 0:
            return jnp.where(later, over(theirs, total), total)
        total = jnp.where(later, over(mine, over(theirs, total)), over(theirs, over(mine, total)))


def join_forward_kernel(place, local_ref, run_ref, mix_ref, mine_ref, theirs_ref, gain_ref, state_ref, prev_ref, u_ref, square_ref, hold):
    @pl.when(pl.program_id(0) == 0)
    def _():
        hold[0:1, :] = arriving(mine_ref, theirs_ref, place[1] == 1)
        hold[1:2, :] = hold[0:1, :]

    state = local_ref[...] + run_ref[...] * hold[0:1, :]
    mix = mix_ref[...]
    rows = lax.broadcasted_iota(jnp.int32, state.shape, 0)
    state_ref[...] = state
    prev_ref[...] = jnp.where(rows == 0, hold[1:2, :], pltpu.roll(state, 1, 0))
    u_ref[...] = (state * gain_ref[...] * (mix * jax.nn.sigmoid(mix))).astype(u_ref.dtype)
    square_ref[...] = jnp.sum(state * state, axis=1, keepdims=True)
    hold[1:2, :] = state[state.shape[0] - 1 :, :]


def join_forward(place, local, run, mix_pre, mine, theirs, gain):
    tokens, width = local.shape
    length = tokens // STEPS
    block = pl.BlockSpec((length, width), lambda i, p: (i, 0))
    pairs = pl.BlockSpec(mine.shape, lambda i, p: (0, 0, 0))
    row = pl.BlockSpec((1, width), lambda i, p: (0, 0))
    full = jax.ShapeDtypeStruct((tokens, width), f32)
    return pl.pallas_call(
        join_forward_kernel,
        grid_spec=pltpu.PrefetchScalarGridSpec(
            num_scalar_prefetch=1,
            grid=(STEPS,),
            in_specs=[block, block, block, pairs, pairs, row],
            out_specs=[block, block, block, pl.BlockSpec((length, 1), lambda i, p: (i, 0))],
            scratch_shapes=[pltpu.VMEM((2, width), f32)],
        ),
        out_shape=(full, full, jax.ShapeDtypeStruct((tokens, width), bf16), jax.ShapeDtypeStruct((tokens, 1), f32)),
        compiler_params=params(),
        cost_estimate=light(),
        name="join_forward",
    )(place, local, run, mix_pre, mine, theirs, gain)


def scan_backward_kernel(
    grad_ref, state_ref, mix_ref, forget_ref, cut_ref, scale_ref, pull_ref, bound_ref, gain_ref, local_ref, run_ref, whole_ref, carry
):
    @pl.when(pl.program_id(0) == 0)
    def _():
        carry[0:1, :] = jnp.ones_like(carry[0:1, :])
        carry[1:2, :] = jnp.zeros_like(carry[1:2, :])

    lift = 1.0 - bound_ref[...]
    gain = gain_ref[...]
    row = lax.broadcasted_iota(jnp.int32, (ROWS, forget_ref.shape[1]), 0)
    blocks = forget_ref.shape[0] // ROWS

    def step(i, after):
        product, message = after
        at = pl.ds(pl.multiple_of((blocks - 1 - i) * ROWS, ROWS), ROWS)
        a = (1.0 - lift * jax.nn.sigmoid(-forget_ref[at, :])) * (1.0 - cut_ref[at, :])
        mix = mix_ref[at, :]
        weighed = grad_ref[at, :] * gain * (mix * jax.nn.sigmoid(mix))
        own = scale_ref[at, :] * weighed - state_ref[at, :] * pull_ref[at, :]
        b = a * own
        for s in (1, 2, 4):
            reach = row < ROWS - s
            b = b + a * jnp.where(reach, pltpu.roll(b, ROWS - s, 0), 0.0)
            a = a * jnp.where(reach, pltpu.roll(a, ROWS - s, 0), 1.0)
        b = b + a * message
        a = a * product
        last = row == ROWS - 1
        local_ref[at, :] = own + jnp.where(last, message, pltpu.roll(b, ROWS - 1, 0))
        run_ref[at, :] = jnp.where(last, product, pltpu.roll(a, ROWS - 1, 0))
        return a[0:1, :], b[0:1, :]

    product, message = lax.fori_loop(0, blocks, step, (carry[0:1, :], carry[1:2, :]), unroll=4)
    carry[0:1, :] = product
    carry[1:2, :] = message
    whole_ref[...] = carry[...]


def scan_backward(grad, state, mix_pre, forget_pre, cut, scale, pull, bound, gain):
    tokens, width = grad.shape
    full = jax.ShapeDtypeStruct((tokens, width), f32)
    block = pl.BlockSpec((tokens // STEPS, width), lambda i: (STEPS - 1 - i, 0))
    column = pl.BlockSpec((tokens // STEPS, 1), lambda i: (STEPS - 1 - i, 0))
    row = pl.BlockSpec((1, width), lambda i: (0, 0))
    return pl.pallas_call(
        scan_backward_kernel,
        grid=(STEPS,),
        in_specs=[block, block, block, block, column, column, column, row, row],
        out_specs=[block, block, pl.BlockSpec((2, width), lambda i: (0, 0))],
        out_shape=(full, full, jax.ShapeDtypeStruct((2, width), f32)),
        scratch_shapes=[pltpu.VMEM((2, width), f32)],
        compiler_params=params(),
        cost_estimate=light(),
        name="scan_backward",
    )(grad, state, mix_pre, forget_pre, cut, scale, pull, bound, gain)


def join_backward_kernel(
    place, local_ref, run_ref, in_ref, forget_ref, prev_ref, cut_ref, mine_ref, theirs_ref, bound_ref, lower_ref, both_ref, hold
):
    @pl.when(pl.program_id(0) == 0)
    def _():
        hold[...] = arriving(mine_ref, theirs_ref, place[1] == 0)
        lower_ref[...] = jnp.zeros_like(lower_ref)

    width = local_ref.shape[1]
    total = local_ref[...] + run_ref[...] * hold[...]
    lift = 1.0 - bound_ref[...]
    fade = jax.nn.sigmoid(-forget_ref[...])
    keep = lift * fade
    pre = in_ref[...]
    sig = jax.nn.sigmoid(pre)
    d_keep = total * (pre * sig) - total * prev_ref[...] * (1.0 - cut_ref[...])
    lower_ref[...] -= jnp.sum(d_keep * fade, axis=0, keepdims=True)
    both_ref[:, :width] = (total * keep * (sig * (1.0 + pre * (1.0 - sig)))).astype(both_ref.dtype)
    both_ref[:, width:] = (-d_keep * lift * fade * (1.0 - fade)).astype(both_ref.dtype)


def join_backward(place, local, run, in_pre, forget_pre, prev, cut, mine, theirs, bound):
    tokens, width = local.shape
    length = tokens // STEPS
    block = pl.BlockSpec((length, width), lambda i, p: (i, 0))
    column = pl.BlockSpec((length, 1), lambda i, p: (i, 0))
    pairs = pl.BlockSpec(mine.shape, lambda i, p: (0, 0, 0))
    row = pl.BlockSpec((1, width), lambda i, p: (0, 0))
    return pl.pallas_call(
        join_backward_kernel,
        grid_spec=pltpu.PrefetchScalarGridSpec(
            num_scalar_prefetch=1,
            grid=(STEPS,),
            in_specs=[block] * 5 + [column, pairs, pairs, row],
            out_specs=[row, pl.BlockSpec((length, 2 * width), lambda i, p: (i, 0))],
            scratch_shapes=[pltpu.VMEM((1, width), f32)],
        ),
        out_shape=(jax.ShapeDtypeStruct((1, width), f32), jax.ShapeDtypeStruct((tokens, 2 * width), bf16)),
        compiler_params=params(),
        cost_estimate=light(),
        name="join_backward",
    )(place, local, run, in_pre, forget_pre, prev, cut, mine, theirs, bound)


def mixing_kernel(grad_ref, state_ref, mix_ref, scale_ref, gain_ref, mixed_ref, mix_grad_ref, sum_ref, cross_ref):
    @pl.when(pl.program_id(0) == 0)
    def _():
        sum_ref[...] = jnp.zeros_like(sum_ref)

    mix = mix_ref[...]
    sig = jax.nn.sigmoid(mix)
    act = mix * sig
    gain = gain_ref[...]
    grad = grad_ref[...]
    state = state_ref[...]
    level = state * scale_ref[...]
    mixed_ref[...] = (level * gain * act).astype(mixed_ref.dtype)
    mix_grad_ref[...] = (grad * level * gain * (sig * (1.0 + mix * (1.0 - sig)))).astype(mix_grad_ref.dtype)
    sum_ref[...] += jnp.sum(grad * level * act, axis=0, keepdims=True)
    cross_ref[...] = jnp.sum(grad * gain * act * state, axis=1, keepdims=True)


def mixing(grad, state, mix_pre, scale, gain):
    tokens, width = grad.shape
    length = tokens // STEPS
    block = pl.BlockSpec((length, width), lambda i: (i, 0))
    column = pl.BlockSpec((length, 1), lambda i: (i, 0))
    row = pl.BlockSpec((1, width), lambda i: (0, 0))
    half = jax.ShapeDtypeStruct((tokens, width), bf16)
    return pl.pallas_call(
        mixing_kernel,
        grid=(STEPS,),
        in_specs=[block, block, block, column, row],
        out_specs=[block, block, row, column],
        out_shape=(half, half, jax.ShapeDtypeStruct((1, width), f32), jax.ShapeDtypeStruct((tokens, 1), f32)),
        compiler_params=params(),
        cost_estimate=light(),
        name="mixing",
    )(grad, state, mix_pre, scale, gain)


TILES = 1
HALVES = 2


def tiled(rows, width):
    return [jax.ShapeDtypeStruct((rows, width // TILES), f32)] * TILES


def columns(refs):
    return jnp.concatenate([ref[...] for ref in refs], axis=1)


def spread(refs, value):
    wide = value.shape[1] // TILES
    for i, ref in enumerate(refs):
        ref[...] = value[:, i * wide : (i + 1) * wide].astype(ref.dtype)


def call(kernel, name, place, grid, in_specs, out_specs, out_shape, *values, scratch=(), **how):
    return pl.pallas_call(
        kernel,
        grid_spec=pltpu.PrefetchScalarGridSpec(
            num_scalar_prefetch=1, grid=grid, in_specs=in_specs, out_specs=out_specs, scratch_shapes=scratch
        ),
        out_shape=out_shape,
        compiler_params=params(),
        cost_estimate=light(),
        name=name,
        **how,
    )(place, *values)


def enter_kernel(place, input_ref, kept_ref, came_ref, scale_ref, middle_ref, level_ref, *halves):
    middle = input_ref[...].astype(f32) + (kept_ref[...] + came_ref[...]) * scale_ref[...]
    middle_ref[...] = middle
    level = middle * rms_scale(middle)
    level_ref[...] = level
    wide = level.shape[1] // HALVES
    for i, ref in enumerate(halves):
        ref[...] = level[:, i * wide : (i + 1) * wide]


def enter(place, k, inputs, kept, came, scale):
    rows, width = kept.shape
    steps = 4
    part = rows // steps
    here = pl.BlockSpec((part, width), lambda i, p: (i, 0))
    full = jax.ShapeDtypeStruct((rows, width), f32)
    among = lambda i, p: ((2 * k + p[2]) * steps + i, 0)
    specs = [pl.BlockSpec((part, width), among), here, here, pl.BlockSpec((part, 1), among)]
    half = pl.BlockSpec((part, width // HALVES), lambda i, p: (i, 0))
    shapes = [full, full] + [jax.ShapeDtypeStruct((rows, width // HALVES), f32)] * HALVES
    done = call(enter_kernel, "enter", place, (steps,), specs, [here, here] + [half] * HALVES, shapes, inputs, kept, came, scale)
    return done[0], done[1], tuple(done[2:])


def feed_kernel(place, mine_ref, norm_ref, gate_w_ref, up_w_ref, pull_ref, *rest):
    theirs_refs = rest[:HALVES]
    nf_ref, hid_ref, dg_ref, du_ref = rest[-4:]
    rows = mine_ref.shape[0]
    core = place[2]
    norm = norm_ref[...]
    nf_ref[pl.ds(pl.multiple_of(core * rows, rows), rows), :] = (mine_ref[...] * norm).astype(bf16)
    nf_ref[pl.ds(pl.multiple_of((1 - core) * rows, rows), rows), :] = (columns(theirs_refs) * norm).astype(bf16)
    nf = nf_ref[...]
    gate = multiply(nf, gate_w_ref[...])
    upward = multiply(nf, up_w_ref[...])
    sig = jax.nn.sigmoid(gate)
    act = gate * sig
    pull = pull_ref[...]
    hid_ref[...] = (act * upward).astype(bf16)
    dg_ref[...] = (pull * upward * (sig * (1.0 + gate * (1.0 - sig)))).astype(bf16)
    du_ref[...] = (pull * act).astype(bf16)


def feed_forward(place, k, mine, theirs, norm, w_gate, w_up, pull, before):
    rows, width = mine.shape
    units = w_gate.shape[1]
    tokens = pull.shape[0]
    shapes = [(tokens, width)] + [(tokens, units)] * 3
    outs = [pl.BlockSpec((2 * rows, n), lambda i, p: (k, 0)) for _, n in shapes]

    def once(shape, at=lambda i, p: (0, 0)):
        return pl.BlockSpec(shape, at, pipeline_mode=pl.Buffered(1))

    specs = [once(v.shape) for v in (mine, norm, w_gate, w_up)] + [once((2 * rows, units), lambda i, p: (k, 0))]
    specs += [once(v.shape) for v in theirs] + [ANY] * len(before)
    return call(
        feed_kernel,
        "feed_forward",
        place,
        (1,),
        specs,
        outs,
        tuple(jax.ShapeDtypeStruct(shape, bf16) for shape in shapes),
        mine,
        norm,
        w_gate,
        w_up,
        pull,
        *theirs,
        *before,
        input_output_aliases={6 + HALVES + i: i for i in range(len(before))},
    )


def product_kernel(pairs, flipped, place, *refs):
    mine_ref, theirs_ref, held = refs[2 * pairs :]
    core = place[2]
    rows = mine_ref.shape[0] // 2
    times = outer_cols if flipped else multiply
    value = times(refs[0][...], refs[1][...])
    for i in range(1, pairs):
        value = value + times(refs[2 * i][...], refs[2 * i + 1][...])
    held[...] = value
    for k in range(2):
        for ref, at in ((mine_ref, core), (theirs_ref, 1 - core)):
            ref[k * rows : (k + 1) * rows, :] = held[pl.ds(pl.multiple_of((2 * k + at) * rows, rows), rows), :]


def product(place, pairs, flipped):
    first = pairs[0][0]
    tokens = (first[0] if isinstance(first, tuple) else first).shape[0]
    width = pairs[0][1].shape[0 if flipped else 1]
    steps = 4
    tile = width // steps
    specs, values = ([], [])
    for left, right in pairs:
        left, block = left if isinstance(left, tuple) else (left, 0)
        deep = right.shape[1 if flipped else 0]
        specs.append(pl.BlockSpec((tokens, deep), lambda i, p, block=block: (0, block)))
        specs.append(pl.BlockSpec((tile, deep), lambda i, p: (i, 0)) if flipped else pl.BlockSpec((deep, tile), lambda i, p: (0, i)))
        values += [left, right]
    out = pl.BlockSpec((tokens // 2, tile), lambda i, p: (0, i))
    shape = jax.ShapeDtypeStruct((tokens // 2, width), f32)
    kernel = functools.partial(product_kernel, len(pairs), flipped)
    held = [pltpu.VMEM((tokens, tile), f32)]
    mine, theirs = call(kernel, "product", place, (steps,), specs, [out, out], [shape, shape], *values, scratch=held)
    return mine, (theirs,)


def merge_kernel(place, full_ref, *refs):
    refs[-1][...] = full_ref[...] + columns(refs[:-1])


def merge(place, full, pieces):
    rows, width = full.shape
    steps = 4
    here = pl.BlockSpec((rows // steps, width), lambda i, p: (i, 0))
    piece = pl.BlockSpec((rows // steps, width // TILES), lambda i, p: (i, 0))
    return call(
        merge_kernel, "merge", place, (steps,), [here] + [piece] * TILES, here, jax.ShapeDtypeStruct(full.shape, f32), full, *pieces
    )


def leave_kernel(place, value_ref, base_ref, kept_ref, came_ref, gain_ref, grad_ref, total_ref, *change_refs, whole):
    @pl.when(pl.program_id(0) == 0)
    def _():
        grad_ref[...] = jnp.zeros_like(grad_ref)

    value = value_ref[...].astype(f32)
    scale = rms_scale(value)
    level = value * scale
    grad = kept_ref[...] + came_ref[...]
    weighed = grad * gain_ref[...]
    change = scale * (weighed - level * jnp.mean(weighed * level, axis=-1, keepdims=True))
    total = base_ref[...].astype(f32) + change
    grad_ref[...] += jnp.sum(grad * level, axis=0, keepdims=True)
    total_ref[...] = total
    spread(change_refs, total if whole else change)


def leave(place, k, value, base, kept, came, gain, whole):
    rows, width = (kept.shape[0] // 2, kept.shape[1])
    steps = 4
    part = rows // steps
    here = pl.BlockSpec((part, width), lambda i, p: (i, 0))
    mine = pl.BlockSpec((part, width), lambda i, p: (k * steps + i, 0))
    among = pl.BlockSpec((part, width), lambda i, p: ((2 * k + p[2]) * steps + i, 0))
    piece = pl.BlockSpec((part, width // TILES), lambda i, p: (i, 0))
    row = pl.BlockSpec((1, width), lambda i, p: (0, 0))
    done = call(
        functools.partial(leave_kernel, whole=whole),
        "leave",
        place,
        (steps,),
        [here if v.shape[0] == rows else among for v in (value, base)] + [mine, mine, row],
        [row, here] + [piece] * TILES,
        [jax.ShapeDtypeStruct((1, width), f32), jax.ShapeDtypeStruct((rows, width), f32)] + tiled(rows, width),
        value,
        base,
        kept,
        came,
        gain,
    )
    return done[0], done[1], tuple(done[2:])


def result_kernel(place, first_ref, second_ref, kept_ref, came_ref, total_ref, *pieces):
    k = pl.program_id(0) // (pl.num_programs(0) // 2)
    total = jnp.where(k == 0, first_ref[...], second_ref[...]) + kept_ref[...] + came_ref[...]
    total_ref[...] = total
    spread(pieces, total)


def result(place, first, second, kept, came):
    rows, width = kept.shape
    steps = 8
    part = rows // steps
    here = pl.BlockSpec((part, width), lambda i, p: (i, 0))
    folded = pl.BlockSpec((part, width), lambda i, p: (lax.rem(i, steps // 2), 0))
    piece = pl.BlockSpec((part, width // TILES), lambda i, p: (i, 0))
    full = jax.ShapeDtypeStruct((rows, width), f32)
    done = call(
        result_kernel,
        "result",
        place,
        (steps,),
        [folded, folded, here, here],
        [here] + [piece] * TILES,
        [full] + tiled(rows, width),
        first,
        second,
        kept,
        came,
    )
    return done[0], tuple(done[1:])


def assemble_kernel(own, based, scaled, place, *refs):
    whole = refs[-1]
    core = place[2]
    groups, at = ([], 0)
    for count in (own, own, TILES, TILES):
        groups.append(refs[at : at + count])
        at += count
    for i, group in enumerate(groups):
        k, where = (i % 2, core if i < 2 else 1 - core)
        value = columns(group)
        if based:
            value = value + refs[at][k, where].astype(f32)
        if scaled:
            value = value * refs[at][...]
        whole[k, where] = value.astype(whole.dtype)


def assemble(place, mine, theirs, kind, base=None, gain=None):
    mine = [v if isinstance(v, (tuple, list)) else (v,) for v in mine]
    rows = mine[0][0].shape[0]
    width = sum(v.shape[1] for v in mine[0])
    steps = 8
    part = rows // steps
    values = [v for group in (*mine, *theirs) for v in group]
    specs = [pl.BlockSpec((part, v.shape[1]), lambda i, p: (i, 0)) for v in values]
    whole = pl.BlockSpec((2, 2, part, width), lambda i, p: (0, 0, i, 0))
    if base is not None:
        specs.append(whole)
        values.append(base.reshape(2, 2, rows, width))
    if gain is not None:
        specs.append(pl.BlockSpec((1, width), lambda i, p: (0, 0)))
        values.append(gain)
    kernel = functools.partial(assemble_kernel, len(mine[0]), base is not None, gain is not None)
    shape = jax.ShapeDtypeStruct((2, 2, rows, width), kind)
    return call(kernel, "assemble", place, (steps,), specs, whole, shape, *values).reshape(4 * rows, width)


def swap_kernel(place, gate_ref, up_ref, out_ref):
    out_ref[...] = jnp.where(place[1] == 0, up_ref[...].astype(f32), gate_ref[...].astype(f32))


def swap(place, k, d_gate, d_upward):
    tokens, units = d_gate.shape
    steps = 4
    here = pl.BlockSpec((tokens // 2 // steps, units), lambda i, p: (k * steps + i, 0))
    out = pl.BlockSpec((tokens // 2 // steps, units), lambda i, p: (i, 0))
    shape = jax.ShapeDtypeStruct((tokens // 2, units), f32)
    return call(swap_kernel, "swap", place, (steps,), [here, here], out, shape, d_gate, d_upward)


def rise_kernel(place, up_ref, down_ref, came_up_ref, came_down_ref, up_out_ref, down_out_ref):
    up_out_ref[...] = up_ref[...] + came_up_ref[...]
    down_out_ref[...] = down_ref[...] + came_down_ref[...]


def rise(place, *values):
    rows, wide = values[0].shape
    steps = 4
    here = pl.BlockSpec((rows // steps, wide), lambda i, p: (i, 0))
    shape = jax.ShapeDtypeStruct((rows, wide), f32)
    return call(rise_kernel, "rise", place, (steps,), [here] * 4, [here, here], [shape, shape], *values)


def settle_kernel(place, block_ref, up_ref, down_ref, out_ref):
    out_ref[...] = block_ref[...] + up_ref[...] + down_ref[...]


def settle(place, *values):
    rows, wide = values[0].shape
    steps = 4
    here = pl.BlockSpec((rows // steps, wide), lambda i, p: (i, 0))
    return call(settle_kernel, "settle", place, (steps,), [here] * 3, here, jax.ShapeDtypeStruct((rows, wide), f32), *values)


def back_kernel(place, left_ref, right_ref, out_ref):
    out_ref[...] = outer_cols(left_ref[...], right_ref[...])


def back(place, left, right):
    tokens, width = left.shape
    deep = right.shape[0]
    steps = 4
    here = pl.BlockSpec((tokens // steps, width), lambda i, p: (i, 0))
    out = pl.BlockSpec((tokens // steps, deep), lambda i, p: (i, 0))
    specs = [here, pl.BlockSpec(right.shape, lambda i, p: (0, 0))]
    return call(back_kernel, "back", place, (steps,), specs, out, jax.ShapeDtypeStruct((tokens, deep), f32), left, right)


def place_block(outs, value, at=0):
    wide = value.shape[1]
    if len(outs) == 1:
        outs[0][0, :, at : at + wide] = value
        return
    for j, ref in enumerate(outs):

        @pl.when(pl.program_id(0) == j)
        def _():
            ref[:, at : at + wide] = value


def weigh_kernel(pairs, halves, place, *refs):
    outs = refs[2 * pairs + (2 if halves else 0) :]
    at = 0
    for i in range(pairs):
        value = inner_rows(refs[2 * i][...], refs[2 * i + 1][...])
        wide = value.shape[1]
        if halves:
            first, second = refs[2 * pairs : 2 * pairs + 2]
            early = pl.program_id(0) < pl.num_programs(0) // 2
            value = value + jnp.where(early, first[0, :, at : at + wide], second[0, :, at : at + wide])
        place_block(outs, value, at)
        at += wide


def weigh_both_kernel(place, left_ref, gate_ref, up_ref, far_left_ref, first_ref, second_ref, *outs):
    half = first_ref.shape[0]
    right = jnp.where(place[1] == 0, gate_ref[...], up_ref[...])
    value = inner_rows(left_ref[...], right)
    value = value + inner_rows(far_left_ref[:half, :], first_ref[...].astype(bf16))
    place_block(outs, value + inner_rows(far_left_ref[half:, :], second_ref[...].astype(bf16)))


def weigh_call(kernel, place, side, lefts, rights, order, wide, halves=(), count=None, first=0):
    count = DEEP if count is None else count
    rows = lefts[0].shape[1] // (2 * DEEP)

    def chosen(j, p):
        return (0, 2 * lax.rem(p[0] + first + j, DEEP) + (p[1] if side == 0 else 1 - p[1]))

    specs = {id(v): pl.BlockSpec((v.shape[0], rows), chosen) for v in lefts}
    specs |= {id(v): pl.BlockSpec(v.shape, lambda j, p: (0, 0)) for v in rights}
    half = pl.BlockSpec((1, rows, wide), lambda j, p: (lax.rem(j, DEEP // 2), 0, 0))
    if count == DEEP:
        block = [pl.BlockSpec((rows, wide), lambda j, p: (0, 0))] * DEEP
        shape = [jax.ShapeDtypeStruct((rows, wide), f32)] * DEEP
    else:
        block = pl.BlockSpec((1, rows, wide), lambda j, p: (j, 0, 0))
        shape = jax.ShapeDtypeStruct((count, rows, wide), f32)
    return call(
        kernel, "weigh", place, (count,), [specs[id(v)] for v in order] + [half] * len(halves), block, shape, *order, *halves
    )


def weigh(place, pairs, side, halves=(), count=None, first=0):
    order = [v for pair in pairs for v in pair]
    wide = sum(right.shape[1] for _, right in pairs)
    kernel = functools.partial(weigh_kernel, len(pairs), len(halves) == 2)
    return weigh_call(kernel, place, side, order[::2], order[1::2], order, wide, halves, count, first)


def weigh_both(place, side, left, gate, up, far_left, first, second):
    order = [left, gate, up, far_left, first, second]
    return weigh_call(weigh_both_kernel, place, side, [left, far_left], [gate, up, first, second], order, gate.shape[1])


SEQ, MP, DEEP = 8, 4, 4
CORE = [(i, i ^ 1) for i in range(MP)]
ACROSS = [(i, i ^ 2) for i in range(MP)]
BESIDE = [(i, i ^ 1) for i in range(SEQ)]
UP = [[(2 * z + y, 2 * z + 2 + y) for z in range(t) for y in range(2)] for t in range(DEEP)]
DOWN = [[(2 * z + y, 2 * z - 2 + y) for z in range(DEEP - t, DEEP) for y in range(2)] for t in range(DEEP)]


def over_core(v):
    return jax.tree.map(lambda part: lax.ppermute(part, "mp", CORE), v)


def over_x(v):
    return lax.ppermute(v, "mp", ACROSS)


def over_y(v):
    return lax.ppermute(v, "seq", BESIDE)


def along(bit):
    return lambda v: lax.ppermute(v, "seq", [(i, i ^ bit) for i in range(SEQ)])


def along_line(t):
    return lambda v: (lax.ppermute(v[0], "seq", UP[t]), lax.ppermute(v[1], "seq", DOWN[t]))


def reaching(reverse):
    def send(whole):
        rounds = [whole]
        for k in range(1, DEEP):
            pairs = [(2 * z + i, 2 * (z + k) + i) for z in range(DEEP - k) for i in range(2)]
            rounds.append(lax.ppermute(whole, "seq", [(b, a) for a, b in pairs] if reverse else pairs))
        return tuple(rounds)

    return send


class Names:
    def __getattr__(self, name):
        return name


N = Names()


def of(name, k):
    return name + str(k)


def sent(name):
    return name + "_"


def wait(name):
    return name + "!"


def flat(reads):
    return [reads] if isinstance(reads, str) else [name for part in reads for name in flat(part)]


class Steps:
    def __init__(self, place, known):
        self.place = place
        self.known = known
        self.steps = {}
        self.arrivals = set()
        self.last = None

    def add(self, name, reads, work, *sends):
        self.steps[name] = (flat(reads), work, sends)

    def settle(self, *names):
        if self.last is None:
            return
        last, sends = self.last
        self.last = None
        names = [v for v in dict.fromkeys(names) if v != last]
        held = {v: self.known[v] for v in [*names, last]}
        self.known.update(together(held))
        done = self.known[last]
        for arrival, how, *part in sends:
            self.known[arrival] = how(done[part[0]] if part else done)
            self.arrivals.add(arrival)

    def run(self, name):
        if name.endswith("!"):
            self.settle()
            name = name[:-1]
            self.arrivals.discard(name)
            self.last = (name, ())
            return
        reads, work, sends = self.steps.pop(name)
        self.settle(*[v for v in reads if v in self.known and v not in self.arrivals])
        self.known[name] = work(*[self.known[v] for v in reads])
        self.last = (name, sends)

    def line(self, name, source):
        reads, work, _ = self.steps[source]
        self.steps[source] = (reads, work, ((sent(of(name, 1)), lambda v: along_line(1)((v[DEEP - 1], v[1]))),))
        for t in range(2, DEEP):
            self.add(
                of(name, t),
                (source, sent(of(name, t - 1))),
                lambda v, came, t=t: rise(self.place, v[DEEP - t], v[t], *came),
                (sent(of(name, t)), along_line(t)),
            )


ORDER = (
    N.in_pre,
    N.forget,
    N.scan,
    N.mix,
    N.stack,
    N.join,
    N.square,
    wait(N.square_),
    N.send0,
    N.square2,
    N.send1,
    wait(N.square2_),
    N.keep0,
    N.keep1,
    N.scale,
    N.pull,
    N.enter0,
    N.feed0,
    N.gates0,
    N.enter1,
    N.feed1,
    wait(N.beside0),
    N.unfeed,
    N.down_far,
    N.unfed,
    N.down_own,
    N.p2,
    N.gates1,
    N.spread,
    wait(N.gates0_),
    N.q2,
    N.beside0_,
    N.leave0,
    N.leave1,
    N.p3,
    N.beside1_,
    N.branch,
    wait(N.spread_),
    N.mixed,
    N.far_nf,
    N.mixing,
    N.cross,
    N.cross2,
    N.mix_send0,
    N.spread_sum,
    wait(N.p3_),
    N.tug,
    N.scan_b,
    N.q3,
    N.pair_own,
    N.pair_far,
    N.stack_b,
    N.join_b,
    wait(N.mix_send0_),
    N.both_send1,
    N.p_sum,
    wait(N.q3_),
    N.origin,
    N.r2,
    N.mix_send1,
    wait(N.both_send1_),
    N.result,
    N.s2,
    wait(N.r2_),
    N.both_send0,
    N.source,
    N.mix_keep,
    N.s3,
    N.t2,
    N.out,
    N.both_keep,
    N.r3,
    N.t3,
    N.u2,
    N.enter_b0,
    N.r_sum,
    N.enter_b1,
    N.norms,
    N.small,
    N.u3,
    N.q_sum,
    wait(N.u3_),
    N.small2,
    N.t_sum,
    wait(N.p_sum_),
    wait(N.small2_),
    N.u_sum,
    N.small3,
    N.d_inputs,
    N.s_sum,
    N.smalls,
)


def planned(
    inputs, seq_start, norm_in, w_input, w_forget, w_mix_gate, lower_bound, mix_gain, w_output, norm_ffn, w_gate, w_up, w_down, cotangent
):
    tokens, width = inputs.shape
    quarter = tokens // 4
    units = w_input.shape[1]
    seq = lax.axis_index("seq")
    core = lax.axis_index("mp") % 2
    y = seq % 2
    place = jnp.stack([seq // 2, y, core])
    bound = lower_bound[None, :]
    gain = mix_gain[None, :]
    places = seq * tokens + jnp.arange(tokens, dtype=jnp.int32)
    cut = (seq_start == places).astype(f32)[:, None]
    known = dict(
        inputs=inputs,
        w_output=w_output,
        w_gate=w_gate,
        w_up=w_up,
        w_down=w_down,
        cot=cotangent,
        norm=norm_ffn[None, :],
        norm_in=norm_in[None, :],
        wi=w_input,
        wf=w_forget,
        wm=w_mix_gate,
    )
    plan = Steps(place, known)
    step = plan.add

    def quarters(v, at):
        parts = v.reshape((2, 2, quarter) + v.shape[1:])
        return lax.dynamic_index_in_dim(parts, at, 1, keepdims=False)

    def add(a, b):
        return a + b

    in_float = inputs.astype(f32)
    known[N.normed] = (in_float * rms_scale(in_float) * norm_in).astype(bf16)
    step(N.in_pre, (N.normed, N.wi), multiply)
    step(N.forget, (N.normed, N.wf), multiply)
    step(N.scan, (N.in_pre, N.forget), lambda a, b: scan_forward(a, b, cut, bound), (N.scan_, reaching(False), 2))
    step(N.mix, (N.normed, N.wm), multiply)
    step(N.stack, N.scan_, lambda v: jnp.stack(v), (N.stack_, over_y))
    step(N.join, (N.scan, N.mix, N.stack, N.stack_), lambda a, b, *v: join_forward(place, a[0], a[1], b, *v, gain))

    step(N.square, N.join, lambda v: v[3][:, 0], (N.square_, over_core))
    step(N.square2, (N.square, N.square_), add, (N.square2_, over_x))
    step(N.scale, (N.square2, N.square2_), lambda a, b: lax.rsqrt((a + b) / width + epsilon)[:, None])
    for k in range(2):
        step(of(N.send, k), (N.join, N.w_output), lambda v, w, k=k: multiply(quarters(v[2], 1 - core)[k], w), (sent(of(N.send, k)), over_core))
        step(
            of(N.keep, k), (N.join, N.w_output, sent(of(N.send, k))), lambda v, w, s, k=k: multiply(quarters(v[2], core)[k], w) + s, (sent(of(N.keep, k)), over_x)
        )
    step(N.pull, (N.cot, N.w_down), lambda a, b: back(place, a, b))

    for k in range(2):
        step(
            of(N.enter, k),
            (N.inputs, of(N.keep, k), sent(of(N.keep, k)), N.scale),
            functools.partial(enter, place, k),
            (sent(of(N.level, k)), over_core, 2),
            (of(N.beside, k), over_y, 1),
        )
        step(
            of(N.feed, k),
            ((of(N.enter, k), sent(of(N.level, k)), N.norm, N.w_gate), (N.w_up, N.pull), (N.feed0, N.gates0) if k else ()),
            lambda e, t, n, g, u, p, *before, k=k: feed_forward(place, k, e[1], t, n, g, u, p, before[0] if before else ()),
        )
        step(of(N.gates, k), of(N.feed, k), lambda v, k=k: swap(place, k, v[2], v[3]), (sent(of(N.gates, k)), over_y))

    step(N.down_far, (N.cot, N.feed1), lambda a, b: weigh(place, [(a, b[1])], 1))
    step(N.down_own, (N.cot, N.feed1), lambda a, b: weigh(place, [(a, b[1])], 0))
    plan.line(N.p, N.down_far)
    plan.line(N.q, N.down_own)
    step(N.p_sum, (N.down_far, N.p3_), lambda b, c: settle(place, b[0], *c), (N.p_sum_, over_y))
    step(N.q_sum, (N.down_own, N.q3_, N.p_sum_), lambda b, c, d: (b[0] + c[0] + c[1] + d).T)
    for k in range(2):
        step(sent(of(N.beside, k)), of(N.beside, k), lambda v: (v,), (sent(sent(of(N.beside, k))), over_core))
    step(
        N.far_nf,
        ((N.beside0_, N.beside1_, N.beside0__, N.beside1__), N.norm),
        lambda a, b, c, d, e: assemble(place, (a, b), (c, d), bf16, gain=e),
    )
    both_args = (N.feed1, N.far_nf, N.gates0_, N.gates1_)
    step(N.pair_far, both_args, lambda f, *v: weigh_both(place, 1, f[0], f[2], f[3], *v))
    step(N.pair_own, both_args, lambda f, *v: weigh_both(place, 0, f[0], f[2], f[3], *v))
    plan.line(N.r, N.pair_far)
    plan.line(N.s, N.pair_own)
    step(N.r_sum, (N.pair_far, N.r3_), lambda b, c: settle(place, b[0], *c), (N.r_sum_, over_y))

    def sort_pair(b, c, theirs):
        mine = b[0] + c[0] + c[1]
        return jnp.where(y == 0, mine, theirs), jnp.where(y == 0, theirs, mine)

    step(N.s_sum, (N.pair_own, N.s3_, N.r_sum_), sort_pair)

    step(
        N.unfeed, (N.feed1, N.w_gate, N.w_up), lambda f, g, u: product(place, [(f[2], g), (f[3], u)], True), (N.unfeed_, over_core, 1)
    )
    step(N.unfed, (N.unfeed, N.unfeed_), lambda a, b: merge(place, a[0], b), (N.unfed_, over_x))
    step(N.spread, (N.feed1, N.w_down), lambda f, w: product(place, [(f[1], w)], False), (N.spread_, over_core, 1))
    step(N.spread_sum, (N.spread, N.spread_, N.cross2_), lambda a, b, c: merge(place, a[0], b), (N.spread_sum_, over_x))
    step(
        N.result,
        (N.enter0, N.enter1, N.spread_sum, N.spread_sum_),
        lambda a, b, c, d: result(place, a[0], b[0], c, d),
        (N.result_, over_core, 1),
    )

    def halves(v):
        return (v[:quarter], v[quarter:])

    step(
        N.out,
        (N.result, N.result_),
        lambda a, b: assemble(place, halves(a[0]), list(zip(*[halves(v) for v in b], strict=True)), bf16),
    )

    for k in range(2):
        step(
            of(N.leave, k),
            ((of(N.enter, k), N.cot, N.unfed, N.unfed_), N.norm),
            lambda e, *v, k=k: leave(place, k, e[0], *v, False),
            (sent(of(N.leave, k)), over_core, 2),
        )
    step(
        N.branch,
        ((N.leave0, N.leave1, N.leave0_, N.leave1_), N.cot),
        lambda a, b, c, d, e: assemble(place, (a[2], b[2]), (c, d), bf16, base=e),
    )
    step(N.mixed, (N.branch, N.w_output), lambda a, b: back(place, a, b))
    step(N.mixing, (N.mixed, N.join, N.mix, N.scale), lambda d, j, m, s: mixing(d, j[0], m, s, gain))
    step(N.cross, N.mixing, lambda v: v[3][:, 0], (N.cross_, over_core))
    step(N.cross2, (N.cross, N.cross_), add, (N.cross2_, over_x))
    step(N.tug, (N.cross2, N.cross2_, N.scale), lambda a, b, s: s**3 * ((a + b)[:, None] / width))
    step(
        N.scan_b,
        ((N.mixed, N.join, N.mix, N.forget), (N.scale, N.tug)),
        lambda d, j, m, f, s, t: scan_backward(d, j[0], m, f, cut, s, t, bound, gain),
        (N.scan_b_, reaching(True), 2),
    )
    step(N.stack_b, N.scan_b_, lambda v: jnp.stack(v), (N.stack_b_, over_y))
    step(
        N.join_b,
        ((N.scan_b, N.in_pre, N.forget, N.join), (N.stack_b, N.stack_b_)),
        lambda s, i, f, j, *v: join_backward(place, s[0], s[1], i, f, j[1], cut, *v, bound),
    )

    def mix_pairs(n, m, b):
        return [(n, m[1]), (b, m[0])]

    for k in range(2):
        step(
            of(N.mix_send, k),
            (N.normed, N.mixing, N.branch),
            lambda *v, k=k: weigh(place, mix_pairs(*v), 1, (), DEEP // 2, k * DEEP // 2),
            (sent(of(N.mix_send, k)), over_y),
        )
        step(
            of(N.both_send, k),
            (N.normed, N.join_b),
            lambda n, b, k=k: weigh(place, [(n, b[1])], 1, (), DEEP // 2, k * DEEP // 2),
            (sent(of(N.both_send, k)), over_y),
        )
    step(N.mix_keep, ((N.normed, N.mixing, N.branch, N.mix_send0_), N.mix_send1_), lambda *v: weigh(place, mix_pairs(*v[:3]), 0, v[3:]))
    step(N.both_keep, (N.normed, N.join_b, N.both_send0_, N.both_send1_), lambda n, b, *v: weigh(place, [(n, b[1])], 0, v))
    plan.line(N.t, N.mix_keep)
    plan.line(N.u, N.both_keep)

    def sort_mix(b, c):
        total = b[0] + c[0] + c[1]
        return total[:, :units], total[:, units:].T

    def sort_both(b, c):
        total = b[0] + c[0] + c[1]
        return total[:, :units], total[:, units:]

    step(N.t_sum, (N.mix_keep, N.t3_), sort_mix)
    step(N.u_sum, (N.both_keep, N.u3_), sort_both)

    step(
        N.origin,
        ((N.join_b, N.mixing, N.wi, N.wf), N.wm),
        lambda b, m, i, f, w: product(place, [((b[1], 0), i), ((b[1], 1), f), (m[1], w)], True),
        (N.origin_, over_core, 1),
    )
    step(N.source, (N.origin, N.origin_), lambda a, b: merge(place, a[0], b), (N.source_, over_x))
    for k in range(2):
        step(
            of(N.enter_b, k),
            ((N.inputs, of(N.leave, k), N.source, N.source_), N.norm_in),
            lambda i, m, *v, k=k: leave(place, k, i, m[1], *v, True),
            (sent(of(N.enter_b, k)), over_core, 2),
        )
    step(
        N.d_inputs,
        (N.enter_b0, N.enter_b1, N.enter_b0_, N.enter_b1_),
        lambda a, b, c, d: assemble(place, (a[1], b[1]), (c, d), f32),
    )
    step(
        N.norms,
        (N.enter_b0, N.enter_b1, N.leave0, N.leave1),
        lambda a, b, c, d: jnp.concatenate([a[0] + b[0], c[0] + d[0]], axis=1)[0],
        (N.norms_, over_core),
    )
    step(
        N.small,
        ((N.norms, N.norms_, N.join_b, N.mixing), N.scan),
        lambda a, b, c, d, e: jnp.concatenate([a + b, c[0][0], d[2][0], e[3][0]]),
        (N.small_, along(1)),
    )
    step(N.small2, (N.small, N.small_), add, (N.small2_, along(2)))
    step(N.small3, (N.small2, N.small2_), add, (N.small3_, along(4)))
    step(N.smalls, (N.small3, N.small3_), add)

    for name in ORDER:
        plan.run(name)
    plan.settle()
    smalls = known[N.smalls]
    piece = width // SEQ
    d_norm_in = lax.dynamic_slice_in_dim(smalls, seq * piece, piece)
    d_norm_ffn = lax.dynamic_slice_in_dim(smalls, width + seq * piece, piece)
    d_lower, d_mix_gain, forget_sum = (smalls[2 * width + i * units : 2 * width + (i + 1) * units] for i in range(3))
    mix_grad, out_grad = known[N.t_sum]
    in_grad, forget_grad = known[N.u_sum]
    gate_grad, up_grad = known[N.s_sum]
    return (
        known[N.out],
        known[N.d_inputs],
        d_norm_in,
        in_grad,
        forget_grad,
        mix_grad,
        d_lower,
        d_mix_gain,
        out_grad,
        d_norm_ffn,
        gate_grad,
        up_grad,
        known[N.q_sum],
        forget_sum / (tokens * SEQ),
    )


def entering(x, axis, combine, identity, reverse):
    length, index = (lax.axis_size(axis), lax.axis_index(axis))
    everything = jax.tree.map(lambda part: lax.all_gather(part, axis), x)
    start = jax.tree.map(
        lambda part, zero: jnp.broadcast_to(jnp.asarray(zero, part.dtype), part.shape), x, identity
    )

    def turn(k, before):
        at = length - 1 - k if reverse else k
        reached = at > index if reverse else at < index
        new = combine(before, jax.tree.map(lambda part: part[at], everything))
        return jax.tree.map(lambda a, b: jnp.where(reached, a, b), new, before)

    return lax.fori_loop(0, length, turn, start)


def compose(earlier, later):
    return (earlier[0] * later[0], later[0] * earlier[1] + later[1])


def carry_forward(whole, ending):
    result = entering(
        (whole, ending), "seq", compose, (jnp.ones_like(whole), jnp.zeros_like(ending)), False
    )
    return result[1]


def carry_backward(whole, leading):
    result = entering(
        (whole, leading), "seq", compose, (jnp.ones_like(whole), jnp.zeros_like(leading)), True
    )
    return result[1]


def general(
    inputs,
    seq_start,
    norm_in,
    w_input,
    w_forget,
    w_mix_gate,
    lower_bound,
    mix_gain,
    w_output,
    norm_ffn,
    w_gate,
    w_up,
    w_down,
    cotangent,
):
    tokens_here = inputs.shape[0]
    width = inputs.shape[1]
    places = lax.axis_index("seq") * tokens_here + jnp.arange(tokens_here, dtype=jnp.int32)
    restart = (seq_start == places).astype(jnp.float32)[:, None]
    in_float = inputs.astype(jnp.float32)
    scale_in = rms_scale(in_float)
    normed = (in_float * scale_in * norm_in).astype(jnp.bfloat16)
    in_pre = multiply(normed, w_input)
    forget_pre = multiply(normed, w_forget)
    mix_pre = multiply(normed, w_mix_gate)
    fade = jax.nn.sigmoid(-forget_pre)
    forget_local = jnp.sum(1.0 - fade, axis=0)
    keep = (1.0 - lower_bound) * fade
    decay = (1.0 - keep) * (1.0 - restart)
    act_in = jax.nn.silu(in_pre)
    drive = act_in * keep
    decay_run, state_local = lax.associative_scan(compose, (decay, drive), axis=0)
    state_in = carry_forward(decay_run[-1], state_local[-1])
    state = state_local + decay_run * state_in
    squares = lax.psum(jnp.sum(state * state, axis=1), "mp")
    mix_scale = lax.rsqrt(squares / width + epsilon)[:, None]
    gate_act = jax.nn.silu(mix_pre)
    normed_state = state * mix_scale
    mixed = (normed_state * mix_gain * gate_act).astype(jnp.bfloat16)
    branch = lax.psum(multiply(mixed, w_output), "mp")
    middle = in_float + branch
    scale_ffn = rms_scale(middle)
    normed_ffn = (middle * scale_ffn * norm_ffn).astype(jnp.bfloat16)
    gate = multiply(normed_ffn, w_gate)
    upward = multiply(normed_ffn, w_up)
    silu_gate = jax.nn.silu(gate)
    hidden = (silu_gate * upward).astype(jnp.bfloat16)
    feed = lax.psum(multiply(hidden, w_down), "mp")
    out = (middle + feed).astype(jnp.bfloat16)
    grad_float = cotangent.astype(jnp.float32)
    d_hidden = outer_cols(cotangent, w_down)
    d_w_down = inner_rows(hidden, cotangent)
    d_gate = (d_hidden * upward * silu_slope(gate)).astype(jnp.bfloat16)
    d_upward = (d_hidden * silu_gate).astype(jnp.bfloat16)
    d_normed_ffn = lax.psum(outer_cols(d_gate, w_gate) + outer_cols(d_upward, w_up), "mp")
    d_w_gate = inner_rows(normed_ffn, d_gate)
    d_w_up = inner_rows(normed_ffn, d_upward)
    d_norm_ffn = jnp.sum(d_normed_ffn * middle * scale_ffn, axis=0)
    scaled_ffn = d_normed_ffn * norm_ffn
    d_middle = (
        grad_float
        + scale_ffn * scaled_ffn
        - middle * scale_ffn**3 * jnp.mean(scaled_ffn * middle, axis=-1, keepdims=True)
    )
    d_branch = d_middle.astype(jnp.bfloat16)
    d_w_output = inner_rows(mixed, d_branch)
    d_mixed = outer_cols(d_branch, w_output)
    d_mix_gain = jnp.sum(d_mixed * normed_state * gate_act, axis=0)
    d_mix_pre = (d_mixed * normed_state * mix_gain * silu_slope(mix_pre)).astype(jnp.bfloat16)
    scaled_mix = d_mixed * mix_gain * gate_act
    cross = lax.psum(jnp.sum(scaled_mix * state, axis=1), "mp")
    d_state = mix_scale * scaled_mix - state * mix_scale**3 * (cross / width)[:, None]
    next_decay = jnp.concatenate([decay[1:], jnp.ones_like(decay[:1])], axis=0)
    tail_decay, tail_grad = lax.associative_scan(
        compose, (next_decay, d_state), reverse=True, axis=0
    )
    carried = carry_backward(decay_run[-1], decay[0] * tail_grad[0])
    total = tail_grad + tail_decay * carried
    prev_state = jnp.concatenate([state_in[None], state[:-1]], axis=0)
    d_keep = total * act_in - total * prev_state * (1.0 - restart)
    d_lower = -jnp.sum(d_keep * fade, axis=0)
    d_in_pre = (total * keep * silu_slope(in_pre)).astype(jnp.bfloat16)
    d_forget_pre = (-d_keep * (1.0 - lower_bound) * fade * (1.0 - fade)).astype(jnp.bfloat16)
    d_normed = lax.psum(
        outer_cols(d_in_pre, w_input)
        + outer_cols(d_forget_pre, w_forget)
        + outer_cols(d_mix_pre, w_mix_gate),
        "mp",
    )
    d_w_input = inner_rows(normed, d_in_pre)
    d_w_forget = inner_rows(normed, d_forget_pre)
    d_w_mix_gate = inner_rows(normed, d_mix_pre)
    d_norm_in = jnp.sum(d_normed * in_float * scale_in, axis=0)
    scaled_in = d_normed * norm_in
    d_inputs = (
        d_middle
        + scale_in * scaled_in
        - in_float * scale_in**3 * jnp.mean(scaled_in * in_float, axis=-1, keepdims=True)
    )
    row_part = (
        lax.psum_scatter(d_w_input, "seq", scatter_dimension=0, tiled=True),
        lax.psum_scatter(d_w_forget, "seq", scatter_dimension=0, tiled=True),
        lax.psum_scatter(d_w_mix_gate, "seq", scatter_dimension=0, tiled=True),
        lax.psum_scatter(d_w_gate, "seq", scatter_dimension=0, tiled=True),
        lax.psum_scatter(d_w_up, "seq", scatter_dimension=0, tiled=True),
        lax.psum_scatter(d_norm_in, "seq", scatter_dimension=0, tiled=True),
        lax.psum_scatter(d_norm_ffn, "seq", scatter_dimension=0, tiled=True),
    )
    col_part = (
        lax.psum_scatter(d_w_output, "seq", scatter_dimension=1, tiled=True),
        lax.psum_scatter(d_w_down, "seq", scatter_dimension=1, tiled=True),
    )
    out_grad = col_part[0]
    down_grad = col_part[1]
    small_part = lax.psum((d_lower, d_mix_gain, forget_local), "seq")
    forget_mean = small_part[2] / (tokens_here * lax.axis_size("seq"))
    return (
        out,
        d_inputs,
        row_part[5],
        row_part[0],
        row_part[1],
        row_part[2],
        small_part[0],
        small_part[1],
        out_grad,
        row_part[6],
        row_part[3],
        row_part[4],
        down_grad,
        forget_mean,
    )


def solution(mesh):
    fits = mesh.shape["seq"] == SEQ and mesh.shape["mp"] == MP
    return jax.shard_map(
        planned if fits else general,
        mesh=mesh,
        in_specs=(
            P("seq", None),
            P("seq"),
            P(),
            P(None, "mp"),
            P(None, "mp"),
            P(None, "mp"),
            P("mp"),
            P("mp"),
            P("mp", None),
            P(),
            P(None, "mp"),
            P(None, "mp"),
            P("mp", None),
            P("seq", None),
        ),
        out_specs=(
            P("seq", None),
            P("seq", None),
            P("seq"),
            P("seq", "mp"),
            P("seq", "mp"),
            P("seq", "mp"),
            P("mp"),
            P("mp"),
            P("mp", "seq"),
            P("seq"),
            P("seq", "mp"),
            P("seq", "mp"),
            P("mp", "seq"),
            P("mp"),
        ),
        check_vma=False,
    )
```

```python
import functools

import jax
import jax.numpy as jnp
from jax import lax
from jax.experimental import pallas as pl
from jax.experimental.pallas import tpu as pltpu
from jax.sharding import PartitionSpec as P

epsilon = 1e-06
f32 = jnp.float32
bf16 = jnp.bfloat16
together = lax.optimization_barrier


def multiply(left, right):
    return jnp.dot(left, right, preferred_element_type=f32)


def inner_rows(left, right):
    return lax.dot_general(left, right, (((0,), (0,)), ((), ())), preferred_element_type=f32)


def outer_cols(left, right):
    return lax.dot_general(left, right, (((1,), (1,)), ((), ())), preferred_element_type=f32)


def rms_scale(values):
    return lax.rsqrt(jnp.mean(values * values, axis=-1, keepdims=True) + epsilon)


def silu_slope(values):
    sig = jax.nn.sigmoid(values)
    return sig * (1.0 + values * (1.0 - sig))


BIG = 48 * 1024 * 1024
ANY = pl.BlockSpec(memory_space=pl.ANY)


def params():
    return pltpu.CompilerParams(vmem_limit_bytes=BIG)


def light():
    return pl.CostEstimate(flops=0, bytes_accessed=1024, transcendentals=0)


ROWS = 8
STEPS = 4


def scan_forward_kernel(in_ref, forget_ref, cut_ref, bound_ref, local_ref, run_ref, whole_ref, sum_ref, carry):
    @pl.when(pl.program_id(0) == 0)
    def _():
        carry[0:1, :] = jnp.ones_like(carry[0:1, :])
        carry[1:2, :] = jnp.zeros_like(carry[1:2, :])
        sum_ref[...] = jnp.zeros_like(sum_ref)

    lift = 1.0 - bound_ref[...]
    shape = (ROWS, forget_ref.shape[1])
    row = lax.broadcasted_iota(jnp.int32, shape, 0)

    def step(i, before):
        product, state, gates = before
        at = pl.ds(pl.multiple_of(i * ROWS, ROWS), ROWS)
        fade = jax.nn.sigmoid(-forget_ref[at, :])
        keep = lift * fade
        a = (1.0 - keep) * (1.0 - cut_ref[at, :])
        pre = in_ref[at, :]
        b = pre * jax.nn.sigmoid(pre) * keep
        for s in (1, 2, 4):
            reach = row >= s
            b = b + a * jnp.where(reach, pltpu.roll(b, s, 0), 0.0)
            a = a * jnp.where(reach, pltpu.roll(a, s, 0), 1.0)
        b = b + a * state
        a = a * product
        local_ref[at, :] = b
        run_ref[at, :] = a
        return a[ROWS - 1 :, :], b[ROWS - 1 :, :], gates + (1.0 - fade)

    start = (carry[0:1, :], carry[1:2, :], jnp.zeros(shape, f32))
    product, state, gates = lax.fori_loop(0, forget_ref.shape[0] // ROWS, step, start, unroll=4)
    carry[0:1, :] = product
    carry[1:2, :] = state
    whole_ref[...] = carry[...]
    sum_ref[...] += jnp.sum(gates, axis=0, keepdims=True)


def scan_forward(in_pre, forget_pre, cut, bound):
    tokens, width = in_pre.shape
    full = jax.ShapeDtypeStruct((tokens, width), f32)
    block = pl.BlockSpec((tokens // STEPS, width), lambda i: (i, 0))
    row = pl.BlockSpec((1, width), lambda i: (0, 0))
    return pl.pallas_call(
        scan_forward_kernel,
        grid=(STEPS,),
        in_specs=[block, block, pl.BlockSpec((tokens // STEPS, 1), lambda i: (i, 0)), row],
        out_specs=[block, block, pl.BlockSpec((2, width), lambda i: (0, 0)), row],
        out_shape=(full, full, jax.ShapeDtypeStruct((2, width), f32), jax.ShapeDtypeStruct((1, width), f32)),
        scratch_shapes=[pltpu.VMEM((2, width), f32)],
        compiler_params=params(),
        cost_estimate=light(),
        name="scan_forward",
    )(in_pre, forget_pre, cut, bound)


def arriving(mine_ref, theirs_ref, later):
    def over(pair, total):
        return pair[0] * total + pair[1]

    total = jnp.zeros_like(mine_ref[0, 0:1, :])
    for k in range(mine_ref.shape[0] - 1, -1, -1):
        mine, theirs = ((ref[k, 0:1, :], ref[k, 1:2, :]) for ref in (mine_ref, theirs_ref))
        if k == 0:
            return jnp.where(later, over(theirs, total), total)
        total = jnp.where(later, over(mine, over(theirs, total)), over(theirs, over(mine, total)))


def join_forward_kernel(place, local_ref, run_ref, mix_ref, mine_ref, theirs_ref, gain_ref, state_ref, prev_ref, u_ref, square_ref, hold):
    @pl.when(pl.program_id(0) == 0)
    def _():
        hold[0:1, :] = arriving(mine_ref, theirs_ref, place[1] == 1)
        hold[1:2, :] = hold[0:1, :]

    state = local_ref[...] + run_ref[...] * hold[0:1, :]
    mix = mix_ref[...]
    rows = lax.broadcasted_iota(jnp.int32, state.shape, 0)
    state_ref[...] = state
    prev_ref[...] = jnp.where(rows == 0, hold[1:2, :], pltpu.roll(state, 1, 0))
    u_ref[...] = (state * gain_ref[...] * (mix * jax.nn.sigmoid(mix))).astype(u_ref.dtype)
    square_ref[...] = jnp.sum(state * state, axis=1, keepdims=True)
    hold[1:2, :] = state[state.shape[0] - 1 :, :]


def join_forward(place, local, run, mix_pre, mine, theirs, gain):
    tokens, width = local.shape
    length = tokens // STEPS
    block = pl.BlockSpec((length, width), lambda i, p: (i, 0))
    pairs = pl.BlockSpec(mine.shape, lambda i, p: (0, 0, 0))
    row = pl.BlockSpec((1, width), lambda i, p: (0, 0))
    full = jax.ShapeDtypeStruct((tokens, width), f32)
    return pl.pallas_call(
        join_forward_kernel,
        grid_spec=pltpu.PrefetchScalarGridSpec(
            num_scalar_prefetch=1,
            grid=(STEPS,),
            in_specs=[block, block, block, pairs, pairs, row],
            out_specs=[block, block, block, pl.BlockSpec((length, 1), lambda i, p: (i, 0))],
            scratch_shapes=[pltpu.VMEM((2, width), f32)],
        ),
        out_shape=(full, full, jax.ShapeDtypeStruct((tokens, width), bf16), jax.ShapeDtypeStruct((tokens, 1), f32)),
        compiler_params=params(),
        cost_estimate=light(),
        name="join_forward",
    )(place, local, run, mix_pre, mine, theirs, gain)


def scan_backward_kernel(
    grad_ref, state_ref, mix_ref, forget_ref, cut_ref, scale_ref, pull_ref, bound_ref, gain_ref, local_ref, run_ref, whole_ref, carry
):
    @pl.when(pl.program_id(0) == 0)
    def _():
        carry[0:1, :] = jnp.ones_like(carry[0:1, :])
        carry[1:2, :] = jnp.zeros_like(carry[1:2, :])

    lift = 1.0 - bound_ref[...]
    gain = gain_ref[...]
    row = lax.broadcasted_iota(jnp.int32, (ROWS, forget_ref.shape[1]), 0)
    blocks = forget_ref.shape[0] // ROWS

    def step(i, after):
        product, message = after
        at = pl.ds(pl.multiple_of((blocks - 1 - i) * ROWS, ROWS), ROWS)
        a = (1.0 - lift * jax.nn.sigmoid(-forget_ref[at, :])) * (1.0 - cut_ref[at, :])
        mix = mix_ref[at, :]
        weighed = grad_ref[at, :] * gain * (mix * jax.nn.sigmoid(mix))
        own = scale_ref[at, :] * weighed - state_ref[at, :] * pull_ref[at, :]
        b = a * own
        for s in (1, 2, 4):
            reach = row < ROWS - s
            b = b + a * jnp.where(reach, pltpu.roll(b, ROWS - s, 0), 0.0)
            a = a * jnp.where(reach, pltpu.roll(a, ROWS - s, 0), 1.0)
        b = b + a * message
        a = a * product
        last = row == ROWS - 1
        local_ref[at, :] = own + jnp.where(last, message, pltpu.roll(b, ROWS - 1, 0))
        run_ref[at, :] = jnp.where(last, product, pltpu.roll(a, ROWS - 1, 0))
        return a[0:1, :], b[0:1, :]

    product, message = lax.fori_loop(0, blocks, step, (carry[0:1, :], carry[1:2, :]), unroll=4)
    carry[0:1, :] = product
    carry[1:2, :] = message
    whole_ref[...] = carry[...]


def scan_backward(grad, state, mix_pre, forget_pre, cut, scale, pull, bound, gain):
    tokens, width = grad.shape
    full = jax.ShapeDtypeStruct((tokens, width), f32)
    block = pl.BlockSpec((tokens // STEPS, width), lambda i: (STEPS - 1 - i, 0))
    column = pl.BlockSpec((tokens // STEPS, 1), lambda i: (STEPS - 1 - i, 0))
    row = pl.BlockSpec((1, width), lambda i: (0, 0))
    return pl.pallas_call(
        scan_backward_kernel,
        grid=(STEPS,),
        in_specs=[block, block, block, block, column, column, column, row, row],
        out_specs=[block, block, pl.BlockSpec((2, width), lambda i: (0, 0))],
        out_shape=(full, full, jax.ShapeDtypeStruct((2, width), f32)),
        scratch_shapes=[pltpu.VMEM((2, width), f32)],
        compiler_params=params(),
        cost_estimate=light(),
        name="scan_backward",
    )(grad, state, mix_pre, forget_pre, cut, scale, pull, bound, gain)


def join_backward_kernel(
    place, local_ref, run_ref, in_ref, forget_ref, prev_ref, cut_ref, mine_ref, theirs_ref, bound_ref, lower_ref, both_ref, hold
):
    @pl.when(pl.program_id(0) == 0)
    def _():
        hold[...] = arriving(mine_ref, theirs_ref, place[1] == 0)
        lower_ref[...] = jnp.zeros_like(lower_ref)

    width = local_ref.shape[1]
    total = local_ref[...] + run_ref[...] * hold[...]
    lift = 1.0 - bound_ref[...]
    fade = jax.nn.sigmoid(-forget_ref[...])
    keep = lift * fade
    pre = in_ref[...]
    sig = jax.nn.sigmoid(pre)
    d_keep = total * (pre * sig) - total * prev_ref[...] * (1.0 - cut_ref[...])
    lower_ref[...] -= jnp.sum(d_keep * fade, axis=0, keepdims=True)
    both_ref[:, :width] = (total * keep * (sig * (1.0 + pre * (1.0 - sig)))).astype(both_ref.dtype)
    both_ref[:, width:] = (-d_keep * lift * fade * (1.0 - fade)).astype(both_ref.dtype)


def join_backward(place, local, run, in_pre, forget_pre, prev, cut, mine, theirs, bound):
    tokens, width = local.shape
    length = tokens // STEPS
    block = pl.BlockSpec((length, width), lambda i, p: (i, 0))
    column = pl.BlockSpec((length, 1), lambda i, p: (i, 0))
    pairs = pl.BlockSpec(mine.shape, lambda i, p: (0, 0, 0))
    row = pl.BlockSpec((1, width), lambda i, p: (0, 0))
    return pl.pallas_call(
        join_backward_kernel,
        grid_spec=pltpu.PrefetchScalarGridSpec(
            num_scalar_prefetch=1,
            grid=(STEPS,),
            in_specs=[block] * 5 + [column, pairs, pairs, row],
            out_specs=[row, pl.BlockSpec((length, 2 * width), lambda i, p: (i, 0))],
            scratch_shapes=[pltpu.VMEM((1, width), f32)],
        ),
        out_shape=(jax.ShapeDtypeStruct((1, width), f32), jax.ShapeDtypeStruct((tokens, 2 * width), bf16)),
        compiler_params=params(),
        cost_estimate=light(),
        name="join_backward",
    )(place, local, run, in_pre, forget_pre, prev, cut, mine, theirs, bound)


def mixing_kernel(grad_ref, state_ref, mix_ref, scale_ref, gain_ref, mixed_ref, mix_grad_ref, sum_ref, cross_ref):
    @pl.when(pl.program_id(0) == 0)
    def _():
        sum_ref[...] = jnp.zeros_like(sum_ref)

    mix = mix_ref[...]
    sig = jax.nn.sigmoid(mix)
    act = mix * sig
    gain = gain_ref[...]
    grad = grad_ref[...]
    state = state_ref[...]
    level = state * scale_ref[...]
    mixed_ref[...] = (level * gain * act).astype(mixed_ref.dtype)
    mix_grad_ref[...] = (grad * level * gain * (sig * (1.0 + mix * (1.0 - sig)))).astype(mix_grad_ref.dtype)
    sum_ref[...] += jnp.sum(grad * level * act, axis=0, keepdims=True)
    cross_ref[...] = jnp.sum(grad * gain * act * state, axis=1, keepdims=True)


def mixing(grad, state, mix_pre, scale, gain):
    tokens, width = grad.shape
    length = tokens // STEPS
    block = pl.BlockSpec((length, width), lambda i: (i, 0))
    column = pl.BlockSpec((length, 1), lambda i: (i, 0))
    row = pl.BlockSpec((1, width), lambda i: (0, 0))
    half = jax.ShapeDtypeStruct((tokens, width), bf16)
    return pl.pallas_call(
        mixing_kernel,
        grid=(STEPS,),
        in_specs=[block, block, block, column, row],
        out_specs=[block, block, row, column],
        out_shape=(half, half, jax.ShapeDtypeStruct((1, width), f32), jax.ShapeDtypeStruct((tokens, 1), f32)),
        compiler_params=params(),
        cost_estimate=light(),
        name="mixing",
    )(grad, state, mix_pre, scale, gain)


TILES = 1
HALVES = 2


def tiled(rows, width):
    return [jax.ShapeDtypeStruct((rows, width // TILES), f32)] * TILES


def columns(refs):
    return jnp.concatenate([ref[...] for ref in refs], axis=1)


def spread(refs, value):
    wide = value.shape[1] // TILES
    for i, ref in enumerate(refs):
        ref[...] = value[:, i * wide : (i + 1) * wide].astype(ref.dtype)


def call(kernel, name, place, grid, in_specs, out_specs, out_shape, *values, scratch=(), **how):
    return pl.pallas_call(
        kernel,
        grid_spec=pltpu.PrefetchScalarGridSpec(
            num_scalar_prefetch=1, grid=grid, in_specs=in_specs, out_specs=out_specs, scratch_shapes=scratch
        ),
        out_shape=out_shape,
        compiler_params=params(),
        cost_estimate=light(),
        name=name,
        **how,
    )(place, *values)


def enter_kernel(place, input_ref, kept_ref, came_ref, scale_ref, middle_ref, level_ref, *halves):
    middle = input_ref[...].astype(f32) + (kept_ref[...] + came_ref[...]) * scale_ref[...]
    middle_ref[...] = middle
    level = middle * rms_scale(middle)
    level_ref[...] = level
    wide = level.shape[1] // HALVES
    for i, ref in enumerate(halves):
        ref[...] = level[:, i * wide : (i + 1) * wide]


def enter(place, k, inputs, kept, came, scale):
    rows, width = kept.shape
    steps = 4
    part = rows // steps
    here = pl.BlockSpec((part, width), lambda i, p: (i, 0))
    full = jax.ShapeDtypeStruct((rows, width), f32)
    among = lambda i, p: ((2 * k + p[2]) * steps + i, 0)
    specs = [pl.BlockSpec((part, width), among), here, here, pl.BlockSpec((part, 1), among)]
    half = pl.BlockSpec((part, width // HALVES), lambda i, p: (i, 0))
    shapes = [full, full] + [jax.ShapeDtypeStruct((rows, width // HALVES), f32)] * HALVES
    done = call(enter_kernel, "enter", place, (steps,), specs, [here, here] + [half] * HALVES, shapes, inputs, kept, came, scale)
    return done[0], done[1], tuple(done[2:])


def feed_kernel(place, mine_ref, norm_ref, gate_w_ref, up_w_ref, pull_ref, *rest):
    theirs_refs = rest[:HALVES]
    nf_ref, hid_ref, dg_ref, du_ref = rest[-4:]
    rows = mine_ref.shape[0]
    core = place[2]
    norm = norm_ref[...]
    nf_ref[pl.ds(pl.multiple_of(core * rows, rows), rows), :] = (mine_ref[...] * norm).astype(bf16)
    nf_ref[pl.ds(pl.multiple_of((1 - core) * rows, rows), rows), :] = (columns(theirs_refs) * norm).astype(bf16)
    nf = nf_ref[...]
    gate = multiply(nf, gate_w_ref[...])
    upward = multiply(nf, up_w_ref[...])
    sig = jax.nn.sigmoid(gate)
    act = gate * sig
    pull = pull_ref[...]
    hid_ref[...] = (act * upward).astype(bf16)
    dg_ref[...] = (pull * upward * (sig * (1.0 + gate * (1.0 - sig)))).astype(bf16)
    du_ref[...] = (pull * act).astype(bf16)


def feed_forward(place, k, mine, theirs, norm, w_gate, w_up, pull, before):
    rows, width = mine.shape
    units = w_gate.shape[1]
    tokens = pull.shape[0]
    shapes = [(tokens, width)] + [(tokens, units)] * 3
    outs = [pl.BlockSpec((2 * rows, n), lambda i, p: (k, 0)) for _, n in shapes]

    def once(shape, at=lambda i, p: (0, 0)):
        return pl.BlockSpec(shape, at, pipeline_mode=pl.Buffered(1))

    specs = [once(v.shape) for v in (mine, norm, w_gate, w_up)] + [once((2 * rows, units), lambda i, p: (k, 0))]
    specs += [once(v.shape) for v in theirs] + [ANY] * len(before)
    return call(
        feed_kernel,
        "feed_forward",
        place,
        (1,),
        specs,
        outs,
        tuple(jax.ShapeDtypeStruct(shape, bf16) for shape in shapes),
        mine,
        norm,
        w_gate,
        w_up,
        pull,
        *theirs,
        *before,
        input_output_aliases={6 + HALVES + i: i for i in range(len(before))},
    )


def product_kernel(pairs, flipped, place, *refs):
    mine_ref, theirs_ref, held = refs[2 * pairs :]
    core = place[2]
    rows = mine_ref.shape[0] // 2
    times = outer_cols if flipped else multiply
    value = times(refs[0][...], refs[1][...])
    for i in range(1, pairs):
        value = value + times(refs[2 * i][...], refs[2 * i + 1][...])
    held[...] = value
    for k in range(2):
        for ref, at in ((mine_ref, core), (theirs_ref, 1 - core)):
            ref[k * rows : (k + 1) * rows, :] = held[pl.ds(pl.multiple_of((2 * k + at) * rows, rows), rows), :]


def product(place, pairs, flipped):
    first = pairs[0][0]
    tokens = (first[0] if isinstance(first, tuple) else first).shape[0]
    width = pairs[0][1].shape[0 if flipped else 1]
    steps = 4
    tile = width // steps
    specs, values = ([], [])
    for left, right in pairs:
        left, block = left if isinstance(left, tuple) else (left, 0)
        deep = right.shape[1 if flipped else 0]
        specs.append(pl.BlockSpec((tokens, deep), lambda i, p, block=block: (0, block)))
        specs.append(pl.BlockSpec((tile, deep), lambda i, p: (i, 0)) if flipped else pl.BlockSpec((deep, tile), lambda i, p: (0, i)))
        values += [left, right]
    out = pl.BlockSpec((tokens // 2, tile), lambda i, p: (0, i))
    shape = jax.ShapeDtypeStruct((tokens // 2, width), f32)
    kernel = functools.partial(product_kernel, len(pairs), flipped)
    held = [pltpu.VMEM((tokens, tile), f32)]
    mine, theirs = call(kernel, "product", place, (steps,), specs, [out, out], [shape, shape], *values, scratch=held)
    return mine, (theirs,)


def merge_kernel(place, full_ref, *refs):
    refs[-1][...] = full_ref[...] + columns(refs[:-1])


def merge(place, full, pieces):
    rows, width = full.shape
    steps = 4
    here = pl.BlockSpec((rows // steps, width), lambda i, p: (i, 0))
    piece = pl.BlockSpec((rows // steps, width // TILES), lambda i, p: (i, 0))
    return call(
        merge_kernel, "merge", place, (steps,), [here] + [piece] * TILES, here, jax.ShapeDtypeStruct(full.shape, f32), full, *pieces
    )


def leave_kernel(place, value_ref, base_ref, kept_ref, came_ref, gain_ref, grad_ref, total_ref, *change_refs, whole):
    @pl.when(pl.program_id(0) == 0)
    def _():
        grad_ref[...] = jnp.zeros_like(grad_ref)

    value = value_ref[...].astype(f32)
    scale = rms_scale(value)
    level = value * scale
    grad = kept_ref[...] + came_ref[...]
    weighed = grad * gain_ref[...]
    change = scale * (weighed - level * jnp.mean(weighed * level, axis=-1, keepdims=True))
    total = base_ref[...].astype(f32) + change
    grad_ref[...] += jnp.sum(grad * level, axis=0, keepdims=True)
    total_ref[...] = total
    spread(change_refs, total if whole else change)


def leave(place, k, value, base, kept, came, gain, whole):
    rows, width = (kept.shape[0] // 2, kept.shape[1])
    steps = 4
    part = rows // steps
    here = pl.BlockSpec((part, width), lambda i, p: (i, 0))
    mine = pl.BlockSpec((part, width), lambda i, p: (k * steps + i, 0))
    among = pl.BlockSpec((part, width), lambda i, p: ((2 * k + p[2]) * steps + i, 0))
    piece = pl.BlockSpec((part, width // TILES), lambda i, p: (i, 0))
    row = pl.BlockSpec((1, width), lambda i, p: (0, 0))
    done = call(
        functools.partial(leave_kernel, whole=whole),
        "leave",
        place,
        (steps,),
        [here if v.shape[0] == rows else among for v in (value, base)] + [mine, mine, row],
        [row, here] + [piece] * TILES,
        [jax.ShapeDtypeStruct((1, width), f32), jax.ShapeDtypeStruct((rows, width), f32)] + tiled(rows, width),
        value,
        base,
        kept,
        came,
        gain,
    )
    return done[0], done[1], tuple(done[2:])


def result_kernel(place, first_ref, second_ref, kept_ref, came_ref, total_ref, *pieces):
    k = pl.program_id(0) // (pl.num_programs(0) // 2)
    total = jnp.where(k == 0, first_ref[...], second_ref[...]) + kept_ref[...] + came_ref[...]
    total_ref[...] = total
    spread(pieces, total)


def result(place, first, second, kept, came):
    rows, width = kept.shape
    steps = 8
    part = rows // steps
    here = pl.BlockSpec((part, width), lambda i, p: (i, 0))
    folded = pl.BlockSpec((part, width), lambda i, p: (lax.rem(i, steps // 2), 0))
    piece = pl.BlockSpec((part, width // TILES), lambda i, p: (i, 0))
    full = jax.ShapeDtypeStruct((rows, width), f32)
    done = call(
        result_kernel,
        "result",
        place,
        (steps,),
        [folded, folded, here, here],
        [here] + [piece] * TILES,
        [full] + tiled(rows, width),
        first,
        second,
        kept,
        came,
    )
    return done[0], tuple(done[1:])


def assemble_kernel(own, based, scaled, place, *refs):
    whole = refs[-1]
    core = place[2]
    groups, at = ([], 0)
    for count in (own, own, TILES, TILES):
        groups.append(refs[at : at + count])
        at += count
    for i, group in enumerate(groups):
        k, where = (i % 2, core if i < 2 else 1 - core)
        value = columns(group)
        if based:
            value = value + refs[at][k, where].astype(f32)
        if scaled:
            value = value * refs[at][...]
        whole[k, where] = value.astype(whole.dtype)


def assemble(place, mine, theirs, kind, base=None, gain=None):
    mine = [v if isinstance(v, (tuple, list)) else (v,) for v in mine]
    rows = mine[0][0].shape[0]
    width = sum(v.shape[1] for v in mine[0])
    steps = 8
    part = rows // steps
    values = [v for group in (*mine, *theirs) for v in group]
    specs = [pl.BlockSpec((part, v.shape[1]), lambda i, p: (i, 0)) for v in values]
    whole = pl.BlockSpec((2, 2, part, width), lambda i, p: (0, 0, i, 0))
    if base is not None:
        specs.append(whole)
        values.append(base.reshape(2, 2, rows, width))
    if gain is not None:
        specs.append(pl.BlockSpec((1, width), lambda i, p: (0, 0)))
        values.append(gain)
    kernel = functools.partial(assemble_kernel, len(mine[0]), base is not None, gain is not None)
    shape = jax.ShapeDtypeStruct((2, 2, rows, width), kind)
    return call(kernel, "assemble", place, (steps,), specs, whole, shape, *values).reshape(4 * rows, width)


def swap_kernel(place, gate_ref, up_ref, out_ref):
    out_ref[...] = jnp.where(place[1] == 0, up_ref[...].astype(f32), gate_ref[...].astype(f32))


def swap(place, k, d_gate, d_upward):
    tokens, units = d_gate.shape
    steps = 4
    here = pl.BlockSpec((tokens // 2 // steps, units), lambda i, p: (k * steps + i, 0))
    out = pl.BlockSpec((tokens // 2 // steps, units), lambda i, p: (i, 0))
    shape = jax.ShapeDtypeStruct((tokens // 2, units), f32)
    return call(swap_kernel, "swap", place, (steps,), [here, here], out, shape, d_gate, d_upward)


def rise_kernel(place, up_ref, down_ref, came_up_ref, came_down_ref, up_out_ref, down_out_ref):
    up_out_ref[...] = up_ref[...] + came_up_ref[...]
    down_out_ref[...] = down_ref[...] + came_down_ref[...]


def rise(place, *values):
    rows, wide = values[0].shape
    steps = 4
    here = pl.BlockSpec((rows // steps, wide), lambda i, p: (i, 0))
    shape = jax.ShapeDtypeStruct((rows, wide), f32)
    return call(rise_kernel, "rise", place, (steps,), [here] * 4, [here, here], [shape, shape], *values)


def settle_kernel(place, block_ref, up_ref, down_ref, out_ref):
    out_ref[...] = block_ref[...] + up_ref[...] + down_ref[...]


def settle(place, *values):
    rows, wide = values[0].shape
    steps = 4
    here = pl.BlockSpec((rows // steps, wide), lambda i, p: (i, 0))
    return call(settle_kernel, "settle", place, (steps,), [here] * 3, here, jax.ShapeDtypeStruct((rows, wide), f32), *values)


def back_kernel(place, left_ref, right_ref, out_ref):
    out_ref[...] = outer_cols(left_ref[...], right_ref[...])


def back(place, left, right):
    tokens, width = left.shape
    deep = right.shape[0]
    steps = 4
    here = pl.BlockSpec((tokens // steps, width), lambda i, p: (i, 0))
    out = pl.BlockSpec((tokens // steps, deep), lambda i, p: (i, 0))
    specs = [here, pl.BlockSpec(right.shape, lambda i, p: (0, 0))]
    return call(back_kernel, "back", place, (steps,), specs, out, jax.ShapeDtypeStruct((tokens, deep), f32), left, right)


def place_block(outs, value, at=0):
    wide = value.shape[1]
    if len(outs) == 1:
        outs[0][0, :, at : at + wide] = value
        return
    for j, ref in enumerate(outs):

        @pl.when(pl.program_id(0) == j)
        def _():
            ref[:, at : at + wide] = value


def weigh_kernel(pairs, halves, place, *refs):
    outs = refs[2 * pairs + (2 if halves else 0) :]
    at = 0
    for i in range(pairs):
        value = inner_rows(refs[2 * i][...], refs[2 * i + 1][...])
        wide = value.shape[1]
        if halves:
            first, second = refs[2 * pairs : 2 * pairs + 2]
            early = pl.program_id(0) < pl.num_programs(0) // 2
            value = value + jnp.where(early, first[0, :, at : at + wide], second[0, :, at : at + wide])
        place_block(outs, value, at)
        at += wide


def weigh_both_kernel(place, left_ref, gate_ref, up_ref, far_left_ref, first_ref, second_ref, *outs):
    half = first_ref.shape[0]
    right = jnp.where(place[1] == 0, gate_ref[...], up_ref[...])
    value = inner_rows(left_ref[...], right)
    value = value + inner_rows(far_left_ref[:half, :], first_ref[...].astype(bf16))
    place_block(outs, value + inner_rows(far_left_ref[half:, :], second_ref[...].astype(bf16)))


def weigh_call(kernel, place, side, lefts, rights, order, wide, halves=(), count=None, first=0):
    count = DEEP if count is None else count
    rows = lefts[0].shape[1] // (2 * DEEP)

    def chosen(j, p):
        return (0, 2 * lax.rem(p[0] + first + j, DEEP) + (p[1] if side == 0 else 1 - p[1]))

    specs = {id(v): pl.BlockSpec((v.shape[0], rows), chosen) for v in lefts}
    specs |= {id(v): pl.BlockSpec(v.shape, lambda j, p: (0, 0)) for v in rights}
    half = pl.BlockSpec((1, rows, wide), lambda j, p: (lax.rem(j, DEEP // 2), 0, 0))
    if count == DEEP:
        block = [pl.BlockSpec((rows, wide), lambda j, p: (0, 0))] * DEEP
        shape = [jax.ShapeDtypeStruct((rows, wide), f32)] * DEEP
    else:
        block = pl.BlockSpec((1, rows, wide), lambda j, p: (j, 0, 0))
        shape = jax.ShapeDtypeStruct((count, rows, wide), f32)
    return call(
        kernel, "weigh", place, (count,), [specs[id(v)] for v in order] + [half] * len(halves), block, shape, *order, *halves
    )


def weigh(place, pairs, side, halves=(), count=None, first=0):
    order = [v for pair in pairs for v in pair]
    wide = sum(right.shape[1] for _, right in pairs)
    kernel = functools.partial(weigh_kernel, len(pairs), len(halves) == 2)
    return weigh_call(kernel, place, side, order[::2], order[1::2], order, wide, halves, count, first)


def weigh_both(place, side, left, gate, up, far_left, first, second):
    order = [left, gate, up, far_left, first, second]
    return weigh_call(weigh_both_kernel, place, side, [left, far_left], [gate, up, first, second], order, gate.shape[1])


SEQ, MP, DEEP = 8, 4, 4
CORE = [(i, i ^ 1) for i in range(MP)]
ACROSS = [(i, i ^ 2) for i in range(MP)]
BESIDE = [(i, i ^ 1) for i in range(SEQ)]
UP = [[(2 * z + y, 2 * z + 2 + y) for z in range(t) for y in range(2)] for t in range(DEEP)]
DOWN = [[(2 * z + y, 2 * z - 2 + y) for z in range(DEEP - t, DEEP) for y in range(2)] for t in range(DEEP)]


def over_core(v):
    return jax.tree.map(lambda part: lax.ppermute(part, "mp", CORE), v)


def over_x(v):
    return lax.ppermute(v, "mp", ACROSS)


def over_y(v):
    return lax.ppermute(v, "seq", BESIDE)


def along(bit):
    return lambda v: lax.ppermute(v, "seq", [(i, i ^ bit) for i in range(SEQ)])


def along_line(t):
    return lambda v: (lax.ppermute(v[0], "seq", UP[t]), lax.ppermute(v[1], "seq", DOWN[t]))


def reaching(reverse):
    def send(whole):
        rounds = [whole]
        for k in range(1, DEEP):
            pairs = [(2 * z + i, 2 * (z + k) + i) for z in range(DEEP - k) for i in range(2)]
            rounds.append(lax.ppermute(whole, "seq", [(b, a) for a, b in pairs] if reverse else pairs))
        return tuple(rounds)

    return send


class Names:
    def __getattr__(self, name):
        return name


N = Names()


def of(name, k):
    return name + str(k)


def sent(name):
    return name + "_"


def wait(name):
    return name + "!"


def flat(reads):
    return [reads] if isinstance(reads, str) else [name for part in reads for name in flat(part)]


class Steps:
    def __init__(self, place, known):
        self.place = place
        self.known = known
        self.steps = {}
        self.arrivals = set()
        self.last = None

    def add(self, name, reads, work, *sends):
        self.steps[name] = (flat(reads), work, sends)

    def settle(self, *names):
        if self.last is None:
            return
        last, sends = self.last
        self.last = None
        names = [v for v in dict.fromkeys(names) if v != last]
        held = {v: self.known[v] for v in [*names, last]}
        self.known.update(together(held))
        done = self.known[last]
        for arrival, how, *part in sends:
            self.known[arrival] = how(done[part[0]] if part else done)
            self.arrivals.add(arrival)

    def run(self, name):
        if name.endswith("!"):
            self.settle()
            name = name[:-1]
            self.arrivals.discard(name)
            self.last = (name, ())
            return
        reads, work, sends = self.steps.pop(name)
        self.settle(*[v for v in reads if v in self.known and v not in self.arrivals])
        self.known[name] = work(*[self.known[v] for v in reads])
        self.last = (name, sends)

    def line(self, name, source):
        reads, work, _ = self.steps[source]
        self.steps[source] = (reads, work, ((sent(of(name, 1)), lambda v: along_line(1)((v[DEEP - 1], v[1]))),))
        for t in range(2, DEEP):
            self.add(
                of(name, t),
                (source, sent(of(name, t - 1))),
                lambda v, came, t=t: rise(self.place, v[DEEP - t], v[t], *came),
                (sent(of(name, t)), along_line(t)),
            )


ORDER = (
    N.in_pre,
    N.forget,
    N.scan,
    N.mix,
    N.stack,
    N.join,
    N.square,
    wait(N.square_),
    N.send0,
    N.square2,
    N.send1,
    wait(N.square2_),
    N.keep0,
    N.keep1,
    N.scale,
    N.pull,
    N.enter0,
    N.feed0,
    N.gates0,
    N.enter1,
    N.feed1,
    wait(N.beside0),
    N.unfeed,
    N.down_far,
    N.unfed,
    N.down_own,
    N.p2,
    N.gates1,
    N.spread,
    wait(N.gates0_),
    N.beside0_,
    N.q2,
    N.leave0,
    N.leave1,
    N.p3,
    N.beside1_,
    N.branch,
    wait(N.spread_),
    N.mixed,
    N.far_nf,
    N.mixing,
    N.cross,
    N.cross2,
    N.mix_send0,
    N.spread_sum,
    wait(N.p3_),
    N.tug,
    N.scan_b,
    N.q3,
    N.pair_own,
    N.pair_far,
    N.stack_b,
    N.join_b,
    wait(N.mix_send0_),
    N.both_send1,
    N.p_sum,
    wait(N.q3_),
    N.origin,
    N.r2,
    N.mix_send1,
    wait(N.both_send1_),
    N.result,
    N.s2,
    wait(N.r2_),
    N.both_send0,
    N.source,
    N.mix_keep,
    N.s3,
    N.t2,
    N.out,
    N.both_keep,
    N.r3,
    N.t3,
    N.u2,
    N.enter_b0,
    N.enter_b1,
    N.r_sum,
    N.norms,
    N.u3,
    N.small,
    N.q_sum,
    wait(N.u3_),
    N.small2,
    N.t_sum,
    wait(N.p_sum_),
    wait(N.small2_),
    N.u_sum,
    N.small3,
    N.d_inputs,
    N.s_sum,
    N.smalls,
)


def planned(
    inputs, seq_start, norm_in, w_input, w_forget, w_mix_gate, lower_bound, mix_gain, w_output, norm_ffn, w_gate, w_up, w_down, cotangent
):
    tokens, width = inputs.shape
    quarter = tokens // 4
    units = w_input.shape[1]
    seq = lax.axis_index("seq")
    core = lax.axis_index("mp") % 2
    y = seq % 2
    place = jnp.stack([seq // 2, y, core])
    bound = lower_bound[None, :]
    gain = mix_gain[None, :]
    places = seq * tokens + jnp.arange(tokens, dtype=jnp.int32)
    cut = (seq_start == places).astype(f32)[:, None]
    known = dict(
        inputs=inputs,
        w_output=w_output,
        w_gate=w_gate,
        w_up=w_up,
        w_down=w_down,
        cot=cotangent,
        norm=norm_ffn[None, :],
        norm_in=norm_in[None, :],
        wi=w_input,
        wf=w_forget,
        wm=w_mix_gate,
    )
    plan = Steps(place, known)
    step = plan.add

    def quarters(v, at):
        parts = v.reshape((2, 2, quarter) + v.shape[1:])
        return lax.dynamic_index_in_dim(parts, at, 1, keepdims=False)

    def add(a, b):
        return a + b

    in_float = inputs.astype(f32)
    known[N.normed] = (in_float * rms_scale(in_float) * norm_in).astype(bf16)
    step(N.in_pre, (N.normed, N.wi), multiply)
    step(N.forget, (N.normed, N.wf), multiply)
    step(N.scan, (N.in_pre, N.forget), lambda a, b: scan_forward(a, b, cut, bound), (N.scan_, reaching(False), 2))
    step(N.mix, (N.normed, N.wm), multiply)
    step(N.stack, N.scan_, lambda v: jnp.stack(v), (N.stack_, over_y))
    step(N.join, (N.scan, N.mix, N.stack, N.stack_), lambda a, b, *v: join_forward(place, a[0], a[1], b, *v, gain))

    step(N.square, N.join, lambda v: v[3][:, 0], (N.square_, over_core))
    step(N.square2, (N.square, N.square_), add, (N.square2_, over_x))
    step(N.scale, (N.square2, N.square2_), lambda a, b: lax.rsqrt((a + b) / width + epsilon)[:, None])
    for k in range(2):
        step(of(N.send, k), (N.join, N.w_output), lambda v, w, k=k: multiply(quarters(v[2], 1 - core)[k], w), (sent(of(N.send, k)), over_core))
        step(
            of(N.keep, k), (N.join, N.w_output, sent(of(N.send, k))), lambda v, w, s, k=k: multiply(quarters(v[2], core)[k], w) + s, (sent(of(N.keep, k)), over_x)
        )
    step(N.pull, (N.cot, N.w_down), lambda a, b: back(place, a, b))

    for k in range(2):
        step(
            of(N.enter, k),
            (N.inputs, of(N.keep, k), sent(of(N.keep, k)), N.scale),
            functools.partial(enter, place, k),
            (sent(of(N.level, k)), over_core, 2),
            (of(N.beside, k), over_y, 1),
        )
        step(
            of(N.feed, k),
            ((of(N.enter, k), sent(of(N.level, k)), N.norm, N.w_gate), (N.w_up, N.pull), (N.feed0, N.gates0) if k else ()),
            lambda e, t, n, g, u, p, *before, k=k: feed_forward(place, k, e[1], t, n, g, u, p, before[0] if before else ()),
        )
        step(of(N.gates, k), of(N.feed, k), lambda v, k=k: swap(place, k, v[2], v[3]), (sent(of(N.gates, k)), over_y))

    step(N.down_far, (N.cot, N.feed1), lambda a, b: weigh(place, [(a, b[1])], 1))
    step(N.down_own, (N.cot, N.feed1), lambda a, b: weigh(place, [(a, b[1])], 0))
    plan.line(N.p, N.down_far)
    plan.line(N.q, N.down_own)
    step(N.p_sum, (N.down_far, N.p3_), lambda b, c: settle(place, b[0], *c), (N.p_sum_, over_y))
    step(N.q_sum, (N.down_own, N.q3_, N.p_sum_), lambda b, c, d: (b[0] + c[0] + c[1] + d).T)
    for k in range(2):
        step(sent(of(N.beside, k)), of(N.beside, k), lambda v: (v,), (sent(sent(of(N.beside, k))), over_core))
    step(
        N.far_nf,
        ((N.beside0_, N.beside1_, N.beside0__, N.beside1__), N.norm),
        lambda a, b, c, d, e: assemble(place, (a, b), (c, d), bf16, gain=e),
    )
    both_args = (N.feed1, N.far_nf, N.gates0_, N.gates1_)
    step(N.pair_far, both_args, lambda f, *v: weigh_both(place, 1, f[0], f[2], f[3], *v))
    step(N.pair_own, both_args, lambda f, *v: weigh_both(place, 0, f[0], f[2], f[3], *v))
    plan.line(N.r, N.pair_far)
    plan.line(N.s, N.pair_own)
    step(N.r_sum, (N.pair_far, N.r3_), lambda b, c: settle(place, b[0], *c), (N.r_sum_, over_y))

    def sort_pair(b, c, theirs):
        mine = b[0] + c[0] + c[1]
        return jnp.where(y == 0, mine, theirs), jnp.where(y == 0, theirs, mine)

    step(N.s_sum, (N.pair_own, N.s3_, N.r_sum_), sort_pair)

    step(
        N.unfeed, (N.feed1, N.w_gate, N.w_up), lambda f, g, u: product(place, [(f[2], g), (f[3], u)], True), (N.unfeed_, over_core, 1)
    )
    step(N.unfed, (N.unfeed, N.unfeed_), lambda a, b: merge(place, a[0], b), (N.unfed_, over_x))
    step(N.spread, (N.feed1, N.w_down), lambda f, w: product(place, [(f[1], w)], False), (N.spread_, over_core, 1))
    step(N.spread_sum, (N.spread, N.spread_, N.cross2_), lambda a, b, c: merge(place, a[0], b), (N.spread_sum_, over_x))
    step(
        N.result,
        (N.enter0, N.enter1, N.spread_sum, N.spread_sum_),
        lambda a, b, c, d: result(place, a[0], b[0], c, d),
        (N.result_, over_core, 1),
    )

    def halves(v):
        return (v[:quarter], v[quarter:])

    step(
        N.out,
        (N.result, N.result_),
        lambda a, b: assemble(place, halves(a[0]), list(zip(*[halves(v) for v in b], strict=True)), bf16),
    )

    for k in range(2):
        step(
            of(N.leave, k),
            ((of(N.enter, k), N.cot, N.unfed, N.unfed_), N.norm),
            lambda e, *v, k=k: leave(place, k, e[0], *v, False),
            (sent(of(N.leave, k)), over_core, 2),
        )
    step(
        N.branch,
        ((N.leave0, N.leave1, N.leave0_, N.leave1_), N.cot),
        lambda a, b, c, d, e: assemble(place, (a[2], b[2]), (c, d), bf16, base=e),
    )
    step(N.mixed, (N.branch, N.w_output), lambda a, b: back(place, a, b))
    step(N.mixing, (N.mixed, N.join, N.mix, N.scale), lambda d, j, m, s: mixing(d, j[0], m, s, gain))
    step(N.cross, N.mixing, lambda v: v[3][:, 0], (N.cross_, over_core))
    step(N.cross2, (N.cross, N.cross_), add, (N.cross2_, over_x))
    step(N.tug, (N.cross2, N.cross2_, N.scale), lambda a, b, s: s**3 * ((a + b)[:, None] / width))
    step(
        N.scan_b,
        ((N.mixed, N.join, N.mix, N.forget), (N.scale, N.tug)),
        lambda d, j, m, f, s, t: scan_backward(d, j[0], m, f, cut, s, t, bound, gain),
        (N.scan_b_, reaching(True), 2),
    )
    step(N.stack_b, N.scan_b_, lambda v: jnp.stack(v), (N.stack_b_, over_y))
    step(
        N.join_b,
        ((N.scan_b, N.in_pre, N.forget, N.join), (N.stack_b, N.stack_b_)),
        lambda s, i, f, j, *v: join_backward(place, s[0], s[1], i, f, j[1], cut, *v, bound),
    )

    def mix_pairs(n, m, b):
        return [(n, m[1]), (b, m[0])]

    for k in range(2):
        step(
            of(N.mix_send, k),
            (N.normed, N.mixing, N.branch),
            lambda *v, k=k: weigh(place, mix_pairs(*v), 1, (), DEEP // 2, k * DEEP // 2),
            (sent(of(N.mix_send, k)), over_y),
        )
        step(
            of(N.both_send, k),
            (N.normed, N.join_b),
            lambda n, b, k=k: weigh(place, [(n, b[1])], 1, (), DEEP // 2, k * DEEP // 2),
            (sent(of(N.both_send, k)), over_y),
        )
    step(N.mix_keep, ((N.normed, N.mixing, N.branch, N.mix_send0_), N.mix_send1_), lambda *v: weigh(place, mix_pairs(*v[:3]), 0, v[3:]))
    step(N.both_keep, (N.normed, N.join_b, N.both_send0_, N.both_send1_), lambda n, b, *v: weigh(place, [(n, b[1])], 0, v))
    plan.line(N.t, N.mix_keep)
    plan.line(N.u, N.both_keep)

    def sort_mix(b, c):
        total = b[0] + c[0] + c[1]
        return total[:, :units], total[:, units:].T

    def sort_both(b, c):
        total = b[0] + c[0] + c[1]
        return total[:, :units], total[:, units:]

    step(N.t_sum, (N.mix_keep, N.t3_), sort_mix)
    step(N.u_sum, (N.both_keep, N.u3_), sort_both)

    step(
        N.origin,
        ((N.join_b, N.mixing, N.wi, N.wf), N.wm),
        lambda b, m, i, f, w: product(place, [((b[1], 0), i), ((b[1], 1), f), (m[1], w)], True),
        (N.origin_, over_core, 1),
    )
    step(N.source, (N.origin, N.origin_), lambda a, b: merge(place, a[0], b), (N.source_, over_x))
    for k in range(2):
        step(
            of(N.enter_b, k),
            ((N.inputs, of(N.leave, k), N.source, N.source_), N.norm_in),
            lambda i, m, *v, k=k: leave(place, k, i, m[1], *v, True),
            (sent(of(N.enter_b, k)), over_core, 2),
        )
    step(
        N.d_inputs,
        (N.enter_b0, N.enter_b1, N.enter_b0_, N.enter_b1_),
        lambda a, b, c, d: assemble(place, (a[1], b[1]), (c, d), f32),
    )
    step(
        N.norms,
        (N.enter_b0, N.enter_b1, N.leave0, N.leave1),
        lambda a, b, c, d: jnp.concatenate([a[0] + b[0], c[0] + d[0]], axis=1)[0],
        (N.norms_, over_core),
    )
    step(
        N.small,
        ((N.norms, N.norms_, N.join_b, N.mixing), N.scan),
        lambda a, b, c, d, e: jnp.concatenate([a + b, c[0][0], d[2][0], e[3][0]]),
        (N.small_, along(1)),
    )
    step(N.small2, (N.small, N.small_), add, (N.small2_, along(2)))
    step(N.small3, (N.small2, N.small2_), add, (N.small3_, along(4)))
    step(N.smalls, (N.small3, N.small3_), add)

    for name in ORDER:
        plan.run(name)
    plan.settle()
    smalls = known[N.smalls]
    piece = width // SEQ
    d_norm_in = lax.dynamic_slice_in_dim(smalls, seq * piece, piece)
    d_norm_ffn = lax.dynamic_slice_in_dim(smalls, width + seq * piece, piece)
    d_lower, d_mix_gain, forget_sum = (smalls[2 * width + i * units : 2 * width + (i + 1) * units] for i in range(3))
    mix_grad, out_grad = known[N.t_sum]
    in_grad, forget_grad = known[N.u_sum]
    gate_grad, up_grad = known[N.s_sum]
    return (
        known[N.out],
        known[N.d_inputs],
        d_norm_in,
        in_grad,
        forget_grad,
        mix_grad,
        d_lower,
        d_mix_gain,
        out_grad,
        d_norm_ffn,
        gate_grad,
        up_grad,
        known[N.q_sum],
        forget_sum / (tokens * SEQ),
    )


def entering(x, axis, combine, identity, reverse):
    length, index = (lax.axis_size(axis), lax.axis_index(axis))
    everything = jax.tree.map(lambda part: lax.all_gather(part, axis), x)
    start = jax.tree.map(
        lambda part, zero: jnp.broadcast_to(jnp.asarray(zero, part.dtype), part.shape), x, identity
    )

    def turn(k, before):
        at = length - 1 - k if reverse else k
        reached = at > index if reverse else at < index
        new = combine(before, jax.tree.map(lambda part: part[at], everything))
        return jax.tree.map(lambda a, b: jnp.where(reached, a, b), new, before)

    return lax.fori_loop(0, length, turn, start)


def compose(earlier, later):
    return (earlier[0] * later[0], later[0] * earlier[1] + later[1])


def carry_forward(whole, ending):
    result = entering(
        (whole, ending), "seq", compose, (jnp.ones_like(whole), jnp.zeros_like(ending)), False
    )
    return result[1]


def carry_backward(whole, leading):
    result = entering(
        (whole, leading), "seq", compose, (jnp.ones_like(whole), jnp.zeros_like(leading)), True
    )
    return result[1]


def general(
    inputs,
    seq_start,
    norm_in,
    w_input,
    w_forget,
    w_mix_gate,
    lower_bound,
    mix_gain,
    w_output,
    norm_ffn,
    w_gate,
    w_up,
    w_down,
    cotangent,
):
    tokens_here = inputs.shape[0]
    width = inputs.shape[1]
    places = lax.axis_index("seq") * tokens_here + jnp.arange(tokens_here, dtype=jnp.int32)
    restart = (seq_start == places).astype(jnp.float32)[:, None]
    in_float = inputs.astype(jnp.float32)
    scale_in = rms_scale(in_float)
    normed = (in_float * scale_in * norm_in).astype(jnp.bfloat16)
    in_pre = multiply(normed, w_input)
    forget_pre = multiply(normed, w_forget)
    mix_pre = multiply(normed, w_mix_gate)
    fade = jax.nn.sigmoid(-forget_pre)
    forget_local = jnp.sum(1.0 - fade, axis=0)
    keep = (1.0 - lower_bound) * fade
    decay = (1.0 - keep) * (1.0 - restart)
    act_in = jax.nn.silu(in_pre)
    drive = act_in * keep
    decay_run, state_local = lax.associative_scan(compose, (decay, drive), axis=0)
    state_in = carry_forward(decay_run[-1], state_local[-1])
    state = state_local + decay_run * state_in
    squares = lax.psum(jnp.sum(state * state, axis=1), "mp")
    mix_scale = lax.rsqrt(squares / width + epsilon)[:, None]
    gate_act = jax.nn.silu(mix_pre)
    normed_state = state * mix_scale
    mixed = (normed_state * mix_gain * gate_act).astype(jnp.bfloat16)
    branch = lax.psum(multiply(mixed, w_output), "mp")
    middle = in_float + branch
    scale_ffn = rms_scale(middle)
    normed_ffn = (middle * scale_ffn * norm_ffn).astype(jnp.bfloat16)
    gate = multiply(normed_ffn, w_gate)
    upward = multiply(normed_ffn, w_up)
    silu_gate = jax.nn.silu(gate)
    hidden = (silu_gate * upward).astype(jnp.bfloat16)
    feed = lax.psum(multiply(hidden, w_down), "mp")
    out = (middle + feed).astype(jnp.bfloat16)
    grad_float = cotangent.astype(jnp.float32)
    d_hidden = outer_cols(cotangent, w_down)
    d_w_down = inner_rows(hidden, cotangent)
    d_gate = (d_hidden * upward * silu_slope(gate)).astype(jnp.bfloat16)
    d_upward = (d_hidden * silu_gate).astype(jnp.bfloat16)
    d_normed_ffn = lax.psum(outer_cols(d_gate, w_gate) + outer_cols(d_upward, w_up), "mp")
    d_w_gate = inner_rows(normed_ffn, d_gate)
    d_w_up = inner_rows(normed_ffn, d_upward)
    d_norm_ffn = jnp.sum(d_normed_ffn * middle * scale_ffn, axis=0)
    scaled_ffn = d_normed_ffn * norm_ffn
    d_middle = (
        grad_float
        + scale_ffn * scaled_ffn
        - middle * scale_ffn**3 * jnp.mean(scaled_ffn * middle, axis=-1, keepdims=True)
    )
    d_branch = d_middle.astype(jnp.bfloat16)
    d_w_output = inner_rows(mixed, d_branch)
    d_mixed = outer_cols(d_branch, w_output)
    d_mix_gain = jnp.sum(d_mixed * normed_state * gate_act, axis=0)
    d_mix_pre = (d_mixed * normed_state * mix_gain * silu_slope(mix_pre)).astype(jnp.bfloat16)
    scaled_mix = d_mixed * mix_gain * gate_act
    cross = lax.psum(jnp.sum(scaled_mix * state, axis=1), "mp")
    d_state = mix_scale * scaled_mix - state * mix_scale**3 * (cross / width)[:, None]
    next_decay = jnp.concatenate([decay[1:], jnp.ones_like(decay[:1])], axis=0)
    tail_decay, tail_grad = lax.associative_scan(
        compose, (next_decay, d_state), reverse=True, axis=0
    )
    carried = carry_backward(decay_run[-1], decay[0] * tail_grad[0])
    total = tail_grad + tail_decay * carried
    prev_state = jnp.concatenate([state_in[None], state[:-1]], axis=0)
    d_keep = total * act_in - total * prev_state * (1.0 - restart)
    d_lower = -jnp.sum(d_keep * fade, axis=0)
    d_in_pre = (total * keep * silu_slope(in_pre)).astype(jnp.bfloat16)
    d_forget_pre = (-d_keep * (1.0 - lower_bound) * fade * (1.0 - fade)).astype(jnp.bfloat16)
    d_normed = lax.psum(
        outer_cols(d_in_pre, w_input)
        + outer_cols(d_forget_pre, w_forget)
        + outer_cols(d_mix_pre, w_mix_gate),
        "mp",
    )
    d_w_input = inner_rows(normed, d_in_pre)
    d_w_forget = inner_rows(normed, d_forget_pre)
    d_w_mix_gate = inner_rows(normed, d_mix_pre)
    d_norm_in = jnp.sum(d_normed * in_float * scale_in, axis=0)
    scaled_in = d_normed * norm_in
    d_inputs = (
        d_middle
        + scale_in * scaled_in
        - in_float * scale_in**3 * jnp.mean(scaled_in * in_float, axis=-1, keepdims=True)
    )
    row_part = (
        lax.psum_scatter(d_w_input, "seq", scatter_dimension=0, tiled=True),
        lax.psum_scatter(d_w_forget, "seq", scatter_dimension=0, tiled=True),
        lax.psum_scatter(d_w_mix_gate, "seq", scatter_dimension=0, tiled=True),
        lax.psum_scatter(d_w_gate, "seq", scatter_dimension=0, tiled=True),
        lax.psum_scatter(d_w_up, "seq", scatter_dimension=0, tiled=True),
        lax.psum_scatter(d_norm_in, "seq", scatter_dimension=0, tiled=True),
        lax.psum_scatter(d_norm_ffn, "seq", scatter_dimension=0, tiled=True),
    )
    col_part = (
        lax.psum_scatter(d_w_output, "seq", scatter_dimension=1, tiled=True),
        lax.psum_scatter(d_w_down, "seq", scatter_dimension=1, tiled=True),
    )
    out_grad = col_part[0]
    down_grad = col_part[1]
    small_part = lax.psum((d_lower, d_mix_gain, forget_local), "seq")
    forget_mean = small_part[2] / (tokens_here * lax.axis_size("seq"))
    return (
        out,
        d_inputs,
        row_part[5],
        row_part[0],
        row_part[1],
        row_part[2],
        small_part[0],
        small_part[1],
        out_grad,
        row_part[6],
        row_part[3],
        row_part[4],
        down_grad,
        forget_mean,
    )


def solution(mesh):
    fits = mesh.shape["seq"] == SEQ and mesh.shape["mp"] == MP
    return jax.shard_map(
        planned if fits else general,
        mesh=mesh,
        in_specs=(
            P("seq", None),
            P("seq"),
            P(),
            P(None, "mp"),
            P(None, "mp"),
            P(None, "mp"),
            P("mp"),
            P("mp"),
            P("mp", None),
            P(),
            P(None, "mp"),
            P(None, "mp"),
            P("mp", None),
            P("seq", None),
        ),
        out_specs=(
            P("seq", None),
            P("seq", None),
            P("seq"),
            P("seq", "mp"),
            P("seq", "mp"),
            P("seq", "mp"),
            P("mp"),
            P("mp"),
            P("mp", "seq"),
            P("seq"),
            P("seq", "mp"),
            P("seq", "mp"),
            P("mp", "seq"),
            P("mp"),
        ),
        check_vma=False,
    )
```
